512 devices in a mesh: col: 64 (over z, x, core), mem: 8 (over y).
Axes of the slice: x: 4, y: 8, z: 8, core: 2. Of those that a mesh axis runs over, the one named last changes fastest.
Arguments:
- ensemble: bfloat16 [320, 393216], P('mem', 'col'), may hold values from -6 to 6
- control: bfloat16 [4, 393216], P(None, 'col'), may hold values from -6 to 6
- pair_home: int32 [16384, 1], replicated, may hold values from 0 to 63; in each aligned block of 256 rows (0 to 255, 256 to 511, ...) at most 5 rows name the same one
- pair_local: int32 [16384], replicated, may hold values from 0 to 23
- pair_count: int32 [64], P('col'), may hold values from 1 to 128, 5120 in all
- pair_shift: float32 [2, 8192], P(None, 'col'), may hold values from -410 to 410
Outputs:
- increment: float32 [4, 393216], P(None, ('col', 'mem'))
The draws below stay inside these ranges and needn't reach their ends.
Inputs may be any that keep to these rules, and one draw needn't show every extreme that they name: `pair_home`: rows 2 (o * 128 + s) and 2 (o * 128 + s) + 1 name the home devices of the two blocks of owner o's slot s; among the 256 rows of one owner no device is named more than 5 times, and for some owner some device is named exactly 5 times. `pair_count`: the counts sum to the number of live pairs; the largest is exactly 128.
All inputs are finite; a program needn't handle non-finite values. No bound on the sum of `pair_count` on one device may be relied on, other than what follows from the above.
Results may differ from the reference program's by a relative error of at most 0.0048.
Values may be sent and summed in bfloat16 or wider, within the bound.
A program may use at most 64 MiB of HBM per device.

```python
import math
import jax
import jax.numpy as jnp
import numpy as np
from jax import lax

MEMBERS = 80
LEVELS = 4
BLOCK_SIDE = 16
BLOCKS_DEV = 24
PEER_CAP = 5
BLOCK = 256
MEMBER_ROWS = 320
SLOTS_DEV = 128
COLUMNS = 393216
N_COL = 64


GRID_KM = 25.0


def draw_pair_shift(key, part):
    key = jax.random.fold_in(key, 11)
    step_key, jitter_key = jax.random.split(key)
    grid_steps = jax.random.randint(step_key, (2, N_COL * SLOTS_DEV), -16, 17)
    jitter = jax.random.uniform(jitter_key, (2, N_COL * SLOTS_DEV), jnp.float32, -10.0, 10.0)
    return grid_steps.astype(jnp.float32) * GRID_KM + jitter


def with_ends(drawn, own_key, low, largest):
    index_at = [jax.random.randint(jax.random.fold_in(own_key, axis), (), 0, length) for axis, length in enumerate(drawn.shape)]
    longest = drawn.shape.index(max(drawn.shape))
    beside = index_at[:longest] + [(index_at[longest] + 1) % drawn.shape[longest]] + index_at[longest + 1:]
    return drawn.at[tuple(index_at)].set(low).at[tuple(beside)].set(largest)


def shard_levels(rng, shape, cuts, low, top_value):
    factor_of = 1.0
    for axis_at, parts in cuts:
        heights = jax.random.uniform(jax.random.fold_in(jax.random.fold_in(rng, 6), axis_at), (parts,), jnp.float32, low / len(cuts), top_value / len(cuts))
        factor_of = factor_of * jnp.repeat(jnp.exp(heights), shape[axis_at] // parts).reshape((-1,) + (1,) * (len(shape) - 1 - axis_at))
    return factor_of


def profile(count, total, bound, lean):
    loads = [(1 << 20) // math.isqrt(grade ** lean) + 1 for grade in range(2, count + 1)]
    spare, holding = total - bound - (count - 1), [1] * (count - 1)
    while spare > 0:
        movable = [i for i in range(count - 1) if holding[i] < bound]
        mass, remaining = sum([loads[i] for i in movable]), spare
        for i in movable:
            extra = min(bound - holding[i], max(1, remaining * loads[i] // mass), spare)
            holding[i] = holding[i] + extra
            spare = spare - extra
    return np.array([bound] + holding)


def ragged_sizes(rng, amount, total, limit, slope):
    if amount == 2:
        one = jax.random.randint(rng, (), max(1, total - limit), min(limit, total - 1) + 1)
        return jnp.stack([one, total - one])
    tallies = jnp.asarray(profile(amount, total, limit, slope), jnp.int32)
    pairs = (amount - 1) // 2
    donor, receiver = tallies[1:1 + 2 * pairs:2], tallies[2:2 + 2 * pairs:2]
    room = jnp.minimum(donor - 1, limit - receiver)
    passed = jax.random.randint(jax.random.fold_in(rng, 1), (pairs,), 0, 1 << 20) % (room + 1)
    tallies = tallies.at[1:1 + 2 * pairs:2].set(donor - passed).at[2:2 + 2 * pairs:2].set(receiver + passed)
    return tallies[jax.random.permutation(jax.random.fold_in(rng, 2), amount)]


def deal_out(rng, own, number, rows, amount, top, limit, lean):
    ranking = jax.random.permutation(rng, amount)
    crowded, ordinary = load_shares(amount, rows * top, limit, lean, True), load_shares(amount, rows * top, limit, lean, False)
    places = jnp.arange(amount)

    def named(tallies, offset_by):
        used = int((tallies > 0).sum())
        fixed = max(1, used // 4)
        passed = fixed + (places - fixed + offset_by * (used - fixed)) % max(1, amount - fixed)
        return jnp.zeros((amount,), jnp.int32).at[ranking[jnp.where(places < fixed, places, passed)]].set(jnp.asarray(tallies, jnp.int32))

    tallies = jnp.where(number % 4 == 0, named(crowded, number // 4), named(ordinary, number - number // 4 - 1))
    mixed = jax.random.permutation(jax.random.fold_in(own, 3), amount)
    giver, taker = mixed[0:amount // 2 * 2:2], mixed[1:amount // 2 * 2:2]
    slack = jnp.minimum(tallies[giver] - 1, limit - tallies[taker]) // 2
    slack = jnp.where((giver == ranking[0]) | (taker == ranking[0]) | (tallies[taker] == 0), 0, jnp.maximum(slack, 0))
    passed = jax.random.randint(jax.random.fold_in(own, 4), (amount // 2,), 0, 1 << 20) % (slack + 1)
    tallies = tallies.at[giver].add(-passed).at[taker].add(passed)
    items = jnp.searchsorted(jnp.cumsum(tallies), jnp.arange(rows * top), side="right").astype(jnp.int32)
    table = items.reshape(top, rows).T
    table = table[jax.random.permutation(jax.random.fold_in(own, 1), rows)]
    offset_by = jax.random.randint(jax.random.fold_in(own, 2), (rows, 1), 0, top)
    return jnp.take_along_axis(table, (jnp.arange(top)[None, :] + offset_by) % top, axis=1)


def load_shares(count, total, most, lean, full):
    weights = [(1 << 20) // math.isqrt(rank ** lean) + 1 for rank in range(1, count + 1)]
    largest = most if full else min(most, max(-(-total // count), total * weights[0] // sum(weights)))
    least = 1 if total - largest >= count - 1 else 0
    holding, rest = [largest] + [least] * (count - 1), total - largest - least * (count - 1)
    while rest > 0:
        free = [i for i in range(1, count) if holding[i] < largest] or [i for i in range(1, count) if holding[i] < most]
        pool, left = sum([weights[i] for i in free]), rest
        for i in free:
            extra = min(most - holding[i], max(1, left * weights[i] // pool), rest)
            holding[i] = holding[i] + extra
            rest = rest - extra
    return np.array(holding)


def bell_draw(key, shape, scale, most, pieces=(), held_as=jnp.bfloat16):
    loudness = shard_levels(key, shape, pieces, -0.22, 0.18) if pieces else 1.0
    values = jax.random.normal(key, shape, jnp.float32) * scale * loudness
    return jnp.minimum(jnp.maximum(values, -most), most).astype(held_as)


def setup_inputs(seed: int = 0) -> dict:
    key_list = jax.random.split(jax.random.key(seed), 7)
    ensemble = bell_draw(key_list[0], (MEMBER_ROWS, COLUMNS), 1.0, 6.0, ((0, 8), (1, 64)))
    control = bell_draw(key_list[1], (LEVELS, COLUMNS), 1.0, 6.0, ((1, 64),))
    pair_home_keys = jax.random.split(jax.random.fold_in(key_list[2], 1), (2 * N_COL * SLOTS_DEV) // (2 * SLOTS_DEV))
    pair_home_turns = jax.random.permutation(jax.random.fold_in(key_list[2], 3), (2 * N_COL * SLOTS_DEV) // (2 * SLOTS_DEV))
    pair_home = jax.vmap(lambda own, number: deal_out(jax.random.fold_in(key_list[2], 2), own, number, 2 * SLOTS_DEV, N_COL, 1, PEER_CAP, 2))(pair_home_keys, pair_home_turns).reshape((2 * N_COL * SLOTS_DEV, 1))
    pair_local = with_ends(jax.random.randint(key_list[3], (2 * N_COL * SLOTS_DEV,), 0, BLOCKS_DEV), jax.random.fold_in(key_list[3], 1), 0, BLOCKS_DEV - 1).astype(jnp.int32)
    pair_count = ragged_sizes(key_list[4], N_COL, N_COL * SLOTS_DEV * 5 // 8, SLOTS_DEV, 2).astype(jnp.int32)
    pair_shift = draw_pair_shift(jax.random.fold_in(key_list[6], 71), 0)
    return dict(ensemble=ensemble, control=control, pair_home=pair_home, pair_local=pair_local, pair_count=pair_count, pair_shift=pair_shift)


SPACING_KM = 200.0
HALF_WIDTH = 250.0

def gaspari_cohn(distance):
    scaled = distance / HALF_WIDTH
    near_part = (((-0.25 * scaled + 0.5) * scaled + 0.625) * scaled - 5.0 / 3.0) * scaled * scaled + 1.0
    bounded = jnp.maximum(scaled, 1.0)
    far_part = ((((scaled / 12.0 - 0.5) * scaled + 0.625) * scaled + 5.0 / 3.0) * scaled - 5.0) * scaled + 4.0 - 2.0 / (3.0 * bounded)
    return jnp.where(scaled <= 1.0, near_part, jnp.where(scaled <= 2.0, far_part, 0.0))

def taper_tiles(offsets, live_slot):
    lattice = jnp.arange(BLOCK_SIDE * BLOCK_SIDE)
    east_km = (lattice % BLOCK_SIDE).astype(jnp.float32) * SPACING_KM
    north_km = (lattice // BLOCK_SIDE).astype(jnp.float32) * SPACING_KM
    delta_east = offsets[0][:, None, None] + east_km[None, None, :] - east_km[None, :, None]
    delta_north = offsets[1][:, None, None] + north_km[None, None, :] - north_km[None, :, None]
    taper = gaspari_cohn(jnp.sqrt(delta_east * delta_east + delta_north * delta_north))
    return (taper * live_slot[:, None, None]).astype(jnp.bfloat16)

def reference(ensemble, control, pair_home, pair_local, pair_count, pair_shift):
    member_rows = ensemble.shape[0]
    columns = ensemble.shape[1]
    blocks_all = columns // BLOCK
    owners = pair_count.shape[0]
    slot_count = pair_shift.shape[1] // owners
    level_of = jnp.arange(member_rows) // MEMBERS
    spread = control[level_of].astype(jnp.float32)
    weighted = (ensemble.astype(jnp.float32) * spread).astype(jnp.bfloat16)
    weighted = weighted.reshape(member_rows, blocks_all, BLOCK)
    block_ids = (pair_home[:, 0] * BLOCKS_DEV + pair_local).astype(jnp.int32).reshape(owners, slot_count, 2)
    offsets_all = pair_shift.reshape(2, owners, slot_count).transpose(1, 0, 2)
    live_all = (jnp.arange(slot_count)[None, :] < pair_count[:, None]).astype(jnp.float32)

    def owner_step(accumulated, inputs):
        chosen, offsets, live_slot = inputs
        taper = taper_tiles(offsets, live_slot).astype(jnp.float32)
        first_side = weighted[:, chosen[:, 0]].astype(jnp.float32)
        second_side = weighted[:, chosen[:, 1]].astype(jnp.float32)
        to_first = jnp.einsum('spq,msq->msp', taper, second_side, precision=lax.Precision.HIGHEST)
        to_second = jnp.einsum('spq,msp->msq', taper, first_side, precision=lax.Precision.HIGHEST)
        to_first = lax.optimization_barrier(to_first.astype(jnp.bfloat16)).astype(jnp.float32)
        to_second = lax.optimization_barrier(to_second.astype(jnp.bfloat16)).astype(jnp.float32)
        accumulated = accumulated.at[:, chosen[:, 0]].add(to_first)
        accumulated = accumulated.at[:, chosen[:, 1]].add(to_second)
        return (accumulated, None)
    accumulated = jnp.zeros((member_rows, blocks_all, BLOCK), jnp.float32)
    accumulated, _ = lax.scan(owner_step, accumulated, (block_ids, offsets_all, live_all))
    product = ensemble.astype(jnp.float32) * accumulated.reshape(member_rows, columns)
    return lax.optimization_barrier(jnp.sum(product.reshape(LEVELS, MEMBERS, columns), axis=1)) / (MEMBERS - 1.0)
```

```python
import functools

import jax
import jax.numpy as jnp
import numpy as np
from jax import lax
from jax.experimental import pallas as pl
from jax.experimental.pallas import tpu as pltpu
from jax.sharding import PartitionSpec as P

MEMBERS = 80
LEVELS = 4
SIDE = 16
BLOCK = 256
SPACING_KM = 200.0
HALF_WIDTH = 250.0
XC = 8
LANES = 128


def gaspari_cohn(squared):
    scaled = jnp.sqrt(squared * (1.0 / (HALF_WIDTH * HALF_WIDTH)))
    near_part = (
        ((-0.25 * scaled + 0.5) * scaled + 0.625) * scaled - 5.0 / 3.0
    ) * scaled * scaled + 1.0
    bounded = jnp.maximum(scaled, 1.0)
    far_part = (
        ((((scaled * (1.0 / 12.0) - 0.5) * scaled + 0.625) * scaled + 5.0 / 3.0) * scaled - 5.0) * scaled
        + 4.0
        - (2.0 / 3.0) / bounded
    )
    return jnp.where(scaled <= 1.0, near_part, jnp.where(scaled <= 2.0, far_part, 0.0))


def lattice_offsets():
    giver = np.arange(SIDE)[:, None]
    lane = np.arange(BLOCK)[None, :]
    east = (giver - lane % SIDE) * SPACING_KM
    north = (SIDE // 2 - lane // SIDE) * SPACING_KM + 0 * giver
    return jnp.asarray(np.stack([east, north]).astype(np.float32))


def pair_kernel(blocks, table, row_count, shifts, live, offsets, weighted, ensemble, out, gram, total, work):
    total[...] = jnp.zeros_like(total)
    rows = row_count.shape[0]

    def scan_row(row, found):
        owner = row // 2
        count = live[owner]

        def scan_entry(k, found):
            word = table[row, k]
            slot = (row % 2) * (LANES // 2) + (word >> 17)

            @pl.when(slot < count)
            def _():
                work[found] = (word & 0xFFFF) | ((row * LANES + (word >> 16)) << 16)

            return found + (slot < count).astype(jnp.int32)

        return lax.fori_loop(0, row_count[row], scan_entry, found)

    found = lax.fori_loop(0, rows, scan_row, jnp.int32(0))

    lane = lax.broadcasted_iota(jnp.int32, (8, LANES), 1)

    def one(n, carry):
        word = work[n]
        receiver = word & 0xFF
        giver = (word >> 8) & 0xFF
        entry = word >> 16
        slot = entry // 2
        owner, place = slot // LANES, slot % LANES
        sign = (1 - 2 * (entry % 2)).astype(jnp.float32)
        east = sign * shifts[2 * owner, place]
        north = sign * shifts[2 * owner + 1, place]
        give = weighted[
            giver // blocks, :, pl.ds(pl.multiple_of((giver % blocks) * BLOCK, BLOCK), BLOCK)
        ]
        take = ensemble[
            receiver // blocks, :, pl.ds(pl.multiple_of((receiver % blocks) * BLOCK, BLOCK), BLOCK)
        ]
        gram[...] = lax.dot_general(
            give, take, (((0,), (0,)), ((), ())), preferred_element_type=jnp.float32
        )
        sums = [jnp.zeros((8, LANES), jnp.float32) for _ in range(2)]
        for half in range(2):
            rows_here = slice(8 * half, 8 * half + 8)
            parts = []
            for side in range(2):
                cols = slice(LANES * side, LANES * side + LANES)
                de = east + offsets[0, rows_here, cols]
                dn = north + offsets[1, rows_here, cols]
                tap = gaspari_cohn(de * de + dn * dn)
                parts.append(tap.astype(jnp.bfloat16).astype(jnp.float32))
            for k in range(8):
                turned = [pltpu.roll(p, 16 * k, 1) if k else p for p in parts]
                low = lane < 16 * k
                middle = jnp.where(low, turned[0], turned[1])
                first = jnp.where(low, 0.0, turned[0])
                last = jnp.where(low, turned[1], 0.0)
                at = 16 * k + 8 * half
                up = LANES + at
                sums[0] += middle * gram[at : at + 8, :LANES] + first * gram[up : up + 8, :LANES]
                sums[1] += last * gram[at : at + 8, LANES:] + middle * gram[up : up + 8, LANES:]
        total[receiver, :, :LANES] += sums[0]
        total[receiver, :, LANES:] += sums[1]
        return carry

    lax.fori_loop(0, found, one, 0)
    out[...] = jnp.sum(total[...], axis=1)


def entry_table(pair_home, pair_local, blocks, own_z, own_xc):
    home = pair_home.reshape(-1, 2)
    local = pair_local.reshape(-1, 2)
    other_home, other_local = home[:, ::-1], local[:, ::-1]
    mine = (home // XC == own_z) & (other_home % XC == own_xc)
    word = (home % XC) * blocks + local + (((other_home // XC) * blocks + other_local) << 8)
    mine = mine.reshape(-1, LANES)
    word = word.reshape(-1, LANES) + (jnp.arange(LANES)[None, :] << 16)
    before = np.triu(np.ones((LANES, LANES), np.float32), 1)
    rank = jnp.dot(
        mine.astype(jnp.bfloat16), jnp.asarray(before, jnp.bfloat16), preferred_element_type=jnp.float32
    ).astype(jnp.int32)
    rank = jnp.where(mine, rank, -1)
    table = jnp.sum(
        jnp.where(rank[:, :, None] == jnp.arange(LANES)[None, None, :], word[:, :, None], 0), axis=1
    )
    return table, jnp.sum(mine.astype(jnp.int32), axis=1)


def shards(ensemble, control, pair_home, pair_local, pair_count, pair_shift):
    member_rows, columns = ensemble.shape
    blocks = columns // BLOCK
    owners = lax.axis_size("col")
    own_index = lax.axis_index("col")
    own_level = (lax.axis_index("mem") * member_rows) // MEMBERS
    own_z, own_xc = own_index // XC, own_index % XC
    z_groups = [[z * XC + xc for z in range(owners // XC)] for xc in range(XC)]
    xc_groups = [[z * XC + xc for xc in range(XC)] for z in range(owners // XC)]

    shifts = lax.all_gather(pair_shift, "col").reshape(2 * owners, -1)
    live = lax.all_gather(pair_count, "col", tiled=True)
    own_control = lax.dynamic_index_in_dim(control, own_level, 0)
    weighted = (ensemble.astype(jnp.float32) * own_control.astype(jnp.float32)).astype(jnp.bfloat16)
    weighted = lax.all_gather(weighted, "col", axis_index_groups=z_groups)
    taking = lax.all_gather(ensemble, "col", axis_index_groups=xc_groups)
    table, row_count = entry_table(pair_home, pair_local, blocks, own_z, own_xc)

    smem = pl.BlockSpec(memory_space=pltpu.SMEM)
    vmem = pl.BlockSpec(memory_space=pltpu.VMEM)
    part = pl.pallas_call(
        functools.partial(pair_kernel, blocks),
        out_shape=jax.ShapeDtypeStruct((XC * blocks, BLOCK), jnp.float32),
        in_specs=[smem] * 4 + [vmem] * 3,
        out_specs=vmem,
        scratch_shapes=[
            pltpu.VMEM((BLOCK, BLOCK), jnp.float32),
            pltpu.VMEM((XC * blocks, 8, BLOCK), jnp.float32),
            pltpu.SMEM((pair_local.shape[0],), jnp.int32),
        ],
        compiler_params=pltpu.CompilerParams(vmem_limit_bytes=40 * 1024 * 1024),
    )(table, row_count, shifts, live, lattice_offsets(), weighted, taking)

    part = part.reshape(XC, columns)
    part = lax.all_to_all(part, "col", 0, 0, axis_index_groups=xc_groups, tiled=True)
    part = jnp.sum(part, axis=0).reshape(lax.axis_size("mem"), -1)
    part = lax.all_to_all(part, "mem", 0, 0, tiled=True)
    return jnp.sum(part.reshape(LEVELS, -1, part.shape[1]), axis=1) / (MEMBERS - 1.0)


def solution(mesh):
    return jax.shard_map(
        shards,
        mesh=mesh,
        in_specs=(P("mem", "col"), P(None, "col"), P(), P(), P("col"), P(None, "col")),
        out_specs=P(None, ("col", "mem")),
        check_vma=False,
    )
```

```python
import functools

import jax
import jax.numpy as jnp
import numpy as np
from jax import lax
from jax.experimental import pallas as pl
from jax.experimental.pallas import tpu as pltpu
from jax.sharding import PartitionSpec as P

MEMBERS = 80
LEVELS = 4
SIDE = 16
BLOCK = 256
SPACING_KM = 200.0
HALF_WIDTH = 250.0
XC = 8
Z = 8
X = 4
GROUP = 4
MESH_ID = pl.DeviceIdType.MESH
LANES = 128


def gaspari_cohn(squared):
    scaled = jnp.sqrt(squared * (1.0 / (HALF_WIDTH * HALF_WIDTH)))
    near_part = (
        ((-0.25 * scaled + 0.5) * scaled + 0.625) * scaled - 5.0 / 3.0
    ) * scaled * scaled + 1.0
    bounded = jnp.maximum(scaled, 1.0)
    far_part = (
        ((((scaled * (1.0 / 12.0) - 0.5) * scaled + 0.625) * scaled + 5.0 / 3.0) * scaled - 5.0) * scaled
        + 4.0
        - (2.0 / 3.0) / bounded
    )
    return jnp.where(scaled <= 1.0, near_part, jnp.where(scaled <= 2.0, far_part, 0.0))


def lattice_offsets():
    giver = np.arange(SIDE)[:, None]
    lane = np.arange(BLOCK)[None, :]
    east = (giver - lane % SIDE) * SPACING_KM
    north = (SIDE // 2 - lane // SIDE) * SPACING_KM + 0 * giver
    return jnp.asarray(np.stack([east, north]).astype(np.float32))


def place():
    col = lax.axis_index("col")
    return col, col // XC, (col % XC) // 2, col % 2


def row_peer(z, x, core, slot):
    return {"col": z * XC + lax.rem(x + slot // 2, X) * 2 + lax.rem(core + slot % 2, 2)}


def column_peer(col, z, step):
    return {"col": col + (lax.rem(z + step, Z) - z) * XC}


def mirrored(slot):
    return (X - slot // 2) % X * 2 + slot % 2


def enter(peers):
    barrier = pltpu.get_barrier_semaphore()
    for peer in peers:
        pl.semaphore_signal(barrier, inc=1, device_id=peer, device_id_type=MESH_ID)
    pl.semaphore_wait(barrier, len(peers))


def turn(a, shift):
    return pltpu.roll(a, shift % a.shape[1], 1)


def make_table(home, local, count, blocks, z, x, core):
    lanes = home.shape[1]
    lane = lax.broadcasted_iota(jnp.int32, home.shape, 1)
    even = (lane & 1) == 0
    other_home = jnp.where(even, turn(home, -1), turn(home, 1))
    other_local = jnp.where(even, turn(local, -1), turn(local, 1))
    mine = ((home >> 3) == z) & ((other_home & 7) == x * 2 + core) & ((lane >> 1) < count)
    slot = ((((home >> 1) & 3) - x) & 3) * 2 + ((home ^ core) & 1)
    turned = ((other_home >> 3) - z) & 7
    word = (slot * blocks + local) | ((turned * blocks + other_local) << 8) | (lane << 16)
    rank = mine.astype(jnp.int32)
    step = 1
    while step < lanes:
        rank = rank + jnp.where(lane >= step, turn(rank, step), 0)
        step *= 2
    found = rank[:, lanes - LANES :]
    found = jnp.max(found, axis=1, keepdims=True)
    value = jnp.where(mine, word, -1)
    move = jnp.where(mine, lane - rank + 1, 0)
    step = 1
    while step < lanes:
        next_value, next_move = turn(value, -step), turn(move, -step)
        arrives, leaves = (next_move & step) != 0, (move & step) != 0
        value = jnp.where(arrives, next_value, jnp.where(leaves, -1, value))
        move = jnp.where(arrives, next_move, jnp.where(leaves, 0, move))
        step *= 2
    return value, jnp.broadcast_to(found, (home.shape[0], LANES))


def gather_kernel(
    blocks, ensemble, control, small, home, local,
    weighted, taking, table, found, east, north,
    seen, z_send, z_recv, x_send, x_recv, core_send, core_recv, row_send, row_recv, col_send, col_recv,
):
    col, z, x, core = place()
    member_rows, columns = ensemble.shape
    half = columns // 2
    level = (lax.axis_index("mem") * member_rows) // MEMBERS
    scale = jnp.zeros((1, columns), jnp.float32)
    for l in range(LEVELS):
        scale = jnp.where(level == l, control[l : l + 1, :].astype(jnp.float32), scale)
    weighted[0] = (ensemble[...].astype(jnp.float32) * scale).astype(jnp.bfloat16)
    taking[0] = ensemble[...]
    seen[pl.ds(pl.multiple_of(col * 8, 8), 8), :] = small[...]

    enter([row_peer(z, x, core, s) for s in range(1, XC)] + [column_peer(col, z, s) for s in range(1, Z)])

    sent = []

    def send(source, target, send_sem, recv_sem, peer):
        copy = pltpu.make_async_remote_copy(
            src_ref=source, dst_ref=target, send_sem=send_sem, recv_sem=recv_sem,
            device_id=peer, device_id_type=MESH_ID,
        )
        copy.start()
        sent.append(copy)
        return copy

    def part(ref, slot, c):
        return ref.at[slot, :, pl.ds(c * half, half)]

    def send_z(way, step, c):
        sign = 1 if way == 0 else -1
        return send(
            part(weighted, (-sign * step) % Z, c), part(weighted, (-sign * (step + 1)) % Z, c),
            z_send.at[way, step, c], z_recv.at[way, step, c], column_peer(col, z, sign % Z),
        )

    def send_x(way, step, c):
        sign = 1 if way == 0 else -1
        return send(
            part(taking, (-sign * step) % X * 2, c), part(taking, (-sign * (step + 1)) % X * 2, c),
            x_send.at[way, step, c], x_recv.at[way, step, c], row_peer(z, x, core, sign % X * 2),
        )

    def send_core(turned, c):
        return send(
            part(taking, turned * 2, c), part(taking, turned * 2 + 1, c),
            core_send.at[turned, c], core_recv.at[turned, c], row_peer(z, x, core, 1),
        )

    row_copies = []
    own_rows = seen.at[pl.ds(pl.multiple_of(col * 8, 8), 8), :]
    for s in range(1, XC):
        row_copies.append(send(own_rows, own_rows, row_send.at[s], row_recv.at[s], row_peer(z, x, core, s)))
    zs, xs, cores = {}, {}, []
    for c in range(2):
        for way in range(2):
            zs[way, 0, c] = send_z(way, 0, c)
            xs[way, 0, c] = send_x(way, 0, c)
    for c in range(2):
        cores.append(send_core(0, c))
    for copy in row_copies:
        copy.wait_recv()
    col_copies = []
    z_rows = seen.at[pl.ds(pl.multiple_of(z * 64, 64), 64), :]
    for s in range(1, Z):
        col_copies.append(send(z_rows, z_rows, col_send.at[s], col_recv.at[s], column_peer(col, z, s)))

    for step in range(4):
        for c in range(2):
            for way in range(2):
                if step < 3 or c == way:
                    zs[way, step, c].wait_recv()
                    if step < 2 or (step == 2 and c == way):
                        zs[way, step + 1, c] = send_z(way, step + 1, c)
            for way in range(2):
                turned = (-(1 if way == 0 else -1) * (step + 1)) % X
                if step == 0 or (step == 1 and c == way):
                    xs[way, step, c].wait_recv()
                    if step == 0 and c == way:
                        xs[way, 1, c] = send_x(way, 1, c)
                    cores.append(send_core(turned, c))
        if step == 0:
            for copy in col_copies:
                copy.wait_recv()
            owners = seen.shape[0] // 8
            count = seen[pl.ds(2, owners, stride=8), :]
            count = jnp.concatenate([count, count], axis=1).astype(jnp.int32)
            table[...], found[...] = make_table(home[...], local[...], count, blocks, z, x, core)
            east[...] = seen[pl.ds(0, owners, stride=8), :]
            north[...] = seen[pl.ds(1, owners, stride=8), :]
    for copy in cores:
        copy.wait_recv()
    for copy in sent:
        copy.wait_send()


def pair_kernel(blocks, table, found, east, north, offsets, weighted, ensemble, out, total, work, *grams):
    total[...] = jnp.zeros_like(total)

    def scan_row(row, base):
        def scan_entry(k, base):
            word = table[row, k]
            work[base] = (word & 0xFFFF) | ((row * 2 * LANES + (word >> 16)) << 16)
            return base + 1

        return lax.fori_loop(0, found[row, 0], scan_entry, base)

    amount = lax.fori_loop(0, table.shape[0], scan_row, jnp.int32(0))
    for g in range(GROUP - 1):
        work[amount + g] = -1

    lane = lax.broadcasted_iota(jnp.int32, (8, LANES), 1)

    def one(word, gram):
        live = word >= 0
        word = jnp.where(live, word, 0)
        receiver = word & 0xFF
        giver = (word >> 8) & 0xFF
        entry = word >> 16
        owner, place_in = entry >> 8, (entry & 0xFF) >> 1
        sign = (1 - 2 * (entry & 1)).astype(jnp.float32)
        shift_e = jnp.where(live, sign * east[owner, place_in], 1e5)
        shift_n = sign * north[owner, place_in]
        give = weighted[
            giver // blocks, :, pl.ds(pl.multiple_of((giver % blocks) * BLOCK, BLOCK), BLOCK)
        ]
        take = ensemble[
            receiver // blocks, :, pl.ds(pl.multiple_of((receiver % blocks) * BLOCK, BLOCK), BLOCK)
        ]
        gram[...] = lax.dot_general(
            give, take, (((0,), (0,)), ((), ())), preferred_element_type=jnp.float32
        )
        sums = [jnp.zeros((8, LANES), jnp.float32) for _ in range(2)]
        for half in range(2):
            rows_here = slice(8 * half, 8 * half + 8)
            parts = []
            for side in range(2):
                cols = slice(LANES * side, LANES * side + LANES)
                de = shift_e + offsets[0, rows_here, cols]
                dn = shift_n + offsets[1, rows_here, cols]
                tap = gaspari_cohn(de * de + dn * dn)
                parts.append(tap.astype(jnp.bfloat16).astype(jnp.float32))
            for k in range(8):
                turned = [pltpu.roll(p, 16 * k, 1) if k else p for p in parts]
                low = lane < 16 * k
                middle = jnp.where(low, turned[0], turned[1])
                first = jnp.where(low, 0.0, turned[0])
                last = jnp.where(low, turned[1], 0.0)
                at = 16 * k + 8 * half
                up = LANES + at
                sums[0] += middle * gram[at : at + 8, :LANES] + first * gram[up : up + 8, :LANES]
                sums[1] += last * gram[at : at + 8, LANES:] + middle * gram[up : up + 8, LANES:]
        return receiver, sums

    def some(n, carry):
        done = [one(work[n * GROUP + g], grams[g]) for g in range(GROUP)]
        for receiver, sums in done:
            total[receiver, :, :LANES] += sums[0]
            total[receiver, :, LANES:] += sums[1]
        return carry

    lax.fori_loop(0, (amount + GROUP - 1) // GROUP, some, 0)
    out[...] = jnp.sum(total[...], axis=1).reshape(out.shape)


def sum_kernel(part, out, rows_in, mine, pieces, row_send, row_recv, mem_send, mem_recv):
    _, z, x, core = place()
    mem = lax.axis_index("mem")
    mems = mine.shape[0]

    def mem_peer(step):
        return {"mem": lax.rem(mem + step, mems)}

    enter([row_peer(z, x, core, s) for s in range(1, XC)] + [mem_peer(s) for s in range(1, mems)])
    copies = []
    for s in range(1, XC):
        copy = pltpu.make_async_remote_copy(
            src_ref=part.at[s], dst_ref=rows_in.at[mirrored(s)],
            send_sem=row_send.at[s], recv_sem=row_recv.at[mirrored(s)],
            device_id=row_peer(z, x, core, s), device_id_type=MESH_ID,
        )
        copy.start()
        copies.append(copy)
    summed = part[0]
    for s in range(1, XC):
        copies[s - 1].wait()
    for s in range(1, XC):
        summed = summed + rows_in[s]
    each = summed.shape[0] // mems
    for m in range(mems):
        mine[m, :each, :] = summed[m * each : (m + 1) * each, :]
        mine[m, each:, :] = jnp.zeros((mine.shape[1] - each, BLOCK), jnp.float32)
    pieces[mem] = mine[mem]
    copies = []
    for s in range(1, mems):
        copy = pltpu.make_async_remote_copy(
            src_ref=mine.at[lax.rem(mem + s, mems)], dst_ref=pieces.at[mem],
            send_sem=mem_send.at[s], recv_sem=mem_recv.at[s],
            device_id=mem_peer(s), device_id_type=MESH_ID,
        )
        copy.start()
        copies.append(copy)
    for copy in copies:
        copy.wait()
    for l in range(LEVELS):
        first = l * (mems // LEVELS)
        both = pieces[first]
        for m in range(first + 1, first + mems // LEVELS):
            both = both + pieces[m]
        both = both / (MEMBERS - 1.0)
        for i in range(each):
            out[l : l + 1, i * BLOCK : (i + 1) * BLOCK] = both[i : i + 1, :]


def shards(ensemble, control, pair_home, pair_local, pair_count, pair_shift):
    member_rows, columns = ensemble.shape
    blocks = columns // BLOCK
    owners = lax.axis_size("col")
    mems = lax.axis_size("mem")
    small = jnp.concatenate(
        [pair_shift, jnp.broadcast_to(pair_count.astype(jnp.float32)[:, None], (1, LANES)), jnp.zeros((5, LANES), jnp.float32)]
    )
    home = pair_home.reshape(owners, -1)
    local = pair_local.reshape(owners, -1)
    smem = pl.BlockSpec(memory_space=pltpu.SMEM)
    vmem = pl.BlockSpec(memory_space=pltpu.VMEM)
    dma = pltpu.SemaphoreType.DMA

    weighted, taking, table, found, east, north = pl.pallas_call(
        functools.partial(gather_kernel, blocks),
        out_shape=(
            jax.ShapeDtypeStruct((Z, member_rows, columns), jnp.bfloat16),
            jax.ShapeDtypeStruct((XC, member_rows, columns), jnp.bfloat16),
            jax.ShapeDtypeStruct(home.shape, jnp.int32),
            jax.ShapeDtypeStruct((owners, LANES), jnp.int32),
            jax.ShapeDtypeStruct((owners, LANES), jnp.float32),
            jax.ShapeDtypeStruct((owners, LANES), jnp.float32),
        ),
        in_specs=[vmem] * 5,
        out_specs=[vmem] * 6,
        scratch_shapes=[
            pltpu.VMEM((owners * 8, LANES), jnp.float32),
            dma((2, 4, 2)), dma((2, 4, 2)), dma((2, 2, 2)), dma((2, 2, 2)), dma((X, 2)), dma((X, 2)),
            dma((XC,)), dma((XC,)), dma((Z,)), dma((Z,)),
        ],
        compiler_params=pltpu.CompilerParams(
            collective_id=0, has_side_effects=True, vmem_limit_bytes=40 * 1024 * 1024
        ),
    )(ensemble, control, small, home, local)

    part = pl.pallas_call(
        functools.partial(pair_kernel, blocks),
        out_shape=jax.ShapeDtypeStruct((XC, blocks, BLOCK), jnp.float32),
        in_specs=[smem] * 4 + [vmem] * 3,
        out_specs=vmem,
        scratch_shapes=[
            pltpu.VMEM((XC * blocks, 8, BLOCK), jnp.float32),
            pltpu.SMEM((pair_local.shape[0] + GROUP,), jnp.int32),
        ] + [pltpu.VMEM((BLOCK, BLOCK), jnp.float32)] * GROUP,
        compiler_params=pltpu.CompilerParams(vmem_limit_bytes=40 * 1024 * 1024),
    )(table, found, east, north, lattice_offsets(), weighted, taking)

    return pl.pallas_call(
        sum_kernel,
        out_shape=jax.ShapeDtypeStruct((LEVELS, columns // mems), jnp.float32),
        in_specs=[vmem],
        out_specs=vmem,
        scratch_shapes=[
            pltpu.VMEM((XC, blocks, BLOCK), jnp.float32),
            pltpu.VMEM((mems, 8, BLOCK), jnp.float32),
            pltpu.VMEM((mems, 8, BLOCK), jnp.float32),
            dma((XC,)), dma((XC,)), dma((mems,)), dma((mems,)),
        ],
        compiler_params=pltpu.CompilerParams(
            collective_id=1, has_side_effects=True, vmem_limit_bytes=8 * 1024 * 1024
        ),
    )(part)


def solution(mesh):
    return jax.shard_map(
        shards,
        mesh=mesh,
        in_specs=(P("mem", "col"), P(None, "col"), P(), P(), P("col"), P(None, "col")),
        out_specs=P(None, ("col", "mem")),
        check_vma=False,
    )
```

```python
import functools

import jax
import jax.numpy as jnp
import numpy as np
from jax import lax
from jax.experimental import pallas as pl
from jax.experimental.pallas import tpu as pltpu
from jax.sharding import PartitionSpec as P

MEMBERS = 80
LEVELS = 4
SIDE = 16
BLOCK = 256
SPACING_KM = 200.0
HALF_WIDTH = 250.0
XC = 8
CAP = 32
ROW_CAP = 16
STRIPE = 2 * CAP
Z = 8
X = 4
GROUP = 4
MESH_ID = pl.DeviceIdType.MESH
LANES = 128


def gaspari_cohn(squared):
    scaled = jnp.sqrt(squared * (1.0 / (HALF_WIDTH * HALF_WIDTH)))
    near_part = (
        ((-0.25 * scaled + 0.5) * scaled + 0.625) * scaled - 5.0 / 3.0
    ) * scaled * scaled + 1.0
    bounded = jnp.maximum(scaled, 1.0)
    far_part = (
        ((((scaled * (1.0 / 12.0) - 0.5) * scaled + 0.625) * scaled + 5.0 / 3.0) * scaled - 5.0) * scaled
        + 4.0
        - (2.0 / 3.0) / bounded
    )
    return jnp.where(scaled <= 1.0, near_part, jnp.where(scaled <= 2.0, far_part, 0.0))


def lattice_offsets():
    giver = np.arange(SIDE)[:, None]
    lane = np.arange(BLOCK)[None, :]
    east = (giver - lane % SIDE) * SPACING_KM
    north = (SIDE // 2 - lane // SIDE) * SPACING_KM + 0 * giver
    return jnp.asarray(np.stack([east, north]).astype(np.float32))


def place():
    col = lax.axis_index("col")
    return col, col // XC, (col % XC) // 2, col % 2


def row_peer(z, x, core, slot):
    return {"col": z * XC + lax.rem(x + slot // 2, X) * 2 + lax.rem(core + slot % 2, 2)}


def column_peer(col, z, step):
    return {"col": col + (lax.rem(z + step, Z) - z) * XC}


def mirrored(slot):
    return (X - slot // 2) % X * 2 + slot % 2


def enter(peers):
    barrier = pltpu.get_barrier_semaphore()
    for peer in peers:
        pl.semaphore_signal(barrier, inc=1, device_id=peer, device_id_type=MESH_ID)
    pl.semaphore_wait(barrier, len(peers))


def turn(a, shift):
    return pltpu.roll(a, shift % a.shape[1], 1)


def own_entries(home, local, count, z, x, core):
    lane = lax.broadcasted_iota(jnp.int32, home.shape, 1)
    even = (lane & 1) == 0
    other_home = jnp.where(even, turn(home, -1), turn(home, 1))
    other_local = jnp.where(even, turn(local, -1), turn(local, 1))
    mine = ((home >> 3) == z) & ((other_home & 7) == x * 2 + core) & ((lane >> 1) < count)
    slot = ((((home >> 1) & 3) - x) & 3) * 2 + ((home ^ core) & 1)
    turned = ((other_home >> 3) - z) & 7
    return mine, slot, other_local, turned


def row_rank(mine):
    rank = mine.astype(jnp.int32)
    lane = lax.broadcasted_iota(jnp.int32, rank.shape, 1)
    step = 1
    while step < rank.shape[1]:
        rank = rank + jnp.where(lane >= step, turn(rank, step), 0)
        step *= 2
    return rank - 1


def pack_rows(mine, rank, arrays):
    lane = lax.broadcasted_iota(jnp.int32, rank.shape, 1)
    move = jnp.where(mine, lane - rank, 0)
    arrays = [jnp.where(mine, a, 0) for a in arrays]
    step = 1
    while step < rank.shape[1]:
        next_move = turn(move, -step)
        arrives, leaves = (next_move & step) != 0, (move & step) != 0
        arrays = [jnp.where(arrives, turn(a, -step), jnp.where(leaves, 0, a)) for a in arrays]
        move = jnp.where(arrives, next_move, jnp.where(leaves, 0, move))
        step *= 2
    return arrays


def group_rank(mine, turned):
    rows, lanes = mine.shape
    line = lax.broadcasted_iota(jnp.int32, (rows, lanes), 0)
    lane = lax.broadcasted_iota(jnp.int32, (rows, lanes), 1)
    rank = jnp.zeros((rows, lanes), jnp.int32)
    for t in range(0, Z, 2):
        low, high = mine & (turned == t), mine & (turned == t + 1)
        upto = low.astype(jnp.int32) + (high.astype(jnp.int32) << 16)
        step = 1
        while step < lanes:
            upto = upto + jnp.where(lane >= step, turn(upto, step), 0)
            step *= 2
        whole = jnp.broadcast_to(upto[:, lanes - 1 :], (rows, lanes))
        above = whole
        step = 1
        while step < rows:
            above = above + jnp.where(line >= step, pltpu.roll(above, step, 0), 0)
            step *= 2
        upto = upto + above - whole
        rank = jnp.where(low, (upto & 0xFFFF) - 1, jnp.where(high, (upto >> 16) - 1, rank))
    return rank


def make_lists(mine, slot, local, giver, turned, east, north):
    in_row = row_rank(mine)
    kept = mine & (in_row < ROW_CAP)
    rank = group_rank(kept, turned)
    kept = kept & (rank < CAP)
    place_at = turned * STRIPE + (rank >> 2) * 8 + (rank & 3)
    code = slot | (local << 3) | (giver << 8) | (place_at << 13) | (1 << 22)
    rank = row_rank(kept)
    code, east, north = pack_rows(kept, rank, [code, east, north])
    rows, positions = code.shape[0], Z * STRIPE
    place_at = jnp.where(code >= (1 << 22), (code >> 13) & 511, -1)
    lane = lax.broadcasted_iota(jnp.int32, (rows, positions), 1)
    words = jnp.zeros((rows, positions), jnp.int32)
    easts = jnp.zeros((rows, positions), jnp.float32)
    norths = jnp.zeros((rows, positions), jnp.float32)
    for j in range(ROW_CAP):
        hit = place_at[:, j : j + 1] == lane
        words = words + jnp.where(hit, code[:, j : j + 1], 0)
        easts = easts + jnp.where(hit, east[:, j : j + 1], 0.0)
        norths = norths + jnp.where(hit, north[:, j : j + 1], 0.0)
    words, easts, norths = [jnp.sum(v, axis=0, keepdims=True) for v in (words, easts, norths)]
    return words, jnp.where(words >= (1 << 22), easts, 1e5), norths, mine & ~kept


def pair_sums(gram, offsets, shifts):
    amount = len(shifts)
    squares = []
    for e, n in shifts:
        de, dn = e + offsets[0], n + offsets[1]
        squares.append(de * de + dn * dn)
    taps = gaspari_cohn(jnp.concatenate(squares)).astype(jnp.bfloat16).astype(jnp.float32)
    left, right = taps[:, :LANES], taps[:, LANES:]
    lane = lax.broadcasted_iota(jnp.int32, left.shape, 1)
    sums = [jnp.zeros(left.shape, jnp.float32) for _ in range(2)]

    def rows(k, side):
        return gram[:, k, :, LANES * side : LANES * side + LANES].reshape(left.shape)

    for k in range(8):
        low = lane < 16 * k
        a, b = turn(left, 16 * k), turn(right, 16 * k)
        middle = jnp.where(low, a, b)
        first = jnp.where(low, 0.0, a)
        last = jnp.where(low, b, 0.0)
        sums[0] = sums[0] + (middle * rows(k, 0) + first * rows(8 + k, 0))
        sums[1] = sums[1] + (last * rows(k, 1) + middle * rows(8 + k, 1))
    sums = jnp.concatenate([jnp.sum(s.reshape(amount, SIDE, LANES), axis=1) for s in sums], axis=1)
    return sums


def products(give, take):
    gram = lax.dot_general(give, take, (((0,), (0,)), ((), ())), preferred_element_type=jnp.float32)
    return gram.reshape(SIDE, SIDE, BLOCK)


def gather_kernel(
    blocks, ensemble, control, small, live, home, local, offsets, *refs,
):
    weighted, refs = refs[:Z], refs[Z:]
    taking, part_out, table, found, extra, east, north = refs[:7]
    (
        seen, counts, words, shifts, words_s, shifts_s, row_sums, gram, local_sem,
        z_send, z_recv, x_send, x_recv, core_send, core_recv, row_send, row_recv, col_send, col_recv,
    ) = refs[7:]
    col, z, x, core = place()
    member_rows, columns = ensemble.shape
    half = blocks // 2
    level = (lax.axis_index("mem") * member_rows) // MEMBERS
    scale = jnp.zeros((1, columns), jnp.float32)
    for l in range(LEVELS):
        scale = jnp.where(level == l, control[l : l + 1, :].astype(jnp.float32), scale)
    for b in range(blocks):
        own = ensemble[:, b * BLOCK : (b + 1) * BLOCK]
        taking[b] = own
        weighted[0][b] = (own.astype(jnp.float32) * scale[:, b * BLOCK : (b + 1) * BLOCK]).astype(jnp.bfloat16)
    seen[pl.ds(pl.multiple_of(col * 8, 8), 8), :] = small[...]
    counts[pl.ds(pl.multiple_of(col * 8, 8), 8), :] = live[...]

    enter([row_peer(z, x, core, s) for s in range(1, XC)] + [column_peer(col, z, s) for s in range(1, Z)])

    sent = []

    def send(source, target, send_sem, recv_sem, peer):
        copy = pltpu.make_async_remote_copy(
            src_ref=source, dst_ref=target, send_sem=send_sem, recv_sem=recv_sem,
            device_id=peer, device_id_type=MESH_ID,
        )
        copy.start()
        sent.append(copy)
        return copy

    def part(ref, slot, c):
        return ref.at[pl.ds(slot * blocks + c * half, half)]

    def send_z(way, step, c):
        sign = 1 if way == 0 else -1
        return send(
            part(weighted[(-sign * step) % Z], 0, c), part(weighted[(-sign * (step + 1)) % Z], 0, c),
            z_send.at[way, step, c], z_recv.at[way, step, c], column_peer(col, z, sign % Z),
        )

    def send_x(way, step, c):
        sign = 1 if way == 0 else -1
        return send(
            part(taking, (-sign * step) % X * 2, c), part(taking, (-sign * (step + 1)) % X * 2, c),
            x_send.at[way, step, c], x_recv.at[way, step, c], row_peer(z, x, core, sign % X * 2),
        )

    def send_core(turned, c):
        return send(
            part(taking, turned * 2, c), part(taking, turned * 2 + 1, c),
            core_send.at[turned, c], core_recv.at[turned, c], row_peer(z, x, core, 1),
        )

    row_copies = []
    for i, ref in enumerate((seen, counts)):
        rows = ref.at[pl.ds(pl.multiple_of(col * 8, 8), 8), :]
        for s in range(1, XC):
            row_copies.append(send(rows, rows, row_send.at[i, s], row_recv.at[i, s], row_peer(z, x, core, s)))
    zs, xs, cores = {}, {}, []
    for c in range(2):
        for way in range(2):
            zs[way, 0, c] = send_z(way, 0, c)
            xs[way, 0, c] = send_x(way, 0, c)
    for c in range(2):
        cores.append(send_core(0, c))
    for copy in row_copies:
        copy.wait_recv()
    col_copies = []
    for i, ref in enumerate((seen, counts)):
        rows = ref.at[pl.ds(pl.multiple_of(z * 64, 64), 64), :]
        for s in range(1, Z):
            col_copies.append(send(rows, rows, col_send.at[i, s], col_recv.at[i, s], column_peer(col, z, s)))

    def arrivals(step, c):
        for way in range(2):
            if step < 3 or c == way:
                zs[way, step, c].wait_recv()
                if step < 2 or (step == 2 and c == way):
                    zs[way, step + 1, c] = send_z(way, step + 1, c)
        for way in range(2):
            turned = (-(1 if way == 0 else -1) * (step + 1)) % X
            if step == 0 or (step == 1 and c == way):
                xs[way, step, c].wait_recv()
                if step == 0 and c == way:
                    xs[way, 1, c] = send_x(way, 1, c)
                cores.append(send_core(turned, c))

    def lists():
        for copy in col_copies:
            copy.wait_recv()
        owners = seen.shape[0] // 8
        rows = [seen[pl.ds(i, owners, stride=8), :] for i in range(4)]
        east[...] = jnp.concatenate(rows[0:2], axis=1)
        north[...] = jnp.concatenate(rows[2:4], axis=1)
        count = counts[pl.ds(0, owners, stride=8), :]
        count = jnp.concatenate([count, count], axis=1)
        mine, slot, giver, turned = own_entries(home[...], local[...], count, z, x, core)
        lane = lax.broadcasted_iota(jnp.int32, mine.shape, 1)
        word, shift_e, shift_n, left = make_lists(mine, slot, local[...], giver, turned, east[...], north[...])
        words[...] = jnp.broadcast_to(word, words.shape)
        shifts[0:1, :] = shift_e
        shifts[1:2, :] = shift_n
        receiver = slot * blocks + local[...]
        rank = row_rank(left)
        word = receiver | ((turned * blocks + giver) << 8) | (lane << 16)
        table[...] = pack_rows(left, rank, [word])[0]
        amount = jnp.max(rank, axis=1, keepdims=True) + 1
        found[...] = jnp.broadcast_to(amount, found.shape)
        extra[...] = jnp.broadcast_to(jnp.max(amount, axis=0, keepdims=True), extra.shape)
        copies = [
            pltpu.make_async_copy(words, words_s, local_sem.at[0]),
            pltpu.make_async_copy(shifts, shifts_s, local_sem.at[1]),
        ]
        for copy in copies:
            copy.start()
        for copy in copies:
            copy.wait()

    def work(turned):
        def some(n, carry):
            pairs = []
            for g in range(GROUP):
                at = turned * STRIPE + n * 8 + g
                word = words_s[0, at]
                gram[g] = products(
                    weighted[turned][(word >> 8) & 31], taking[(word & 7) * blocks + ((word >> 3) & 31)]
                )
                pairs.append((shifts_s[0, at], shifts_s[1, at]))
            sums = pair_sums(gram, offsets, pairs)
            row_sums[turned * (STRIPE // 8) + n] = jnp.concatenate([sums, jnp.zeros((8 - GROUP, BLOCK), jnp.float32)])
            return carry

        lax.fori_loop(0, STRIPE // 8, some, 0)

    arrivals(0, 0)
    arrivals(0, 1)
    lists()
    arrivals(1, 0)
    arrivals(1, 1)
    for copy in cores:
        copy.wait_recv()
    work(0)
    work(7)
    arrivals(2, 0)
    work(1)
    work(6)
    arrivals(2, 1)
    work(2)
    work(5)
    work(3)
    arrivals(3, 0)
    arrivals(3, 1)
    work(4)
    count = part_out.shape[0]
    taken = (words[0:1, :] & 7) * blocks + ((words[0:1, :] >> 3) & 31)
    hot = (lax.broadcasted_iota(jnp.int32, (count, taken.shape[1]), 0) == taken).astype(jnp.float32)
    part_out[...] = jnp.dot(
        hot, row_sums[...].reshape(taken.shape[1], BLOCK),
        preferred_element_type=jnp.float32, precision=lax.Precision.HIGHEST,
    )
    for copy in sent:
        copy.wait_send()


def extra_kernel(blocks, extra, part, table, found, east, north, offsets, *refs):
    weighted, taking, out = refs[:Z], refs[Z], refs[Z + 1]
    table_s, found_s, east_s, north_s, gram, sems = refs[Z + 2 :]
    out[...] = part[...]

    @pl.when(extra[0, 0] > 0)
    def _():
        copies = [
            pltpu.make_async_copy(a, b, sems.at[i])
            for i, (a, b) in enumerate([(table, table_s), (found, found_s), (east, east_s), (north, north_s)])
        ]
        for copy in copies:
            copy.start()
        for copy in copies:
            copy.wait()

        def row_step(row, carry):
            def entry_step(k, carry):
                word = table_s[row, k]
                receiver, giver, lane = word & 0xFF, (word >> 8) & 0xFF, word >> 16
                take = taking[receiver]
                from_slot = giver // blocks
                for t in range(Z):

                    @pl.when(from_slot == t)
                    def _():
                        gram[0] = products(weighted[t][giver - t * blocks], take)

                sums = pair_sums(gram, offsets, [(east_s[row, lane], north_s[row, lane])])
                out[pl.ds(receiver, 1), :] += sums
                return carry

            return lax.fori_loop(0, found_s[row, 0], entry_step, carry)

        lax.fori_loop(0, table.shape[0], row_step, 0)


def sum_kernel(part, out, rows_in, mine, pieces, row_send, row_recv, mem_send, mem_recv):
    _, z, x, core = place()
    mem = lax.axis_index("mem")
    mems = mine.shape[0]

    def mem_peer(step):
        return {"mem": lax.rem(mem + step, mems)}

    enter([row_peer(z, x, core, s) for s in range(1, XC)] + [mem_peer(s) for s in range(1, mems)])
    copies = []
    for s in range(1, XC):
        copy = pltpu.make_async_remote_copy(
            src_ref=part.at[s], dst_ref=rows_in.at[mirrored(s)],
            send_sem=row_send.at[s], recv_sem=row_recv.at[mirrored(s)],
            device_id=row_peer(z, x, core, s), device_id_type=MESH_ID,
        )
        copy.start()
        copies.append(copy)
    summed = part[0]
    for s in range(1, XC):
        copies[s - 1].wait()
    for s in range(1, XC):
        summed = summed + rows_in[s]
    each = summed.shape[0] // mems
    for m in range(mems):
        mine[m, :each, :] = summed[m * each : (m + 1) * each, :]
        mine[m, each:, :] = jnp.zeros((mine.shape[1] - each, BLOCK), jnp.float32)
    pieces[mem] = mine[mem]
    copies = []
    for s in range(1, mems):
        copy = pltpu.make_async_remote_copy(
            src_ref=mine.at[lax.rem(mem + s, mems)], dst_ref=pieces.at[mem],
            send_sem=mem_send.at[s], recv_sem=mem_recv.at[s],
            device_id=mem_peer(s), device_id_type=MESH_ID,
        )
        copy.start()
        copies.append(copy)
    for copy in copies:
        copy.wait()
    for l in range(LEVELS):
        first = l * (mems // LEVELS)
        both = pieces[first]
        for m in range(first + 1, first + mems // LEVELS):
            both = both + pieces[m]
        both = both / (MEMBERS - 1.0)
        for i in range(each):
            out[l : l + 1, i * BLOCK : (i + 1) * BLOCK] = both[i : i + 1, :]


def shards(ensemble, control, pair_home, pair_local, pair_count, pair_shift):
    member_rows, columns = ensemble.shape
    blocks = columns // BLOCK
    owners = lax.axis_size("col")
    mems = lax.axis_size("mem")
    entries = 2 * pair_shift.shape[1]
    sign = jnp.asarray(np.array([1.0, -1.0], np.float32))
    both = (pair_shift[:, :, None] * sign).reshape(2, entries)
    small = jnp.concatenate([both.reshape(4, LANES), jnp.zeros((4, LANES), jnp.float32)])
    live = jnp.broadcast_to(pair_count[:, None], (8, LANES))
    home = pair_home.reshape(owners, entries)
    local = pair_local.reshape(owners, entries)
    offsets = lattice_offsets()
    smem = pl.BlockSpec(memory_space=pltpu.SMEM)
    vmem = pl.BlockSpec(memory_space=pltpu.VMEM)
    dma = pltpu.SemaphoreType.DMA
    shape = jax.ShapeDtypeStruct
    positions = Z * STRIPE

    *weighted, taking, part, table, found, extra, east, north = pl.pallas_call(
        functools.partial(gather_kernel, blocks),
        out_shape=[shape((blocks, member_rows, BLOCK), jnp.bfloat16)] * Z + [
            shape((XC * blocks, member_rows, BLOCK), jnp.bfloat16),
            shape((XC * blocks, BLOCK), jnp.float32),
            shape(home.shape, jnp.int32),
            shape((owners, LANES), jnp.int32),
            shape((8, LANES), jnp.int32),
            shape(home.shape, jnp.float32),
            shape(home.shape, jnp.float32),
        ],
        in_specs=[vmem] * 7,
        out_specs=[vmem] * (Z + 7),
        scratch_shapes=[
            pltpu.VMEM((owners * 8, LANES), jnp.float32),
            pltpu.VMEM((owners * 8, LANES), jnp.int32),
            pltpu.VMEM((8, positions), jnp.int32),
            pltpu.VMEM((8, positions), jnp.float32),
            pltpu.SMEM((8, positions), jnp.int32),
            pltpu.SMEM((8, positions), jnp.float32),
            pltpu.VMEM((positions // 8, 8, BLOCK), jnp.float32),
            pltpu.VMEM((GROUP, SIDE, SIDE, BLOCK), jnp.float32),
            dma((2,)),
            dma((2, 4, 2)), dma((2, 4, 2)), dma((2, 2, 2)), dma((2, 2, 2)), dma((X, 2)), dma((X, 2)),
            dma((2, XC)), dma((2, XC)), dma((2, Z)), dma((2, Z)),
        ],
        compiler_params=pltpu.CompilerParams(
            collective_id=0, has_side_effects=True, vmem_limit_bytes=28 * 1024 * 1024
        ),
    )(ensemble, control, small, live, home, local, offsets)

    part = pl.pallas_call(
        functools.partial(extra_kernel, blocks),
        out_shape=shape(part.shape, part.dtype),
        in_specs=[smem] + [vmem] * (Z + 7),
        out_specs=vmem,
        scratch_shapes=[
            pltpu.SMEM(table.shape, jnp.int32), pltpu.SMEM(found.shape, jnp.int32),
            pltpu.SMEM(east.shape, jnp.float32), pltpu.SMEM(north.shape, jnp.float32),
            pltpu.VMEM((1, SIDE, SIDE, BLOCK), jnp.float32),
            dma((4,)),
        ],
        compiler_params=pltpu.CompilerParams(vmem_limit_bytes=24 * 1024 * 1024),
    )(extra, part, table, found, east, north, offsets, *weighted, taking)
    part = part.reshape(XC, blocks, BLOCK)

    return pl.pallas_call(
        sum_kernel,
        out_shape=jax.ShapeDtypeStruct((LEVELS, columns // mems), jnp.float32),
        in_specs=[vmem],
        out_specs=vmem,
        scratch_shapes=[
            pltpu.VMEM((XC, blocks, BLOCK), jnp.float32),
            pltpu.VMEM((mems, 8, BLOCK), jnp.float32),
            pltpu.VMEM((mems, 8, BLOCK), jnp.float32),
            dma((XC,)), dma((XC,)), dma((mems,)), dma((mems,)),
        ],
        compiler_params=pltpu.CompilerParams(
            collective_id=1, has_side_effects=True, vmem_limit_bytes=8 * 1024 * 1024
        ),
    )(part)


def solution(mesh):
    return jax.shard_map(
        shards,
        mesh=mesh,
        in_specs=(P("mem", "col"), P(None, "col"), P(), P(), P("col"), P(None, "col")),
        out_specs=P(None, ("col", "mem")),
        check_vma=False,
    )
```

```python
import functools

import jax
import jax.numpy as jnp
import numpy as np
from jax import lax
from jax.experimental import pallas as pl
from jax.experimental.pallas import tpu as pltpu
from jax.sharding import PartitionSpec as P

MEMBERS = 80
LEVELS = 4
SIDE = 16
BLOCK = 256
SPACING_KM = 200.0
HALF_WIDTH = 250.0
XC = 8
Z = 8
X = 4
LANES = 128
BATCH = 4
GROUP = 8
ROW_CAP = 16
SLOTS = ((0, 7, 1, 6, 2), (5, 3), (4,))
CAPS = (160, 80, 48)
STARTS = (0, 160, 240)
POSITIONS = 384
USED = 1 << 25
MESH_ID = pl.DeviceIdType.MESH


def gaspari_cohn(squared):
    scaled = jnp.sqrt(squared * (1.0 / (HALF_WIDTH * HALF_WIDTH)))
    near_part = (
        ((-0.25 * scaled + 0.5) * scaled + 0.625) * scaled - 5.0 / 3.0
    ) * scaled * scaled + 1.0
    bounded = jnp.maximum(scaled, 1.0)
    far_part = (
        ((((scaled * (1.0 / 12.0) - 0.5) * scaled + 0.625) * scaled + 5.0 / 3.0) * scaled - 5.0) * scaled
        + 4.0
        - (2.0 / 3.0) / bounded
    )
    return jnp.where(scaled <= 1.0, near_part, jnp.where(scaled <= 2.0, far_part, 0.0))


def tap_rows(east, north):
    shape = (east.shape[0] if east.ndim else 1, BLOCK)
    lane = lax.broadcasted_iota(jnp.int32, shape, 1) + SIDE // 2
    de = east - SPACING_KM * ((lane & (SIDE - 1)) - SIDE // 2).astype(jnp.float32)
    dn = north + SPACING_KM * (SIDE // 2 - (lane >> 4)).astype(jnp.float32)
    return gaspari_cohn(de * de + dn * dn).astype(jnp.bfloat16).astype(jnp.float32)


def place():
    col = lax.axis_index("col")
    return col, col // XC, (col % XC) // 2, col % 2


def row_peer(z, x, core, slot):
    return {"col": z * XC + lax.rem(x + slot // 2, X) * 2 + lax.rem(core + slot % 2, 2)}


def column_peer(col, z, step):
    return {"col": col + (lax.rem(z + step, Z) - z) * XC}


def mirrored(slot):
    return (X - slot // 2) % X * 2 + slot % 2


def enter(peers):
    barrier = pltpu.get_barrier_semaphore()
    for peer in peers:
        pl.semaphore_signal(barrier, inc=1, device_id=peer, device_id_type=MESH_ID)
    pl.semaphore_wait(barrier, len(peers))


def turn(a, shift):
    return pltpu.roll(a, shift % a.shape[1], 1)


def own_entries(home, local, count, z, x, core):
    lane = lax.broadcasted_iota(jnp.int32, home.shape, 1)
    even = (lane & 1) == 0
    other_home = jnp.where(even, turn(home, -1), turn(home, 1))
    other_local = jnp.where(even, turn(local, -1), turn(local, 1))
    mine = ((home >> 3) == z) & ((other_home & 7) == x * 2 + core) & ((lane >> 1) < count)
    slot = ((((home >> 1) & 3) - x) & 3) * 2 + ((home ^ core) & 1)
    turned = ((other_home >> 3) - z) & 7
    return mine, slot, other_local, turned


def by_slot(turned, values):
    found = jnp.zeros_like(turned)
    for t, value in values.items():
        found = jnp.where(turned == t, value, found)
    return found


def row_rank(mine):
    rank = mine.astype(jnp.int32)
    lane = lax.broadcasted_iota(jnp.int32, rank.shape, 1)
    step = 1
    while step < rank.shape[1]:
        rank = rank + jnp.where(lane >= step, turn(rank, step), 0)
        step *= 2
    return rank - 1


def pack_rows(mine, rank, arrays):
    lane = lax.broadcasted_iota(jnp.int32, rank.shape, 1)
    move = jnp.where(mine, lane - rank, 0)
    arrays = [jnp.where(mine, a, 0) for a in arrays]
    step = 1
    while step < rank.shape[1]:
        next_move = turn(move, -step)
        arrives, leaves = (next_move & step) != 0, (move & step) != 0
        arrays = [jnp.where(arrives, turn(a, -step), jnp.where(leaves, 0, a)) for a in arrays]
        move = jnp.where(arrives, next_move, jnp.where(leaves, 0, move))
        step *= 2
    return arrays


def group_rank(mine, group):
    rows, lanes = mine.shape
    line = lax.broadcasted_iota(jnp.int32, (rows, lanes), 0)
    lane = lax.broadcasted_iota(jnp.int32, (rows, lanes), 1)
    rank = jnp.zeros((rows, lanes), jnp.int32)
    for t in range(0, len(CAPS), 2):
        low, high = mine & (group == t), mine & (group == t + 1)
        upto = low.astype(jnp.int32) + (high.astype(jnp.int32) << 16)
        step = 1
        while step < lanes:
            upto = upto + jnp.where(lane >= step, turn(upto, step), 0)
            step *= 2
        whole = jnp.broadcast_to(upto[:, lanes - 1 :], (rows, lanes))
        above = whole
        step = 1
        while step < rows:
            above = above + jnp.where(line >= step, pltpu.roll(above, step, 0), 0)
            step *= 2
        upto = upto + above - whole
        rank = jnp.where(low, (upto & 0xFFFF) - 1, jnp.where(high, (upto >> 16) - 1, rank))
    return rank


def make_lists(mine, slot, local, giver, turned, east, north, blocks):
    in_row = row_rank(mine)
    kept = mine & (in_row < ROW_CAP)
    group = by_slot(turned, {t: g for g, slots in enumerate(SLOTS) for t in slots})
    rank = group_rank(kept, group)
    kept = kept & (rank < by_slot(group, dict(enumerate(CAPS))))
    place_at = by_slot(group, dict(enumerate(STARTS))) + rank
    giver = giver + by_slot(turned, {t: i * blocks for slots in SLOTS for i, t in enumerate(slots)})
    code = slot | (local << 3) | (giver << 8) | (place_at << 15) | USED
    rank = row_rank(kept)
    code, east, north = pack_rows(kept, rank, [code, east, north])
    rows = code.shape[0]
    place_at = jnp.where(code >= USED, (code >> 15) & 1023, -1)
    lane = lax.broadcasted_iota(jnp.int32, (rows, POSITIONS), 1)
    words = jnp.zeros((rows, POSITIONS), jnp.int32)
    easts = jnp.zeros((rows, POSITIONS), jnp.float32)
    norths = jnp.zeros((rows, POSITIONS), jnp.float32)
    for j in range(ROW_CAP):
        hit = place_at[:, j : j + 1] == lane
        words = words + jnp.where(hit, code[:, j : j + 1], 0)
        easts = easts + jnp.where(hit, east[:, j : j + 1], 0.0)
        norths = norths + jnp.where(hit, north[:, j : j + 1], 0.0)
    words, easts, norths = [jnp.sum(v, axis=0, keepdims=True) for v in (words, easts, norths)]
    return words, jnp.where(words >= USED, easts, 1e5), norths, mine & ~kept


def pair_sums(gram, rows):
    amount = len(rows)
    within = lax.broadcasted_iota(jnp.int32, (SIDE, BLOCK), 1) & (SIDE - 1)
    within = jnp.abs(within - lax.broadcasted_iota(jnp.int32, (SIDE, BLOCK), 0)) <= SIDE // 4
    taps = jnp.concatenate([
        jnp.where(within, pltpu.roll(jnp.broadcast_to(r, (SIDE, BLOCK)), 0, 1, stride=1, stride_axis=0), 0.0)
        for r in rows
    ])
    left, right = taps[:, :LANES], taps[:, LANES:]
    lane = lax.broadcasted_iota(jnp.int32, left.shape, 1)
    sums = [jnp.zeros(left.shape, jnp.float32) for _ in range(2)]

    def part(k, side):
        return gram[:, k, :, LANES * side : LANES * side + LANES].reshape(left.shape)

    for k in range(8):
        low = lane < 16 * k
        a, b = turn(left, 16 * k), turn(right, 16 * k)
        middle = jnp.where(low, a, b)
        sums[0] = sums[0] + middle * part(k, 0)
        sums[1] = sums[1] + middle * part(8 + k, 1)
        if k < 4:
            sums[0] = sums[0] + jnp.where(low, 0.0, a) * part(8 + k, 0)
        else:
            sums[1] = sums[1] + jnp.where(low, b, 0.0) * part(k, 1)
    return jnp.concatenate([jnp.sum(s.reshape(amount, SIDE, LANES), axis=1) for s in sums], axis=1)


def products(give, take):
    gram = lax.dot_general(give, take, (((0,), (0,)), ((), ())), preferred_element_type=jnp.float32)
    return gram.reshape(SIDE, SIDE, BLOCK)


def gather_kernel(
    blocks, ensemble, control, small, live, home, local, *refs,
):
    givers, refs = refs[:3], refs[3:]
    taking, part_out, table, found, extra, east, north = refs[:7]
    (
        seen, counts, words, taps, words_s, row_sums, gram_a, gram_b, local_sem,
        z_send, z_recv, x_send, x_recv, core_send, core_recv, row_send, row_recv, col_send, col_recv,
    ) = refs[7:]
    col, z, x, core = place()
    member_rows, columns = ensemble.shape
    half = blocks // 2
    level = (lax.axis_index("mem") * member_rows) // MEMBERS
    scale = jnp.zeros((1, columns), jnp.float32)
    for l in range(LEVELS):
        scale = jnp.where(level == l, control[l : l + 1, :].astype(jnp.float32), scale)
    for b in range(blocks):
        own = ensemble[:, b * BLOCK : (b + 1) * BLOCK]
        taking[b] = own
        givers[0][b] = (own.astype(jnp.float32) * scale[:, b * BLOCK : (b + 1) * BLOCK]).astype(jnp.bfloat16)
    seen[pl.ds(pl.multiple_of(col * 8, 8), 8), :] = small[...]
    counts[pl.ds(pl.multiple_of(col * 8, 8), 8), :] = live[...]

    enter([row_peer(z, x, core, s) for s in range(1, XC)] + [column_peer(col, z, s) for s in range(1, Z)])

    sent = []

    def send(source, target, send_sem, recv_sem, peer):
        copy = pltpu.make_async_remote_copy(
            src_ref=source, dst_ref=target, send_sem=send_sem, recv_sem=recv_sem,
            device_id=peer, device_id_type=MESH_ID,
        )
        copy.start()
        sent.append(copy)
        return copy

    def part(ref, slot, c):
        return ref.at[pl.ds(slot * blocks + c * half, half)]

    def giver_part(turned, c):
        for ref, slots in zip(givers, SLOTS):
            if turned in slots:
                return part(ref, slots.index(turned), c)

    def send_z(way, step, c):
        sign = 1 if way == 0 else -1
        return send(
            giver_part(-sign * step % Z, c), giver_part(-sign * (step + 1) % Z, c),
            z_send.at[way, step, c], z_recv.at[way, step, c], column_peer(col, z, sign % Z),
        )

    def send_x(way, step, c):
        sign = 1 if way == 0 else -1
        return send(
            part(taking, (-sign * step) % X * 2, c), part(taking, (-sign * (step + 1)) % X * 2, c),
            x_send.at[way, step, c], x_recv.at[way, step, c], row_peer(z, x, core, sign % X * 2),
        )

    def send_core(turned, c):
        return send(
            part(taking, turned * 2, c), part(taking, turned * 2 + 1, c),
            core_send.at[turned, c], core_recv.at[turned, c], row_peer(z, x, core, 1),
        )

    row_copies = []
    for i, ref in enumerate((seen, counts)):
        rows = ref.at[pl.ds(pl.multiple_of(col * 8, 8), 8), :]
        for s in range(1, XC):
            row_copies.append(send(rows, rows, row_send.at[i, s], row_recv.at[i, s], row_peer(z, x, core, s)))
    zs, xs, cores = {}, {}, []
    for c in range(2):
        for way in range(2):
            zs[way, 0, c] = send_z(way, 0, c)
            xs[way, 0, c] = send_x(way, 0, c)
    for c in range(2):
        cores.append(send_core(0, c))
    for copy in row_copies:
        copy.wait_recv()
    col_copies = []
    for i, ref in enumerate((seen, counts)):
        rows = ref.at[pl.ds(pl.multiple_of(z * 64, 64), 64), :]
        for s in range(1, Z):
            col_copies.append(send(rows, rows, col_send.at[i, s], col_recv.at[i, s], column_peer(col, z, s)))

    def arrivals(step, c):
        for way in range(2):
            if step < 3 or c == way:
                zs[way, step, c].wait_recv()
                if step < 2 or (step == 2 and c == way):
                    zs[way, step + 1, c] = send_z(way, step + 1, c)
        for way in range(2):
            turned = (-(1 if way == 0 else -1) * (step + 1)) % X
            if step == 0 or (step == 1 and c == way):
                xs[way, step, c].wait_recv()
                if step == 0 and c == way:
                    xs[way, 1, c] = send_x(way, 1, c)
                cores.append(send_core(turned, c))

    def lists():
        for copy in col_copies:
            copy.wait_recv()
        owners = seen.shape[0] // 8
        rows = [seen[pl.ds(i, owners, stride=8), :] for i in range(4)]
        east[...] = jnp.concatenate(rows[0:2], axis=1)
        north[...] = jnp.concatenate(rows[2:4], axis=1)
        count = counts[pl.ds(0, owners, stride=8), :]
        count = jnp.concatenate([count, count], axis=1)
        homes = jnp.concatenate([home[pl.ds(i, owners, stride=2), :] for i in range(2)], axis=1)
        locals_ = jnp.concatenate([local[pl.ds(i, owners, stride=2), :] for i in range(2)], axis=1)
        mine, slot, giver, turned = own_entries(homes, locals_, count, z, x, core)
        lane = lax.broadcasted_iota(jnp.int32, mine.shape, 1)
        word, shift_e, shift_n, left = make_lists(
            mine, slot, locals_, giver, turned, east[...], north[...], blocks
        )
        words[...] = jnp.broadcast_to(word, words.shape)
        copy = pltpu.make_async_copy(words, words_s, local_sem.at[0])
        copy.start()
        shift = jnp.concatenate([shift_e, shift_n, jnp.zeros((6, POSITIONS), jnp.float32)]).T
        for at in range(0, POSITIONS, LANES):
            taps[at : at + LANES, :] = tap_rows(shift[at : at + LANES, 0:1], shift[at : at + LANES, 1:2])
        receiver = slot * blocks + locals_
        rank = row_rank(left)
        table[...] = pack_rows(left, rank, [receiver | (turned << 8) | (giver << 11) | (lane << 16)])[0]
        amount = jnp.max(rank, axis=1, keepdims=True) + 1
        found[...] = jnp.broadcast_to(amount, found.shape)
        extra[...] = jnp.broadcast_to(jnp.max(amount, axis=0, keepdims=True), extra.shape)
        copy.wait()

    def work(group):
        first = STARTS[group] // GROUP

        def some(n, carry):
            sums = []
            for batch, gram in enumerate((gram_a, gram_b)):
                for g in range(BATCH):
                    word = words_s[0, n * GROUP + batch * BATCH + g]
                    gram[g] = products(
                        givers[group][(word >> 8) & 127], taking[(word & 7) * blocks + ((word >> 3) & 31)]
                    )
            rows = taps[pl.ds(pl.multiple_of(n * GROUP, GROUP), GROUP), :]
            for batch, gram in enumerate((gram_a, gram_b)):
                at = batch * BATCH
                sums.append(pair_sums(gram, [rows[at + g : at + g + 1, :] for g in range(BATCH)]))
            row_sums[n] = jnp.concatenate(sums)
            return carry

        lax.fori_loop(first, first + CAPS[group] // GROUP, some, 0)

    row_sums[...] = jnp.zeros_like(row_sums)
    arrivals(0, 0)
    arrivals(0, 1)
    lists()
    arrivals(1, 0)
    arrivals(1, 1)
    for copy in cores:
        copy.wait_recv()
    work(0)
    arrivals(2, 0)
    arrivals(2, 1)
    work(1)
    arrivals(3, 0)
    arrivals(3, 1)
    work(2)
    count = part_out.shape[0]
    taken = (words[0:1, :] & 7) * blocks + ((words[0:1, :] >> 3) & 31)
    hot = (lax.broadcasted_iota(jnp.int32, (count, taken.shape[1]), 0) == taken).astype(jnp.float32)
    part_out[...] = jnp.dot(
        hot, row_sums[...].reshape(taken.shape[1], BLOCK),
        preferred_element_type=jnp.float32, precision=lax.Precision.HIGHEST,
    )
    for copy in sent:
        copy.wait_send()


def extra_kernel(blocks, extra, part, table, found, east, north, near, middle, far, taking, *refs):
    out, table_s, found_s, east_s, north_s, gram, sems = refs
    out[...] = part[...]

    @pl.when(extra[0, 0] > 0)
    def _():
        copies = [
            pltpu.make_async_copy(a, b, sems.at[i])
            for i, (a, b) in enumerate([(table, table_s), (found, found_s), (east, east_s), (north, north_s)])
        ]
        for copy in copies:
            copy.start()
        for copy in copies:
            copy.wait()

        def row_step(row, carry):
            def entry_step(k, carry):
                word = table_s[row, k]
                receiver, turned, giver, lane = word & 255, (word >> 8) & 7, (word >> 11) & 31, word >> 16
                take = taking[receiver]
                for ref, slots in zip((near, middle, far), SLOTS):
                    for i, t in enumerate(slots):

                        @pl.when(turned == t)
                        def _():
                            gram[0] = products(ref[i * blocks + giver], take)

                out[pl.ds(receiver, 1), :] += pair_sums(gram, [tap_rows(east_s[row, lane], north_s[row, lane])])
                return carry

            return lax.fori_loop(0, found_s[row, 0], entry_step, carry)

        lax.fori_loop(0, table.shape[0], row_step, 0)


def sum_kernel(part, out, rows_in, mine, pieces, row_send, row_recv, mem_send, mem_recv):
    _, z, x, core = place()
    mem = lax.axis_index("mem")
    mems = mine.shape[0]

    def mem_peer(step):
        return {"mem": lax.rem(mem + step, mems)}

    enter([row_peer(z, x, core, s) for s in range(1, XC)] + [mem_peer(s) for s in range(1, mems)])
    copies = []
    for s in range(1, XC):
        copy = pltpu.make_async_remote_copy(
            src_ref=part.at[s], dst_ref=rows_in.at[mirrored(s)],
            send_sem=row_send.at[s], recv_sem=row_recv.at[mirrored(s)],
            device_id=row_peer(z, x, core, s), device_id_type=MESH_ID,
        )
        copy.start()
        copies.append(copy)
    summed = part[0]
    for s in range(1, XC):
        copies[s - 1].wait()
    for s in range(1, XC):
        summed = summed + rows_in[s]
    each = summed.shape[0] // mems
    for m in range(mems):
        mine[m, :each, :] = summed[m * each : (m + 1) * each, :]
        mine[m, each:, :] = jnp.zeros((mine.shape[1] - each, BLOCK), jnp.float32)
    pieces[mem] = mine[mem]
    copies = []
    for s in range(1, mems):
        copy = pltpu.make_async_remote_copy(
            src_ref=mine.at[lax.rem(mem + s, mems)], dst_ref=pieces.at[mem],
            send_sem=mem_send.at[s], recv_sem=mem_recv.at[s],
            device_id=mem_peer(s), device_id_type=MESH_ID,
        )
        copy.start()
        copies.append(copy)
    for copy in copies:
        copy.wait()
    for l in range(LEVELS):
        first = l * (mems // LEVELS)
        both = pieces[first]
        for m in range(first + 1, first + mems // LEVELS):
            both = both + pieces[m]
        both = both / (MEMBERS - 1.0)
        for i in range(each):
            out[l : l + 1, i * BLOCK : (i + 1) * BLOCK] = both[i : i + 1, :]


def shards(ensemble, control, pair_home, pair_local, pair_count, pair_shift):
    member_rows, columns = ensemble.shape
    blocks = columns // BLOCK
    owners = lax.axis_size("col")
    mems = lax.axis_size("mem")
    entries = 2 * pair_shift.shape[1]
    sign = jnp.asarray(np.array([1.0, -1.0], np.float32))
    both = (pair_shift[:, :, None] * sign).reshape(2, entries)
    small = jnp.concatenate([both.reshape(4, LANES), jnp.zeros((4, LANES), jnp.float32)])
    live = jnp.broadcast_to(pair_count[:, None], (8, LANES))
    home = pair_home.reshape(-1, LANES)
    local = pair_local.reshape(-1, LANES)
    smem = pl.BlockSpec(memory_space=pltpu.SMEM)
    vmem = pl.BlockSpec(memory_space=pltpu.VMEM)
    dma = pltpu.SemaphoreType.DMA
    shape = jax.ShapeDtypeStruct

    *givers, taking, part, table, found, extra, east, north = pl.pallas_call(
        functools.partial(gather_kernel, blocks),
        out_shape=[shape((len(slots) * blocks, member_rows, BLOCK), jnp.bfloat16) for slots in SLOTS] + [
            shape((XC * blocks, member_rows, BLOCK), jnp.bfloat16),
            shape((XC * blocks, BLOCK), jnp.float32),
            shape((owners, entries), jnp.int32),
            shape((owners, LANES), jnp.int32),
            shape((8, LANES), jnp.int32),
            shape((owners, entries), jnp.float32),
            shape((owners, entries), jnp.float32),
        ],
        in_specs=[vmem] * 6,
        out_specs=[vmem] * 10,
        scratch_shapes=[
            pltpu.VMEM((owners * 8, LANES), jnp.float32),
            pltpu.VMEM((owners * 8, LANES), jnp.int32),
            pltpu.VMEM((8, POSITIONS), jnp.int32),
            pltpu.VMEM((POSITIONS, BLOCK), jnp.float32),
            pltpu.SMEM((8, POSITIONS), jnp.int32),
            pltpu.VMEM((POSITIONS // GROUP, GROUP, BLOCK), jnp.float32),
            pltpu.VMEM((BATCH, SIDE, SIDE, BLOCK), jnp.float32),
            pltpu.VMEM((BATCH, SIDE, SIDE, BLOCK), jnp.float32),
            dma((1,)),
            dma((2, 4, 2)), dma((2, 4, 2)), dma((2, 2, 2)), dma((2, 2, 2)), dma((X, 2)), dma((X, 2)),
            dma((2, XC)), dma((2, XC)), dma((2, Z)), dma((2, Z)),
        ],
        compiler_params=pltpu.CompilerParams(
            collective_id=0, has_side_effects=True, vmem_limit_bytes=28 * 1024 * 1024
        ),
    )(ensemble, control, small, live, home, local)

    part = pl.pallas_call(
        functools.partial(extra_kernel, blocks),
        out_shape=shape(part.shape, part.dtype),
        in_specs=[smem] + [vmem] * 9,
        out_specs=vmem,
        scratch_shapes=[
            pltpu.SMEM(table.shape, jnp.int32), pltpu.SMEM(found.shape, jnp.int32),
            pltpu.SMEM(east.shape, jnp.float32), pltpu.SMEM(north.shape, jnp.float32),
            pltpu.VMEM((1, SIDE, SIDE, BLOCK), jnp.float32),
            dma((4,)),
        ],
        compiler_params=pltpu.CompilerParams(vmem_limit_bytes=24 * 1024 * 1024),
    )(extra, part, table, found, east, north, *givers, taking)
    part = part.reshape(XC, blocks, BLOCK)

    return pl.pallas_call(
        sum_kernel,
        out_shape=jax.ShapeDtypeStruct((LEVELS, columns // mems), jnp.float32),
        in_specs=[vmem],
        out_specs=vmem,
        scratch_shapes=[
            pltpu.VMEM((XC, blocks, BLOCK), jnp.float32),
            pltpu.VMEM((mems, 8, BLOCK), jnp.float32),
            pltpu.VMEM((mems, 8, BLOCK), jnp.float32),
            dma((XC,)), dma((XC,)), dma((mems,)), dma((mems,)),
        ],
        compiler_params=pltpu.CompilerParams(
            collective_id=1, has_side_effects=True, vmem_limit_bytes=8 * 1024 * 1024
        ),
    )(part)


def solution(mesh):
    return jax.shard_map(
        shards,
        mesh=mesh,
        in_specs=(P("mem", "col"), P(None, "col"), P(), P(), P("col"), P(None, "col")),
        out_specs=P(None, ("col", "mem")),
        check_vma=False,
    )
```

```python
import functools

import jax
import jax.numpy as jnp
import numpy as np
from jax import lax
from jax.experimental import pallas as pl
from jax.experimental.pallas import tpu as pltpu
from jax.sharding import PartitionSpec as P

MEMBERS = 80
LEVELS = 4
SIDE = 16
BLOCK = 256
SPACING_KM = 200.0
HALF_WIDTH = 250.0
XC = 8
Z = 8
X = 4
LANES = 128
GROUP = 8
ROW_CAP = 16
SLOTS = ((0, 7, 1, 6, 2), (5, 3), (4,))
CAPS = (160, 80, 48)
STARTS = (0, 160, 240)
POSITIONS = 384
USED = 1 << 25
MESH_ID = pl.DeviceIdType.MESH


def gaspari_cohn(squared):
    scaled = jnp.sqrt(squared * (1.0 / (HALF_WIDTH * HALF_WIDTH)))
    near_part = (
        ((-0.25 * scaled + 0.5) * scaled + 0.625) * scaled - 5.0 / 3.0
    ) * scaled * scaled + 1.0
    bounded = jnp.maximum(scaled, 1.0)
    far_part = (
        ((((scaled * (1.0 / 12.0) - 0.5) * scaled + 0.625) * scaled + 5.0 / 3.0) * scaled - 5.0) * scaled
        + 4.0
        - (2.0 / 3.0) / bounded
    )
    return jnp.where(scaled <= 1.0, near_part, jnp.where(scaled <= 2.0, far_part, 0.0))


def tap_rows(east, north):
    shape = (east.shape[0] if east.ndim else 1, BLOCK)
    lane = lax.broadcasted_iota(jnp.int32, shape, 1) + SIDE // 2
    de = east - SPACING_KM * ((lane & (SIDE - 1)) - SIDE // 2).astype(jnp.float32)
    dn = north + SPACING_KM * (SIDE // 2 - (lane >> 4)).astype(jnp.float32)
    return gaspari_cohn(de * de + dn * dn).astype(jnp.bfloat16).astype(jnp.float32)


def place():
    col = lax.axis_index("col")
    return col, col // XC, (col % XC) // 2, col % 2


def row_peer(z, x, core, slot):
    return {"col": z * XC + lax.rem(x + slot // 2, X) * 2 + lax.rem(core + slot % 2, 2)}


def column_peer(col, z, step):
    return {"col": col + (lax.rem(z + step, Z) - z) * XC}


def mirrored(slot):
    return (X - slot // 2) % X * 2 + slot % 2


def greet(peers):
    barrier = pltpu.get_barrier_semaphore()
    for peer in peers:
        pl.semaphore_signal(barrier, inc=1, device_id=peer, device_id_type=MESH_ID)
    return lambda: pl.semaphore_wait(barrier, len(peers))


def turn(a, shift):
    return pltpu.roll(a, shift % a.shape[1], 1)


def own_entries(home, local, count, z, x, core):
    lane = lax.broadcasted_iota(jnp.int32, home.shape, 1)
    even = (lane & 1) == 0
    other_home = jnp.where(even, turn(home, -1), turn(home, 1))
    other_local = jnp.where(even, turn(local, -1), turn(local, 1))
    mine = ((home >> 3) == z) & ((other_home & 7) == x * 2 + core) & ((lane >> 1) < count)
    slot = ((((home >> 1) & 3) - x) & 3) * 2 + ((home ^ core) & 1)
    turned = ((other_home >> 3) - z) & 7
    return mine, slot, other_local, turned


def by_slot(turned, values):
    found = jnp.zeros_like(turned)
    for t, value in values.items():
        found = jnp.where(turned == t, value, found)
    return found


def row_rank(mine):
    rank = mine.astype(jnp.int32)
    lane = lax.broadcasted_iota(jnp.int32, rank.shape, 1)
    step = 1
    while step < rank.shape[1]:
        rank = rank + jnp.where(lane >= step, turn(rank, step), 0)
        step *= 2
    return rank - 1


def pack_rows(mine, rank, arrays):
    lane = lax.broadcasted_iota(jnp.int32, rank.shape, 1)
    move = jnp.where(mine, lane - rank, 0)
    arrays = [jnp.where(mine, a, 0) for a in arrays]
    step = 1
    while step < rank.shape[1]:
        next_move = turn(move, -step)
        arrives, leaves = (next_move & step) != 0, (move & step) != 0
        arrays = [jnp.where(arrives, turn(a, -step), jnp.where(leaves, 0, a)) for a in arrays]
        move = jnp.where(arrives, next_move, jnp.where(leaves, 0, move))
        step *= 2
    return arrays


def group_rank(mine, group):
    rows, lanes = mine.shape
    line = lax.broadcasted_iota(jnp.int32, (rows, lanes), 0)
    lane = lax.broadcasted_iota(jnp.int32, (rows, lanes), 1)
    rank = jnp.zeros((rows, lanes), jnp.int32)
    for t in range(0, len(CAPS), 2):
        low, high = mine & (group == t), mine & (group == t + 1)
        upto = low.astype(jnp.int32) + (high.astype(jnp.int32) << 16)
        step = 1
        while step < lanes:
            upto = upto + jnp.where(lane >= step, turn(upto, step), 0)
            step *= 2
        whole = jnp.broadcast_to(upto[:, lanes - 1 :], (rows, lanes))
        above = whole
        step = 1
        while step < rows:
            above = above + jnp.where(line >= step, pltpu.roll(above, step, 0), 0)
            step *= 2
        upto = upto + above - whole
        rank = jnp.where(low, (upto & 0xFFFF) - 1, jnp.where(high, (upto >> 16) - 1, rank))
    return rank


def make_lists(mine, slot, local, giver, turned, east, north, blocks):
    in_row = row_rank(mine)
    kept = mine & (in_row < ROW_CAP)
    group = by_slot(turned, {t: g for g, slots in enumerate(SLOTS) for t in slots})
    rank = group_rank(kept, group)
    kept = kept & (rank < by_slot(group, dict(enumerate(CAPS))))
    place_at = by_slot(group, dict(enumerate(STARTS))) + rank
    giver = giver + by_slot(turned, {t: i * blocks for slots in SLOTS for i, t in enumerate(slots)})
    code = slot | (local << 3) | (giver << 8) | (place_at << 15) | USED
    rank = row_rank(kept)
    code, east, north = pack_rows(kept, rank, [code, east, north])
    rows = code.shape[0]
    place_at = jnp.where(code >= USED, (code >> 15) & 1023, -1)
    lane = lax.broadcasted_iota(jnp.int32, (rows, POSITIONS), 1)
    words = jnp.zeros((rows, POSITIONS), jnp.int32)
    easts = jnp.zeros((rows, POSITIONS), jnp.float32)
    norths = jnp.zeros((rows, POSITIONS), jnp.float32)
    for j in range(ROW_CAP):
        hit = place_at[:, j : j + 1] == lane
        words = words + jnp.where(hit, code[:, j : j + 1], 0)
        easts = easts + jnp.where(hit, east[:, j : j + 1], 0.0)
        norths = norths + jnp.where(hit, north[:, j : j + 1], 0.0)
    words, easts, norths = [jnp.sum(v, axis=0, keepdims=True) for v in (words, easts, norths)]
    return words, jnp.where(words >= USED, easts, 1e5), norths, mine & ~kept


def taper_tile(row):
    within = lax.broadcasted_iota(jnp.int32, (SIDE, BLOCK), 1) & (SIDE - 1)
    within = jnp.abs(within - lax.broadcasted_iota(jnp.int32, (SIDE, BLOCK), 0)) <= SIDE // 4
    taps = pltpu.roll(jnp.broadcast_to(row, (SIDE, BLOCK)), 0, 1, stride=1, stride_axis=0)
    taps = jnp.where(within, taps, 0.0)
    left, right = taps[:, :LANES], taps[:, LANES:]
    lane = lax.broadcasted_iota(jnp.int32, left.shape, 1)
    none = jnp.zeros(left.shape, jnp.bfloat16)
    upper, lower = [], []
    for k in range(8):
        low = lane < 16 * k
        a, b = turn(left, 16 * k), turn(right, 16 * k)
        middle = jnp.where(low, a, b).astype(jnp.bfloat16)
        if k < 4:
            upper.append(jnp.concatenate([middle, none], axis=1))
            lower.append(jnp.concatenate([jnp.where(low, 0.0, a).astype(jnp.bfloat16), middle], axis=1))
        else:
            upper.append(jnp.concatenate([middle, jnp.where(low, b, 0.0).astype(jnp.bfloat16)], axis=1))
            lower.append(jnp.concatenate([none, middle], axis=1))
    return jnp.concatenate(upper + lower)


def pair_sum(row, give, take):
    reached = jnp.dot(give, taper_tile(row), preferred_element_type=jnp.float32)
    return jnp.sum(reached * take.astype(jnp.float32), axis=0, keepdims=True)


def gather_kernel(
    blocks, ensemble, control, small, live, home, local, *refs,
):
    givers, refs = refs[:3], refs[3:]
    taking, part_out, table, found, extra, east, north = refs[:7]
    (
        seen, counts, words, taps, words_s, row_sums, local_sem,
        z_send, z_recv, x_send, x_recv, core_send, core_recv, row_send, row_recv, col_send, col_recv,
    ) = refs[7:]
    col, z, x, core = place()
    entered = greet([row_peer(z, x, core, s) for s in range(1, XC)] + [column_peer(col, z, s) for s in range(1, Z)])
    member_rows, columns = ensemble.shape
    half = blocks // 2
    level = (lax.axis_index("mem") * member_rows) // MEMBERS
    scale = jnp.zeros((1, columns), jnp.float32)
    for l in range(LEVELS):
        scale = jnp.where(level == l, control[l : l + 1, :].astype(jnp.float32), scale)
    for b in range(blocks):
        own = ensemble[:, b * BLOCK : (b + 1) * BLOCK]
        taking[b] = own
        givers[0][b] = (own.astype(jnp.float32) * scale[:, b * BLOCK : (b + 1) * BLOCK]).astype(jnp.bfloat16)
    seen[pl.ds(pl.multiple_of(col * 8, 8), 8), :] = small[...]
    counts[pl.ds(pl.multiple_of(col * 8, 8), 8), :] = live[...]

    entered()

    sent = []

    def send(source, target, send_sem, recv_sem, peer):
        copy = pltpu.make_async_remote_copy(
            src_ref=source, dst_ref=target, send_sem=send_sem, recv_sem=recv_sem,
            device_id=peer, device_id_type=MESH_ID,
        )
        copy.start()
        sent.append(copy)
        return copy

    def part(ref, slot, c):
        return ref.at[pl.ds(slot * blocks + c * half, half)]

    def giver_part(turned, c):
        for ref, slots in zip(givers, SLOTS):
            if turned in slots:
                return part(ref, slots.index(turned), c)

    def send_z(way, step, c):
        sign = 1 if way == 0 else -1
        return send(
            giver_part(-sign * step % Z, c), giver_part(-sign * (step + 1) % Z, c),
            z_send.at[way, step, c], z_recv.at[way, step, c], column_peer(col, z, sign % Z),
        )

    def send_x(way, step, c):
        sign = 1 if way == 0 else -1
        return send(
            part(taking, (-sign * step) % X * 2, c), part(taking, (-sign * (step + 1)) % X * 2, c),
            x_send.at[way, step, c], x_recv.at[way, step, c], row_peer(z, x, core, sign % X * 2),
        )

    def send_core(turned, c):
        return send(
            part(taking, turned * 2, c), part(taking, turned * 2 + 1, c),
            core_send.at[turned, c], core_recv.at[turned, c], row_peer(z, x, core, 1),
        )

    row_copies = []
    for i, ref in enumerate((seen, counts)):
        rows = ref.at[pl.ds(pl.multiple_of(col * 8, 8), 8), :]
        for s in range(1, XC):
            row_copies.append(send(rows, rows, row_send.at[i, s], row_recv.at[i, s], row_peer(z, x, core, s)))
    zs, xs, cores = {}, {}, []
    for c in range(2):
        for way in range(2):
            zs[way, 0, c] = send_z(way, 0, c)
            xs[way, 0, c] = send_x(way, 0, c)
    for c in range(2):
        cores.append(send_core(0, c))
    for copy in row_copies:
        copy.wait_recv()
    col_copies = []
    for i, ref in enumerate((seen, counts)):
        rows = ref.at[pl.ds(pl.multiple_of(z * 64, 64), 64), :]
        for s in range(1, Z):
            col_copies.append(send(rows, rows, col_send.at[i, s], col_recv.at[i, s], column_peer(col, z, s)))

    def arrivals(step, c):
        for way in range(2):
            if step < 3 or c == way:
                zs[way, step, c].wait_recv()
                if step < 2 or (step == 2 and c == way):
                    zs[way, step + 1, c] = send_z(way, step + 1, c)
        for way in range(2):
            turned = (-(1 if way == 0 else -1) * (step + 1)) % X
            if step == 0 or (step == 1 and c == way):
                xs[way, step, c].wait_recv()
                if step == 0 and c == way:
                    xs[way, 1, c] = send_x(way, 1, c)
                cores.append(send_core(turned, c))

    def lists():
        for copy in col_copies:
            copy.wait_recv()
        owners = seen.shape[0] // 8
        rows = [seen[pl.ds(i, owners, stride=8), :] for i in range(4)]
        east[...] = jnp.concatenate(rows[0:2], axis=1)
        north[...] = jnp.concatenate(rows[2:4], axis=1)
        count = counts[pl.ds(0, owners, stride=8), :]
        count = jnp.concatenate([count, count], axis=1)
        homes = jnp.concatenate([home[pl.ds(i, owners, stride=2), :] for i in range(2)], axis=1)
        locals_ = jnp.concatenate([local[pl.ds(i, owners, stride=2), :] for i in range(2)], axis=1)
        mine, slot, giver, turned = own_entries(homes, locals_, count, z, x, core)
        lane = lax.broadcasted_iota(jnp.int32, mine.shape, 1)
        word, shift_e, shift_n, left = make_lists(
            mine, slot, locals_, giver, turned, east[...], north[...], blocks
        )
        words[...] = jnp.broadcast_to(word, words.shape)
        copy = pltpu.make_async_copy(words, words_s, local_sem.at[0])
        copy.start()
        shift = jnp.concatenate([shift_e, shift_n, jnp.zeros((6, POSITIONS), jnp.float32)]).T
        for at in range(0, POSITIONS, LANES):
            taps[at : at + LANES, :] = tap_rows(shift[at : at + LANES, 0:1], shift[at : at + LANES, 1:2])
        receiver = slot * blocks + locals_
        rank = row_rank(left)
        table[...] = pack_rows(left, rank, [receiver | (turned << 8) | (giver << 11) | (lane << 16)])[0]
        amount = jnp.max(rank, axis=1, keepdims=True) + 1
        found[...] = jnp.broadcast_to(amount, found.shape)
        extra[...] = jnp.broadcast_to(jnp.max(amount, axis=0, keepdims=True), extra.shape)
        copy.wait()

    def work(group, begin=0, end=None):
        first = STARTS[group] // GROUP

        def some(n, carry):
            rows = taps[pl.ds(pl.multiple_of(n * GROUP, GROUP), GROUP), :]
            sums = []
            for g in range(GROUP):
                word = words_s[0, n * GROUP + g]
                sums.append(pair_sum(
                    rows[g : g + 1, :],
                    givers[group][(word >> 8) & 127], taking[(word & 7) * blocks + ((word >> 3) & 31)],
                ))
            row_sums[n] = jnp.concatenate(sums)
            return carry

        end = CAPS[group] if end is None else end
        lax.fori_loop(first + begin // GROUP, first + end // GROUP, some, 0)

    row_sums[...] = jnp.zeros_like(row_sums)
    lists()
    arrivals(0, 0)
    arrivals(0, 1)
    arrivals(1, 0)
    arrivals(1, 1)
    for copy in cores:
        copy.wait_recv()
    work(0, 0, 56)
    arrivals(2, 0)
    work(0, 56, 112)
    arrivals(2, 1)
    work(0, 112)
    work(1)
    arrivals(3, 0)
    arrivals(3, 1)
    work(2)
    count = part_out.shape[0]
    taken = (words[0:1, :] & 7) * blocks + ((words[0:1, :] >> 3) & 31)
    hot = (lax.broadcasted_iota(jnp.int32, (count, taken.shape[1]), 0) == taken).astype(jnp.float32)
    part_out[...] = jnp.dot(
        hot, row_sums[...].reshape(taken.shape[1], BLOCK),
        preferred_element_type=jnp.float32, precision=lax.Precision.HIGHEST,
    )
    for copy in sent:
        copy.wait_send()


def extra_kernel(blocks, extra, part, table, found, east, north, near, middle, far, taking, *refs):
    out, table_s, found_s, east_s, north_s, sems = refs
    out[...] = part[...]

    @pl.when(extra[0, 0] > 0)
    def _():
        copies = [
            pltpu.make_async_copy(a, b, sems.at[i])
            for i, (a, b) in enumerate([(table, table_s), (found, found_s), (east, east_s), (north, north_s)])
        ]
        for copy in copies:
            copy.start()
        for copy in copies:
            copy.wait()

        def row_step(row, carry):
            def entry_step(k, carry):
                word = table_s[row, k]
                receiver, turned, giver, lane = word & 255, (word >> 8) & 7, (word >> 11) & 31, word >> 16
                line = tap_rows(east_s[row, lane], north_s[row, lane])
                for ref, slots in zip((near, middle, far), SLOTS):
                    for i, t in enumerate(slots):

                        @pl.when(turned == t)
                        def _():
                            out[pl.ds(receiver, 1), :] += pair_sum(line, ref[i * blocks + giver], taking[receiver])

                return carry

            return lax.fori_loop(0, found_s[row, 0], entry_step, carry)

        lax.fori_loop(0, table.shape[0], row_step, 0)


def sum_kernel(part, out, rows_in, mine, pieces, row_send, row_recv, mem_send, mem_recv):
    _, z, x, core = place()
    mem = lax.axis_index("mem")
    mems = mine.shape[0]

    def mem_peer(step):
        return {"mem": lax.rem(mem + step, mems)}

    greet([row_peer(z, x, core, s) for s in range(1, XC)] + [mem_peer(s) for s in range(1, mems)])()
    copies = []
    for s in range(1, XC):
        copy = pltpu.make_async_remote_copy(
            src_ref=part.at[s], dst_ref=rows_in.at[mirrored(s)],
            send_sem=row_send.at[s], recv_sem=row_recv.at[mirrored(s)],
            device_id=row_peer(z, x, core, s), device_id_type=MESH_ID,
        )
        copy.start()
        copies.append(copy)
    summed = part[0]
    for s in range(1, XC):
        copies[s - 1].wait()
    for s in range(1, XC):
        summed = summed + rows_in[s]
    each = summed.shape[0] // mems
    for m in range(mems):
        mine[m, :each, :] = summed[m * each : (m + 1) * each, :]
        mine[m, each:, :] = jnp.zeros((mine.shape[1] - each, BLOCK), jnp.float32)
    pieces[mem] = mine[mem]
    copies = []
    for s in range(1, mems):
        copy = pltpu.make_async_remote_copy(
            src_ref=mine.at[lax.rem(mem + s, mems)], dst_ref=pieces.at[mem],
            send_sem=mem_send.at[s], recv_sem=mem_recv.at[s],
            device_id=mem_peer(s), device_id_type=MESH_ID,
        )
        copy.start()
        copies.append(copy)
    for copy in copies:
        copy.wait()
    for l in range(LEVELS):
        first = l * (mems // LEVELS)
        both = pieces[first]
        for m in range(first + 1, first + mems // LEVELS):
            both = both + pieces[m]
        both = both / (MEMBERS - 1.0)
        for i in range(each):
            out[l : l + 1, i * BLOCK : (i + 1) * BLOCK] = both[i : i + 1, :]


def shards(ensemble, control, pair_home, pair_local, pair_count, pair_shift):
    member_rows, columns = ensemble.shape
    blocks = columns // BLOCK
    owners = lax.axis_size("col")
    mems = lax.axis_size("mem")
    entries = 2 * pair_shift.shape[1]
    sign = jnp.asarray(np.array([1.0, -1.0], np.float32))
    both = (pair_shift[:, :, None] * sign).reshape(2, entries)
    small = jnp.concatenate([both.reshape(4, LANES), jnp.zeros((4, LANES), jnp.float32)])
    live = jnp.broadcast_to(pair_count[:, None], (8, LANES))
    home = pair_home.reshape(-1, LANES)
    local = pair_local.reshape(-1, LANES)
    smem = pl.BlockSpec(memory_space=pltpu.SMEM)
    vmem = pl.BlockSpec(memory_space=pltpu.VMEM)
    dma = pltpu.SemaphoreType.DMA
    shape = jax.ShapeDtypeStruct

    *givers, taking, part, table, found, extra, east, north = pl.pallas_call(
        functools.partial(gather_kernel, blocks),
        out_shape=[shape((len(slots) * blocks, member_rows, BLOCK), jnp.bfloat16) for slots in SLOTS] + [
            shape((XC * blocks, member_rows, BLOCK), jnp.bfloat16),
            shape((XC * blocks, BLOCK), jnp.float32),
            shape((owners, entries), jnp.int32),
            shape((owners, LANES), jnp.int32),
            shape((8, LANES), jnp.int32),
            shape((owners, entries), jnp.float32),
            shape((owners, entries), jnp.float32),
        ],
        in_specs=[vmem] * 6,
        out_specs=[vmem] * 10,
        scratch_shapes=[
            pltpu.VMEM((owners * 8, LANES), jnp.float32),
            pltpu.VMEM((owners * 8, LANES), jnp.int32),
            pltpu.VMEM((8, POSITIONS), jnp.int32),
            pltpu.VMEM((POSITIONS, BLOCK), jnp.float32),
            pltpu.SMEM((8, POSITIONS), jnp.int32),
            pltpu.VMEM((POSITIONS // GROUP, GROUP, BLOCK), jnp.float32),
            dma((1,)),
            dma((2, 4, 2)), dma((2, 4, 2)), dma((2, 2, 2)), dma((2, 2, 2)), dma((X, 2)), dma((X, 2)),
            dma((2, XC)), dma((2, XC)), dma((2, Z)), dma((2, Z)),
        ],
        compiler_params=pltpu.CompilerParams(
            collective_id=0, has_side_effects=True, vmem_limit_bytes=28 * 1024 * 1024
        ),
    )(ensemble, control, small, live, home, local)

    part = pl.pallas_call(
        functools.partial(extra_kernel, blocks),
        out_shape=shape(part.shape, part.dtype),
        in_specs=[smem] + [vmem] * 9,
        out_specs=vmem,
        scratch_shapes=[
            pltpu.SMEM(table.shape, jnp.int32), pltpu.SMEM(found.shape, jnp.int32),
            pltpu.SMEM(east.shape, jnp.float32), pltpu.SMEM(north.shape, jnp.float32),
            dma((4,)),
        ],
        compiler_params=pltpu.CompilerParams(vmem_limit_bytes=24 * 1024 * 1024),
    )(extra, part, table, found, east, north, *givers, taking)
    part = part.reshape(XC, blocks, BLOCK)

    return pl.pallas_call(
        sum_kernel,
        out_shape=jax.ShapeDtypeStruct((LEVELS, columns // mems), jnp.float32),
        in_specs=[vmem],
        out_specs=vmem,
        scratch_shapes=[
            pltpu.VMEM((XC, blocks, BLOCK), jnp.float32),
            pltpu.VMEM((mems, 8, BLOCK), jnp.float32),
            pltpu.VMEM((mems, 8, BLOCK), jnp.float32),
            dma((XC,)), dma((XC,)), dma((mems,)), dma((mems,)),
        ],
        compiler_params=pltpu.CompilerParams(
            collective_id=1, has_side_effects=True, vmem_limit_bytes=8 * 1024 * 1024
        ),
    )(part)


def solution(mesh):
    return jax.shard_map(
        shards,
        mesh=mesh,
        in_specs=(P("mem", "col"), P(None, "col"), P(), P(), P("col"), P(None, "col")),
        out_specs=P(None, ("col", "mem")),
        check_vma=False,
    )
```

```python
import functools

import jax
import jax.numpy as jnp
import numpy as np
from jax import lax
from jax.experimental import pallas as pl
from jax.experimental.pallas import tpu as pltpu
from jax.sharding import PartitionSpec as P

MEMBERS = 80
LEVELS = 4
SIDE = 16
BLOCK = 256
SPACING_KM = 200.0
HALF_WIDTH = 250.0
XC = 8
Z = 8
X = 4
LANES = 128
GROUP = 16
ROW_CAP = 16
SLOTS = ((0, 7, 1), (6, 2), (5, 3), (4,))
CAPS = (112, 80, 80, 48)
STARTS = (0, 112, 192, 272)
EARLY = 256
POSITIONS = 384
USED = 1 << 25
MESH_ID = pl.DeviceIdType.MESH


def gaspari_cohn(squared):
    scaled = jnp.sqrt(squared * (1.0 / (HALF_WIDTH * HALF_WIDTH)))
    near_part = (
        ((-0.25 * scaled + 0.5) * scaled + 0.625) * scaled - 5.0 / 3.0
    ) * scaled * scaled + 1.0
    bounded = jnp.maximum(scaled, 1.0)
    far_part = (
        ((((scaled * (1.0 / 12.0) - 0.5) * scaled + 0.625) * scaled + 5.0 / 3.0) * scaled - 5.0) * scaled
        + 4.0
        - (2.0 / 3.0) / bounded
    )
    return jnp.where(scaled <= 1.0, near_part, jnp.where(scaled <= 2.0, far_part, 0.0))


def tap_rows(east, north):
    shape = (east.shape[0] if east.ndim else 1, BLOCK)
    lane = lax.broadcasted_iota(jnp.int32, shape, 1) + SIDE // 2
    de = east - SPACING_KM * ((lane & (SIDE - 1)) - SIDE // 2).astype(jnp.float32)
    dn = north + SPACING_KM * (SIDE // 2 - (lane >> 4)).astype(jnp.float32)
    return gaspari_cohn(de * de + dn * dn).astype(jnp.bfloat16).astype(jnp.float32)


def place():
    col = lax.axis_index("col")
    return col, col // XC, (col % XC) // 2, col % 2


def row_peer(z, x, core, slot):
    return {"col": z * XC + lax.rem(x + slot // 2, X) * 2 + lax.rem(core + slot % 2, 2)}


def column_peer(col, z, step):
    return {"col": col + (lax.rem(z + step, Z) - z) * XC}


def mirrored(slot):
    return (X - slot // 2) % X * 2 + slot % 2


def greet(peers):
    barrier = pltpu.get_barrier_semaphore()
    for peer in peers:
        pl.semaphore_signal(barrier, inc=1, device_id=peer, device_id_type=MESH_ID)
    return lambda: pl.semaphore_wait(barrier, len(peers))


def turn(a, shift):
    return pltpu.roll(a, shift % a.shape[1], 1)


def own_entries(home, local, count, z, x, core):
    lane = lax.broadcasted_iota(jnp.int32, home.shape, 1)
    even = (lane & 1) == 0
    other_home = jnp.where(even, turn(home, -1), turn(home, 1))
    other_local = jnp.where(even, turn(local, -1), turn(local, 1))
    mine = ((home >> 3) == z) & ((other_home & 7) == x * 2 + core) & ((lane >> 1) < count)
    slot = ((((home >> 1) & 3) - x) & 3) * 2 + ((home ^ core) & 1)
    turned = ((other_home >> 3) - z) & 7
    return mine, slot, other_local, turned


def by_slot(turned, values):
    found = jnp.zeros_like(turned)
    for t, value in values.items():
        found = jnp.where(turned == t, value, found)
    return found


def row_rank(mine):
    rank = mine.astype(jnp.int32)
    lane = lax.broadcasted_iota(jnp.int32, rank.shape, 1)
    step = 1
    while step < rank.shape[1]:
        rank = rank + jnp.where(lane >= step, turn(rank, step), 0)
        step *= 2
    return rank - 1


def pack_rows(mine, rank, arrays):
    lane = lax.broadcasted_iota(jnp.int32, rank.shape, 1)
    move = jnp.where(mine, lane - rank, 0)
    arrays = [jnp.where(mine, a, 0) for a in arrays]
    step = 1
    while step < rank.shape[1]:
        next_move = turn(move, -step)
        arrives, leaves = (next_move & step) != 0, (move & step) != 0
        arrays = [jnp.where(arrives, turn(a, -step), jnp.where(leaves, 0, a)) for a in arrays]
        move = jnp.where(arrives, next_move, jnp.where(leaves, 0, move))
        step *= 2
    return arrays


def group_rank(mine, group):
    rows, lanes = mine.shape
    line = lax.broadcasted_iota(jnp.int32, (rows, lanes), 0)
    lane = lax.broadcasted_iota(jnp.int32, (rows, lanes), 1)
    rank = jnp.zeros((rows, lanes), jnp.int32)
    for t in range(0, len(CAPS), 2):
        low, high = mine & (group == t), mine & (group == t + 1)
        upto = low.astype(jnp.int32) + (high.astype(jnp.int32) << 16)
        step = 1
        while step < lanes:
            upto = upto + jnp.where(lane >= step, turn(upto, step), 0)
            step *= 2
        whole = jnp.broadcast_to(upto[:, lanes - 1 :], (rows, lanes))
        above = whole
        step = 1
        while step < rows:
            above = above + jnp.where(line >= step, pltpu.roll(above, step, 0), 0)
            step *= 2
        upto = upto + above - whole
        rank = jnp.where(low, (upto & 0xFFFF) - 1, jnp.where(high, (upto >> 16) - 1, rank))
    return rank


def make_lists(mine, slot, local, giver, turned, east, north, blocks):
    in_row = row_rank(mine)
    kept = mine & (in_row < ROW_CAP)
    group = by_slot(turned, {t: g for g, slots in enumerate(SLOTS) for t in slots})
    rank = group_rank(kept, group)
    kept = kept & (rank < by_slot(group, dict(enumerate(CAPS))))
    place_at = by_slot(group, dict(enumerate(STARTS))) + rank
    giver = giver + by_slot(turned, {t: i * blocks for slots in SLOTS for i, t in enumerate(slots)})
    code = slot | (local << 3) | (giver << 8) | (place_at << 15) | USED
    rank = row_rank(kept)
    code, east, north = pack_rows(kept, rank, [code, east, north])
    rows = code.shape[0]
    place_at = jnp.where(code >= USED, (code >> 15) & 1023, -1)
    lane = lax.broadcasted_iota(jnp.int32, (rows, POSITIONS), 1)
    words = jnp.zeros((rows, POSITIONS), jnp.int32)
    easts = jnp.zeros((rows, POSITIONS), jnp.float32)
    norths = jnp.zeros((rows, POSITIONS), jnp.float32)
    for j in range(ROW_CAP):
        hit = place_at[:, j : j + 1] == lane
        words = words + jnp.where(hit, code[:, j : j + 1], 0)
        easts = easts + jnp.where(hit, east[:, j : j + 1], 0.0)
        norths = norths + jnp.where(hit, north[:, j : j + 1], 0.0)
    words, easts, norths = [jnp.sum(v, axis=0, keepdims=True) for v in (words, easts, norths)]
    return words, jnp.where(words >= USED, easts, 1e5), norths, mine & ~kept


def taper_tile(row):
    within = lax.broadcasted_iota(jnp.int32, (SIDE, BLOCK), 1) & (SIDE - 1)
    within = jnp.abs(within - lax.broadcasted_iota(jnp.int32, (SIDE, BLOCK), 0)) <= SIDE // 4
    taps = pltpu.roll(jnp.broadcast_to(row, (SIDE, BLOCK)), 0, 1, stride=1, stride_axis=0)
    taps = jnp.where(within, taps, 0.0)
    left, right = taps[:, :LANES], taps[:, LANES:]
    lane = lax.broadcasted_iota(jnp.int32, left.shape, 1)
    none = jnp.zeros(left.shape, jnp.bfloat16)
    upper, lower = [], []
    for k in range(8):
        low = lane < 16 * k
        a, b = turn(left, 16 * k), turn(right, 16 * k)
        middle = jnp.where(low, a, b).astype(jnp.bfloat16)
        if k < 4:
            upper.append(jnp.concatenate([middle, none], axis=1))
            lower.append(jnp.concatenate([jnp.where(low, 0.0, a).astype(jnp.bfloat16), middle], axis=1))
        else:
            upper.append(jnp.concatenate([middle, jnp.where(low, b, 0.0).astype(jnp.bfloat16)], axis=1))
            lower.append(jnp.concatenate([none, middle], axis=1))
    return jnp.concatenate(upper + lower)


def pair_sum(row, give, take):
    reached = jnp.dot(give, taper_tile(row), preferred_element_type=jnp.float32)
    return jnp.sum(reached * take.astype(jnp.float32), axis=0, keepdims=True)


def gather_kernel(
    blocks, ensemble, control, small, live, home, local, *refs,
):
    givers, refs = refs[: len(SLOTS)], refs[len(SLOTS) :]
    taking, part_out, table, found, extra, east, north = refs[:7]
    (
        seen, counts, words, taps, words_s, row_sums, local_sem,
        z_send, z_recv, x_send, x_recv, core_send, core_recv, row_send, row_recv, col_send, col_recv,
    ) = refs[7:]
    col, z, x, core = place()
    entered = greet([row_peer(z, x, core, s) for s in range(1, XC)] + [column_peer(col, z, s) for s in range(1, Z)])
    member_rows, columns = ensemble.shape
    half = blocks // 2
    level = (lax.axis_index("mem") * member_rows) // MEMBERS
    scale = jnp.zeros((1, columns), jnp.float32)
    for l in range(LEVELS):
        scale = jnp.where(level == l, control[l : l + 1, :].astype(jnp.float32), scale)
    for b in range(blocks):
        own = ensemble[:, b * BLOCK : (b + 1) * BLOCK]
        taking[b] = own
        givers[0][b] = (own.astype(jnp.float32) * scale[:, b * BLOCK : (b + 1) * BLOCK]).astype(jnp.bfloat16)
    seen[pl.ds(pl.multiple_of(col * 8, 8), 8), :] = small[...]
    counts[pl.ds(pl.multiple_of(col * 8, 8), 8), :] = live[...]

    entered()

    sent = []

    def send(source, target, send_sem, recv_sem, peer):
        copy = pltpu.make_async_remote_copy(
            src_ref=source, dst_ref=target, send_sem=send_sem, recv_sem=recv_sem,
            device_id=peer, device_id_type=MESH_ID,
        )
        copy.start()
        sent.append(copy)
        return copy

    def part(ref, slot, c):
        return ref.at[pl.ds(slot * blocks + c * half, half)]

    def giver_part(turned, c):
        for ref, slots in zip(givers, SLOTS):
            if turned in slots:
                return part(ref, slots.index(turned), c)

    def send_z(way, step, c):
        sign = 1 if way == 0 else -1
        return send(
            giver_part(-sign * step % Z, c), giver_part(-sign * (step + 1) % Z, c),
            z_send.at[way, step, c], z_recv.at[way, step, c], column_peer(col, z, sign % Z),
        )

    def send_x(way, step, c):
        sign = 1 if way == 0 else -1
        return send(
            part(taking, (-sign * step) % X * 2, c), part(taking, (-sign * (step + 1)) % X * 2, c),
            x_send.at[way, step, c], x_recv.at[way, step, c], row_peer(z, x, core, sign % X * 2),
        )

    def send_core(turned, c):
        return send(
            part(taking, turned * 2, c), part(taking, turned * 2 + 1, c),
            core_send.at[turned, c], core_recv.at[turned, c], row_peer(z, x, core, 1),
        )

    row_copies = []
    for i, ref in enumerate((seen, counts)):
        rows = ref.at[pl.ds(pl.multiple_of(col * 8, 8), 8), :]
        for s in range(1, XC):
            row_copies.append(send(rows, rows, row_send.at[i, s], row_recv.at[i, s], row_peer(z, x, core, s)))
    zs, xs, cores = {}, {}, []
    for c in range(2):
        for way in range(2):
            zs[way, 0, c] = send_z(way, 0, c)
            xs[way, 0, c] = send_x(way, 0, c)
    for c in range(2):
        cores.append(send_core(0, c))
    for copy in row_copies:
        copy.wait_recv()
    col_copies = []
    for i, ref in enumerate((seen, counts)):
        rows = ref.at[pl.ds(pl.multiple_of(z * 64, 64), 64), :]
        for s in range(1, Z):
            col_copies.append(send(rows, rows, col_send.at[i, s], col_recv.at[i, s], column_peer(col, z, s)))

    def row_arrivals(step, c):
        for way in range(2):
            turned = (-(1 if way == 0 else -1) * (step + 1)) % X
            if step == 0 or (step == 1 and c == way):
                xs[way, step, c].wait_recv()
                if step == 0 and c == way:
                    xs[way, 1, c] = send_x(way, 1, c)
                cores.append(send_core(turned, c))

    def arrivals(step, c, rows=True):
        if rows:
            row_arrivals(step, c)
        for way in range(2):
            if step < 3 or c == way:
                zs[way, step, c].wait_recv()
                if step < 2 or (step == 2 and c == way):
                    zs[way, step + 1, c] = send_z(way, step + 1, c)
    def lists():
        for copy in col_copies:
            copy.wait_recv()
        owners = seen.shape[0] // 8
        rows = [seen[pl.ds(i, owners, stride=8), :] for i in range(4)]
        east[...] = jnp.concatenate(rows[0:2], axis=1)
        north[...] = jnp.concatenate(rows[2:4], axis=1)
        count = counts[pl.ds(0, owners, stride=8), :]
        count = jnp.concatenate([count, count], axis=1)
        homes = jnp.concatenate([home[pl.ds(i, owners, stride=2), :] for i in range(2)], axis=1)
        locals_ = jnp.concatenate([local[pl.ds(i, owners, stride=2), :] for i in range(2)], axis=1)
        mine, slot, giver, turned = own_entries(homes, locals_, count, z, x, core)
        lane = lax.broadcasted_iota(jnp.int32, mine.shape, 1)
        word, shift_e, shift_n, left = make_lists(
            mine, slot, locals_, giver, turned, east[...], north[...], blocks
        )
        words[...] = jnp.broadcast_to(word, words.shape)
        copy = pltpu.make_async_copy(words, words_s, local_sem.at[0])
        copy.start()
        shift = jnp.concatenate([shift_e, shift_n, jnp.zeros((6, POSITIONS), jnp.float32)]).T
        for at in range(0, POSITIONS, LANES):
            taps[at : at + LANES, :] = tap_rows(shift[at : at + LANES, 0:1], shift[at : at + LANES, 1:2])
        receiver = slot * blocks + locals_
        rank = row_rank(left)
        table[...] = pack_rows(left, rank, [receiver | (turned << 8) | (giver << 11) | (lane << 16)])[0]
        amount = jnp.max(rank, axis=1, keepdims=True) + 1
        found[...] = jnp.broadcast_to(amount, found.shape)
        extra[...] = jnp.broadcast_to(jnp.max(amount, axis=0, keepdims=True), extra.shape)
        copy.wait()

    def work(group, begin=0, end=None):
        first = STARTS[group] // GROUP

        def some(n, carry):
            rows = taps[pl.ds(pl.multiple_of(n * GROUP, GROUP), GROUP), :]
            sums = []
            for g in range(GROUP):
                word = words_s[0, n * GROUP + g]
                sums.append(pair_sum(
                    rows[g : g + 1, :],
                    givers[group][(word >> 8) & 127], taking[(word & 7) * blocks + ((word >> 3) & 31)],
                ))
            row_sums[n] = jnp.concatenate(sums)
            return carry

        end = CAPS[group] if end is None else end
        lax.fori_loop(first + begin // GROUP, first + end // GROUP, some, 0)

    row_sums[...] = jnp.zeros_like(row_sums)
    lists()
    arrivals(0, 0)
    arrivals(0, 1)
    arrivals(1, 0)
    row_arrivals(1, 1)
    for copy in cores:
        copy.wait_recv()
    work(0, 0, 48)
    arrivals(1, 1, False)
    work(0, 48)
    arrivals(2, 0)
    work(1)
    arrivals(2, 1)
    work(2)

    taken = (words[0:1, :] & 7) * blocks + ((words[0:1, :] >> 3) & 31)
    count = part_out.shape[0]

    def spread(begin, end):
        hot = lax.broadcasted_iota(jnp.int32, (count, end - begin), 0) == taken[:, begin:end]
        sums = row_sums[begin // GROUP : end // GROUP].reshape(end - begin, BLOCK)
        return jnp.dot(
            hot.astype(jnp.float32), sums, preferred_element_type=jnp.float32, precision=lax.Precision.HIGHEST
        )

    part_out[...] = spread(0, EARLY)
    arrivals(3, 0)
    arrivals(3, 1)
    work(3)
    part_out[...] += spread(EARLY, POSITIONS)
    for copy in sent:
        copy.wait_send()


def extra_kernel(blocks, extra, part, table, found, east, north, *refs):
    givers, taking, refs = refs[: len(SLOTS)], refs[len(SLOTS)], refs[len(SLOTS) + 1 :]
    out, table_s, found_s, east_s, north_s, sems = refs
    out[...] = part[...]

    @pl.when(extra[0, 0] > 0)
    def _():
        copies = [
            pltpu.make_async_copy(a, b, sems.at[i])
            for i, (a, b) in enumerate([(table, table_s), (found, found_s), (east, east_s), (north, north_s)])
        ]
        for copy in copies:
            copy.start()
        for copy in copies:
            copy.wait()

        def row_step(row, carry):
            def entry_step(k, carry):
                word = table_s[row, k]
                receiver, turned, giver, lane = word & 255, (word >> 8) & 7, (word >> 11) & 31, word >> 16
                line = tap_rows(east_s[row, lane], north_s[row, lane])
                for ref, slots in zip(givers, SLOTS):
                    for i, t in enumerate(slots):

                        @pl.when(turned == t)
                        def _():
                            out[pl.ds(receiver, 1), :] += pair_sum(line, ref[i * blocks + giver], taking[receiver])

                return carry

            return lax.fori_loop(0, found_s[row, 0], entry_step, carry)

        lax.fori_loop(0, table.shape[0], row_step, 0)


def sum_kernel(part, out, rows_in, mine, pieces, row_send, row_recv, mem_send, mem_recv):
    _, z, x, core = place()
    mem = lax.axis_index("mem")
    mems = mine.shape[0]

    def mem_peer(step):
        return {"mem": lax.rem(mem + step, mems)}

    greet([row_peer(z, x, core, s) for s in range(1, XC)] + [mem_peer(s) for s in range(1, mems)])()
    copies = []
    for s in range(1, XC):
        copy = pltpu.make_async_remote_copy(
            src_ref=part.at[s], dst_ref=rows_in.at[mirrored(s)],
            send_sem=row_send.at[s], recv_sem=row_recv.at[mirrored(s)],
            device_id=row_peer(z, x, core, s), device_id_type=MESH_ID,
        )
        copy.start()
        copies.append(copy)
    summed = part[0]
    for s in range(1, XC):
        copies[s - 1].wait()
    for s in range(1, XC):
        summed = summed + rows_in[s]
    each = summed.shape[0] // mems
    for m in range(mems):
        mine[m, :each, :] = summed[m * each : (m + 1) * each, :]
        mine[m, each:, :] = jnp.zeros((mine.shape[1] - each, BLOCK), jnp.float32)
    pieces[mem] = mine[mem]
    copies = []
    for s in range(1, mems):
        copy = pltpu.make_async_remote_copy(
            src_ref=mine.at[lax.rem(mem + s, mems)], dst_ref=pieces.at[mem],
            send_sem=mem_send.at[s], recv_sem=mem_recv.at[s],
            device_id=mem_peer(s), device_id_type=MESH_ID,
        )
        copy.start()
        copies.append(copy)
    for copy in copies:
        copy.wait()
    for l in range(LEVELS):
        first = l * (mems // LEVELS)
        both = pieces[first]
        for m in range(first + 1, first + mems // LEVELS):
            both = both + pieces[m]
        both = both / (MEMBERS - 1.0)
        for i in range(each):
            out[l : l + 1, i * BLOCK : (i + 1) * BLOCK] = both[i : i + 1, :]


def shards(ensemble, control, pair_home, pair_local, pair_count, pair_shift):
    member_rows, columns = ensemble.shape
    blocks = columns // BLOCK
    owners = lax.axis_size("col")
    mems = lax.axis_size("mem")
    entries = 2 * pair_shift.shape[1]
    sign = jnp.asarray(np.array([1.0, -1.0], np.float32))
    both = (pair_shift[:, :, None] * sign).reshape(2, entries)
    small = jnp.concatenate([both.reshape(4, LANES), jnp.zeros((4, LANES), jnp.float32)])
    live = jnp.broadcast_to(pair_count[:, None], (8, LANES))
    home = pair_home.reshape(-1, LANES)
    local = pair_local.reshape(-1, LANES)
    smem = pl.BlockSpec(memory_space=pltpu.SMEM)
    vmem = pl.BlockSpec(memory_space=pltpu.VMEM)
    dma = pltpu.SemaphoreType.DMA
    shape = jax.ShapeDtypeStruct

    *givers, taking, part, table, found, extra, east, north = pl.pallas_call(
        functools.partial(gather_kernel, blocks),
        out_shape=[shape((len(slots) * blocks, member_rows, BLOCK), jnp.bfloat16) for slots in SLOTS] + [
            shape((XC * blocks, member_rows, BLOCK), jnp.bfloat16),
            shape((XC * blocks, BLOCK), jnp.float32),
            shape((owners, entries), jnp.int32),
            shape((owners, LANES), jnp.int32),
            shape((8, LANES), jnp.int32),
            shape((owners, entries), jnp.float32),
            shape((owners, entries), jnp.float32),
        ],
        in_specs=[vmem] * 6,
        out_specs=[vmem] * (len(SLOTS) + 7),
        scratch_shapes=[
            pltpu.VMEM((owners * 8, LANES), jnp.float32),
            pltpu.VMEM((owners * 8, LANES), jnp.int32),
            pltpu.VMEM((8, POSITIONS), jnp.int32),
            pltpu.VMEM((POSITIONS, BLOCK), jnp.float32),
            pltpu.SMEM((8, POSITIONS), jnp.int32),
            pltpu.VMEM((POSITIONS // GROUP, GROUP, BLOCK), jnp.float32),
            dma((1,)),
            dma((2, 4, 2)), dma((2, 4, 2)), dma((2, 2, 2)), dma((2, 2, 2)), dma((X, 2)), dma((X, 2)),
            dma((2, XC)), dma((2, XC)), dma((2, Z)), dma((2, Z)),
        ],
        compiler_params=pltpu.CompilerParams(
            collective_id=0, has_side_effects=True, vmem_limit_bytes=28 * 1024 * 1024
        ),
    )(ensemble, control, small, live, home, local)

    part = pl.pallas_call(
        functools.partial(extra_kernel, blocks),
        out_shape=shape(part.shape, part.dtype),
        in_specs=[smem] + [vmem] * (len(SLOTS) + 6),
        out_specs=vmem,
        scratch_shapes=[
            pltpu.SMEM(table.shape, jnp.int32), pltpu.SMEM(found.shape, jnp.int32),
            pltpu.SMEM(east.shape, jnp.float32), pltpu.SMEM(north.shape, jnp.float32),
            dma((4,)),
        ],
        compiler_params=pltpu.CompilerParams(vmem_limit_bytes=24 * 1024 * 1024),
    )(extra, part, table, found, east, north, *givers, taking)
    part = part.reshape(XC, blocks, BLOCK)

    return pl.pallas_call(
        sum_kernel,
        out_shape=jax.ShapeDtypeStruct((LEVELS, columns // mems), jnp.float32),
        in_specs=[vmem],
        out_specs=vmem,
        scratch_shapes=[
            pltpu.VMEM((XC, blocks, BLOCK), jnp.float32),
            pltpu.VMEM((mems, 8, BLOCK), jnp.float32),
            pltpu.VMEM((mems, 8, BLOCK), jnp.float32),
            dma((XC,)), dma((XC,)), dma((mems,)), dma((mems,)),
        ],
        compiler_params=pltpu.CompilerParams(
            collective_id=1, has_side_effects=True, vmem_limit_bytes=8 * 1024 * 1024
        ),
    )(part)


def solution(mesh):
    return jax.shard_map(
        shards,
        mesh=mesh,
        in_specs=(P("mem", "col"), P(None, "col"), P(), P(), P("col"), P(None, "col")),
        out_specs=P(None, ("col", "mem")),
        check_vma=False,
    )
```

```python
import functools

import jax
import jax.numpy as jnp
import numpy as np
from jax import lax
from jax.experimental import pallas as pl
from jax.experimental.pallas import tpu as pltpu
from jax.sharding import PartitionSpec as P

MEMBERS = 80
LEVELS = 4
SIDE = 16
BLOCK = 256
SPACING_KM = 200.0
HALF_WIDTH = 250.0
XC = 8
Z = 8
X = 4
LANES = 128
GROUP = 16
ROW_CAP = 16
SLOTS = ((0, 7, 1), (6, 2), (5, 3), (4,))
CAPS = (112, 80, 80, 48)
STARTS = (0, 112, 192, 272)
EARLY = 256
POSITIONS = 384
USED = 1 << 25
MESH_ID = pl.DeviceIdType.MESH


def gaspari_cohn(squared):
    scaled = jnp.sqrt(squared * (1.0 / (HALF_WIDTH * HALF_WIDTH)))
    near_part = (
        ((-0.25 * scaled + 0.5) * scaled + 0.625) * scaled - 5.0 / 3.0
    ) * scaled * scaled + 1.0
    bounded = jnp.maximum(scaled, 1.0)
    far_part = (
        ((((scaled * (1.0 / 12.0) - 0.5) * scaled + 0.625) * scaled + 5.0 / 3.0) * scaled - 5.0) * scaled
        + 4.0
        - (2.0 / 3.0) / bounded
    )
    return jnp.where(scaled <= 1.0, near_part, jnp.where(scaled <= 2.0, far_part, 0.0))


def tap_rows(east, north):
    shape = (east.shape[0] if east.ndim else 1, BLOCK)
    lane = lax.broadcasted_iota(jnp.int32, shape, 1) + SIDE // 2
    de = east - SPACING_KM * ((lane & (SIDE - 1)) - SIDE // 2).astype(jnp.float32)
    dn = north + SPACING_KM * (SIDE // 2 - (lane >> 4)).astype(jnp.float32)
    return gaspari_cohn(de * de + dn * dn).astype(jnp.bfloat16).astype(jnp.float32)


def place():
    col = lax.axis_index("col")
    return col, col // XC, (col % XC) // 2, col % 2


def row_peer(z, x, core, slot):
    return {"col": z * XC + lax.rem(x + slot // 2, X) * 2 + lax.rem(core + slot % 2, 2)}


def column_peer(col, z, step):
    return {"col": col + (lax.rem(z + step, Z) - z) * XC}


def mirrored(slot):
    return (X - slot // 2) % X * 2 + slot % 2


def greet(peers):
    barrier = pltpu.get_barrier_semaphore()
    for peer in peers:
        pl.semaphore_signal(barrier, inc=1, device_id=peer, device_id_type=MESH_ID)
    return lambda: pl.semaphore_wait(barrier, len(peers))


def turn(a, shift):
    return pltpu.roll(a, shift % a.shape[1], 1)


def own_entries(home, local, count, z, x, core):
    lane = lax.broadcasted_iota(jnp.int32, home.shape, 1)
    even = (lane & 1) == 0
    other_home = jnp.where(even, turn(home, -1), turn(home, 1))
    other_local = jnp.where(even, turn(local, -1), turn(local, 1))
    mine = ((home >> 3) == z) & ((other_home & 7) == x * 2 + core) & ((lane >> 1) < count)
    slot = ((((home >> 1) & 3) - x) & 3) * 2 + ((home ^ core) & 1)
    turned = ((other_home >> 3) - z) & 7
    return mine, slot, other_local, turned


def by_slot(turned, values):
    found = jnp.zeros_like(turned)
    for t, value in values.items():
        found = jnp.where(turned == t, value, found)
    return found


def row_rank(mine):
    rank = mine.astype(jnp.int32)
    lane = lax.broadcasted_iota(jnp.int32, rank.shape, 1)
    step = 1
    while step < rank.shape[1]:
        rank = rank + jnp.where(lane >= step, turn(rank, step), 0)
        step *= 2
    return rank - 1


def pack_rows(mine, rank, arrays):
    lane = lax.broadcasted_iota(jnp.int32, rank.shape, 1)
    move = jnp.where(mine, lane - rank, 0)
    arrays = [jnp.where(mine, a, 0) for a in arrays]
    step = 1
    while step < rank.shape[1]:
        next_move = turn(move, -step)
        arrives, leaves = (next_move & step) != 0, (move & step) != 0
        arrays = [jnp.where(arrives, turn(a, -step), jnp.where(leaves, 0, a)) for a in arrays]
        move = jnp.where(arrives, next_move, jnp.where(leaves, 0, move))
        step *= 2
    return arrays


def group_rank(mine, group):
    rows, lanes = mine.shape
    line = lax.broadcasted_iota(jnp.int32, (rows, lanes), 0)
    lane = lax.broadcasted_iota(jnp.int32, (rows, lanes), 1)
    rank = jnp.zeros((rows, lanes), jnp.int32)
    for t in range(0, len(CAPS), 2):
        low, high = mine & (group == t), mine & (group == t + 1)
        upto = low.astype(jnp.int32) + (high.astype(jnp.int32) << 16)
        step = 1
        while step < lanes:
            upto = upto + jnp.where(lane >= step, turn(upto, step), 0)
            step *= 2
        whole = jnp.broadcast_to(upto[:, lanes - 1 :], (rows, lanes))
        above = whole
        step = 1
        while step < rows:
            above = above + jnp.where(line >= step, pltpu.roll(above, step, 0), 0)
            step *= 2
        upto = upto + above - whole
        rank = jnp.where(low, (upto & 0xFFFF) - 1, jnp.where(high, (upto >> 16) - 1, rank))
    return rank


def make_lists(mine, slot, local, giver, turned, east, north, blocks):
    in_row = row_rank(mine)
    kept = mine & (in_row < ROW_CAP)
    group = by_slot(turned, {t: g for g, slots in enumerate(SLOTS) for t in slots})
    rank = group_rank(kept, group)
    kept = kept & (rank < by_slot(group, dict(enumerate(CAPS))))
    place_at = by_slot(group, dict(enumerate(STARTS))) + rank
    giver = giver + by_slot(turned, {t: i * blocks for slots in SLOTS for i, t in enumerate(slots)})
    code = slot | (local << 3) | (giver << 8) | (place_at << 15) | USED
    rank = row_rank(kept)
    code, east, north = pack_rows(kept, rank, [code, east, north])
    rows = code.shape[0]
    place_at = jnp.where(code >= USED, (code >> 15) & 1023, -1)
    lane = lax.broadcasted_iota(jnp.int32, (rows, POSITIONS), 1)
    words = jnp.zeros((rows, POSITIONS), jnp.int32)
    easts = jnp.zeros((rows, POSITIONS), jnp.float32)
    norths = jnp.zeros((rows, POSITIONS), jnp.float32)
    for j in range(ROW_CAP):
        hit = place_at[:, j : j + 1] == lane
        words = words + jnp.where(hit, code[:, j : j + 1], 0)
        easts = easts + jnp.where(hit, east[:, j : j + 1], 0.0)
        norths = norths + jnp.where(hit, north[:, j : j + 1], 0.0)
    words, easts, norths = [jnp.sum(v, axis=0, keepdims=True) for v in (words, easts, norths)]
    return words, jnp.where(words >= USED, easts, 1e5), norths, mine & ~kept


def taper_tile(row):
    within = lax.broadcasted_iota(jnp.int32, (SIDE, BLOCK), 1) & (SIDE - 1)
    within = jnp.abs(within - lax.broadcasted_iota(jnp.int32, (SIDE, BLOCK), 0)) <= SIDE // 4
    taps = pltpu.roll(jnp.broadcast_to(row, (SIDE, BLOCK)), 0, 1, stride=1, stride_axis=0)
    taps = jnp.where(within, taps, 0.0)
    left, right = taps[:, :LANES], taps[:, LANES:]
    lane = lax.broadcasted_iota(jnp.int32, left.shape, 1)
    middle, first, last = [], [], []
    for k in range(8):
        low = lane < 16 * k
        a, b = turn(left, 16 * k), turn(right, 16 * k)
        middle.append(jnp.where(low, a, b).astype(jnp.bfloat16))
        if k < 4:
            first.append(jnp.where(low, 0.0, a).astype(jnp.bfloat16))
        else:
            last.append(jnp.where(low, b, 0.0).astype(jnp.bfloat16))
    return jnp.concatenate(middle + first + last)


def pair_sum(row, give, take):
    south, north = [give[:, i * LANES : (i + 1) * LANES].astype(jnp.float32) for i in range(2)]
    low = lax.broadcasted_iota(jnp.int32, south.shape, 1) < LANES // 2
    give = jnp.concatenate([
        jnp.concatenate([south, jnp.where(low, north, 0.0)], axis=1),
        jnp.concatenate([north, jnp.where(low, 0.0, south)], axis=1),
    ]).astype(jnp.bfloat16)
    reached = jnp.dot(give, taper_tile(row), preferred_element_type=jnp.float32)
    count = take.shape[0]
    sums = [
        jnp.sum(reached[i * count : (i + 1) * count] * take[:, i * LANES : (i + 1) * LANES].astype(jnp.float32),
                axis=0, keepdims=True)
        for i in range(2)
    ]
    return jnp.concatenate(sums, axis=1)


def gather_kernel(
    blocks, ensemble, control, small, live, home, local, *refs,
):
    givers, refs = refs[: len(SLOTS)], refs[len(SLOTS) :]
    taking, part_out, table, found, extra, east, north = refs[:7]
    (
        seen, counts, words, taps, words_s, row_sums, local_sem,
        z_send, z_recv, x_send, x_recv, core_send, core_recv, row_send, row_recv, col_send, col_recv,
    ) = refs[7:]
    col, z, x, core = place()
    entered = greet([row_peer(z, x, core, s) for s in range(1, XC)] + [column_peer(col, z, s) for s in range(1, Z)])
    member_rows, columns = ensemble.shape
    half = blocks // 2
    level = (lax.axis_index("mem") * member_rows) // MEMBERS
    scale = jnp.zeros((1, columns), jnp.float32)
    for l in range(LEVELS):
        scale = jnp.where(level == l, control[l : l + 1, :].astype(jnp.float32), scale)
    for b in range(blocks):
        own = ensemble[:, b * BLOCK : (b + 1) * BLOCK]
        taking[b] = own
        givers[0][b] = (own.astype(jnp.float32) * scale[:, b * BLOCK : (b + 1) * BLOCK]).astype(jnp.bfloat16)
    seen[pl.ds(pl.multiple_of(col * 8, 8), 8), :] = small[...]
    counts[pl.ds(pl.multiple_of(col * 8, 8), 8), :] = live[...]

    entered()

    sent = []

    def send(source, target, send_sem, recv_sem, peer):
        copy = pltpu.make_async_remote_copy(
            src_ref=source, dst_ref=target, send_sem=send_sem, recv_sem=recv_sem,
            device_id=peer, device_id_type=MESH_ID,
        )
        copy.start()
        sent.append(copy)
        return copy

    def part(ref, slot, c):
        return ref.at[pl.ds(slot * blocks + c * half, half)]

    def giver_part(turned, c):
        for ref, slots in zip(givers, SLOTS):
            if turned in slots:
                return part(ref, slots.index(turned), c)

    def send_z(way, step, c):
        sign = 1 if way == 0 else -1
        return send(
            giver_part(-sign * step % Z, c), giver_part(-sign * (step + 1) % Z, c),
            z_send.at[way, step, c], z_recv.at[way, step, c], column_peer(col, z, sign % Z),
        )

    def send_x(way, step, c):
        sign = 1 if way == 0 else -1
        return send(
            part(taking, (-sign * step) % X * 2, c), part(taking, (-sign * (step + 1)) % X * 2, c),
            x_send.at[way, step, c], x_recv.at[way, step, c], row_peer(z, x, core, sign % X * 2),
        )

    def send_core(turned, c):
        return send(
            part(taking, turned * 2, c), part(taking, turned * 2 + 1, c),
            core_send.at[turned, c], core_recv.at[turned, c], row_peer(z, x, core, 1),
        )

    row_copies = []
    for i, ref in enumerate((seen, counts)):
        rows = ref.at[pl.ds(pl.multiple_of(col * 8, 8), 8), :]
        for s in range(1, XC):
            row_copies.append(send(rows, rows, row_send.at[i, s], row_recv.at[i, s], row_peer(z, x, core, s)))
    zs, xs, cores = {}, {}, []
    for c in range(2):
        for way in range(2):
            zs[way, 0, c] = send_z(way, 0, c)
            xs[way, 0, c] = send_x(way, 0, c)
    for c in range(2):
        cores.append(send_core(0, c))
    for copy in row_copies:
        copy.wait_recv()
    col_copies = []
    for i, ref in enumerate((seen, counts)):
        rows = ref.at[pl.ds(pl.multiple_of(z * 64, 64), 64), :]
        for s in range(1, Z):
            col_copies.append(send(rows, rows, col_send.at[i, s], col_recv.at[i, s], column_peer(col, z, s)))

    def row_arrivals(step, c):
        for way in range(2):
            turned = (-(1 if way == 0 else -1) * (step + 1)) % X
            if step == 0 or (step == 1 and c == way):
                xs[way, step, c].wait_recv()
                if step == 0 and c == way:
                    xs[way, 1, c] = send_x(way, 1, c)
                cores.append(send_core(turned, c))

    def arrivals(step, c, rows=True):
        if rows:
            row_arrivals(step, c)
        for way in range(2):
            if step < 3 or c == way:
                zs[way, step, c].wait_recv()
                if step < 2 or (step == 2 and c == way):
                    zs[way, step + 1, c] = send_z(way, step + 1, c)
    def lists():
        for copy in col_copies:
            copy.wait_recv()
        owners = seen.shape[0] // 8
        rows = [seen[pl.ds(i, owners, stride=8), :] for i in range(4)]
        east[...] = jnp.concatenate(rows[0:2], axis=1)
        north[...] = jnp.concatenate(rows[2:4], axis=1)
        count = counts[pl.ds(0, owners, stride=8), :]
        count = jnp.concatenate([count, count], axis=1)
        homes = jnp.concatenate([home[pl.ds(i, owners, stride=2), :] for i in range(2)], axis=1)
        locals_ = jnp.concatenate([local[pl.ds(i, owners, stride=2), :] for i in range(2)], axis=1)
        mine, slot, giver, turned = own_entries(homes, locals_, count, z, x, core)
        lane = lax.broadcasted_iota(jnp.int32, mine.shape, 1)
        word, shift_e, shift_n, left = make_lists(
            mine, slot, locals_, giver, turned, east[...], north[...], blocks
        )
        words[...] = jnp.broadcast_to(word, words.shape)
        copy = pltpu.make_async_copy(words, words_s, local_sem.at[0])
        copy.start()
        shift = jnp.concatenate([shift_e, shift_n, jnp.zeros((6, POSITIONS), jnp.float32)]).T
        for at in range(0, POSITIONS, LANES):
            taps[at : at + LANES, :] = tap_rows(shift[at : at + LANES, 0:1], shift[at : at + LANES, 1:2])
        receiver = slot * blocks + locals_
        rank = row_rank(left)
        table[...] = pack_rows(left, rank, [receiver | (turned << 8) | (giver << 11) | (lane << 16)])[0]
        amount = jnp.max(rank, axis=1, keepdims=True) + 1
        found[...] = jnp.broadcast_to(amount, found.shape)
        extra[...] = jnp.broadcast_to(jnp.max(amount, axis=0, keepdims=True), extra.shape)
        copy.wait()

    def work(group, begin=0, end=None):
        first = STARTS[group] // GROUP

        def some(n, carry):
            rows = taps[pl.ds(pl.multiple_of(n * GROUP, GROUP), GROUP), :]
            sums = []
            for g in range(GROUP):
                word = words_s[0, n * GROUP + g]
                sums.append(pair_sum(
                    rows[g : g + 1, :],
                    givers[group][(word >> 8) & 127], taking[(word & 7) * blocks + ((word >> 3) & 31)],
                ))
            row_sums[n] = jnp.concatenate(sums)
            return carry

        end = CAPS[group] if end is None else end
        lax.fori_loop(first + begin // GROUP, first + end // GROUP, some, 0)

    row_sums[...] = jnp.zeros_like(row_sums)
    lists()
    arrivals(0, 0)
    arrivals(0, 1)
    arrivals(1, 0)
    row_arrivals(1, 1)
    for copy in cores:
        copy.wait_recv()
    work(0, 0, 48)
    arrivals(1, 1, False)
    work(0, 48)
    arrivals(2, 0)
    work(1)
    arrivals(2, 1)
    work(2)

    taken = (words[0:1, :] & 7) * blocks + ((words[0:1, :] >> 3) & 31)
    count = part_out.shape[0]

    def spread(begin, end):
        hot = lax.broadcasted_iota(jnp.int32, (count, end - begin), 0) == taken[:, begin:end]
        sums = row_sums[begin // GROUP : end // GROUP].reshape(end - begin, BLOCK)
        return jnp.dot(
            hot.astype(jnp.float32), sums, preferred_element_type=jnp.float32, precision=lax.Precision.HIGHEST
        )

    part_out[...] = spread(0, EARLY)
    arrivals(3, 0)
    arrivals(3, 1)
    work(3)
    part_out[...] += spread(EARLY, POSITIONS)
    for copy in sent:
        copy.wait_send()


def extra_kernel(blocks, extra, part, table, found, east, north, *refs):
    givers, taking, refs = refs[: len(SLOTS)], refs[len(SLOTS)], refs[len(SLOTS) + 1 :]
    out, table_s, found_s, east_s, north_s, sems = refs
    out[...] = part[...]

    @pl.when(extra[0, 0] > 0)
    def _():
        copies = [
            pltpu.make_async_copy(a, b, sems.at[i])
            for i, (a, b) in enumerate([(table, table_s), (found, found_s), (east, east_s), (north, north_s)])
        ]
        for copy in copies:
            copy.start()
        for copy in copies:
            copy.wait()

        def row_step(row, carry):
            def entry_step(k, carry):
                word = table_s[row, k]
                receiver, turned, giver, lane = word & 255, (word >> 8) & 7, (word >> 11) & 31, word >> 16
                line = tap_rows(east_s[row, lane], north_s[row, lane])
                for ref, slots in zip(givers, SLOTS):
                    for i, t in enumerate(slots):

                        @pl.when(turned == t)
                        def _():
                            out[pl.ds(receiver, 1), :] += pair_sum(line, ref[i * blocks + giver], taking[receiver])

                return carry

            return lax.fori_loop(0, found_s[row, 0], entry_step, carry)

        lax.fori_loop(0, table.shape[0], row_step, 0)


def sum_kernel(part, out, rows_in, mine, pieces, row_send, row_recv, mem_send, mem_recv):
    _, z, x, core = place()
    mem = lax.axis_index("mem")
    mems = mine.shape[0]

    def mem_peer(step):
        return {"mem": lax.rem(mem + step, mems)}

    greet([row_peer(z, x, core, s) for s in range(1, XC)] + [mem_peer(s) for s in range(1, mems)])()
    copies = []
    for s in range(1, XC):
        copy = pltpu.make_async_remote_copy(
            src_ref=part.at[s], dst_ref=rows_in.at[mirrored(s)],
            send_sem=row_send.at[s], recv_sem=row_recv.at[mirrored(s)],
            device_id=row_peer(z, x, core, s), device_id_type=MESH_ID,
        )
        copy.start()
        copies.append(copy)
    summed = part[0]
    for s in range(1, XC):
        copies[s - 1].wait()
    for s in range(1, XC):
        summed = summed + rows_in[s]
    each = summed.shape[0] // mems
    for m in range(mems):
        mine[m, :each, :] = summed[m * each : (m + 1) * each, :]
        mine[m, each:, :] = jnp.zeros((mine.shape[1] - each, BLOCK), jnp.float32)
    pieces[mem] = mine[mem]
    copies = []
    for s in range(1, mems):
        copy = pltpu.make_async_remote_copy(
            src_ref=mine.at[lax.rem(mem + s, mems)], dst_ref=pieces.at[mem],
            send_sem=mem_send.at[s], recv_sem=mem_recv.at[s],
            device_id=mem_peer(s), device_id_type=MESH_ID,
        )
        copy.start()
        copies.append(copy)
    for copy in copies:
        copy.wait()
    for l in range(LEVELS):
        first = l * (mems // LEVELS)
        both = pieces[first]
        for m in range(first + 1, first + mems // LEVELS):
            both = both + pieces[m]
        both = both / (MEMBERS - 1.0)
        for i in range(each):
            out[l : l + 1, i * BLOCK : (i + 1) * BLOCK] = both[i : i + 1, :]


def shards(ensemble, control, pair_home, pair_local, pair_count, pair_shift):
    member_rows, columns = ensemble.shape
    blocks = columns // BLOCK
    owners = lax.axis_size("col")
    mems = lax.axis_size("mem")
    entries = 2 * pair_shift.shape[1]
    sign = jnp.asarray(np.array([1.0, -1.0], np.float32))
    both = (pair_shift[:, :, None] * sign).reshape(2, entries)
    small = jnp.concatenate([both.reshape(4, LANES), jnp.zeros((4, LANES), jnp.float32)])
    live = jnp.broadcast_to(pair_count[:, None], (8, LANES))
    home = pair_home.reshape(-1, LANES)
    local = pair_local.reshape(-1, LANES)
    smem = pl.BlockSpec(memory_space=pltpu.SMEM)
    vmem = pl.BlockSpec(memory_space=pltpu.VMEM)
    dma = pltpu.SemaphoreType.DMA
    shape = jax.ShapeDtypeStruct

    *givers, taking, part, table, found, extra, east, north = pl.pallas_call(
        functools.partial(gather_kernel, blocks),
        out_shape=[shape((len(slots) * blocks, member_rows, BLOCK), jnp.bfloat16) for slots in SLOTS] + [
            shape((XC * blocks, member_rows, BLOCK), jnp.bfloat16),
            shape((XC * blocks, BLOCK), jnp.float32),
            shape((owners, entries), jnp.int32),
            shape((owners, LANES), jnp.int32),
            shape((8, LANES), jnp.int32),
            shape((owners, entries), jnp.float32),
            shape((owners, entries), jnp.float32),
        ],
        in_specs=[vmem] * 6,
        out_specs=[vmem] * (len(SLOTS) + 7),
        scratch_shapes=[
            pltpu.VMEM((owners * 8, LANES), jnp.float32),
            pltpu.VMEM((owners * 8, LANES), jnp.int32),
            pltpu.VMEM((8, POSITIONS), jnp.int32),
            pltpu.VMEM((POSITIONS, BLOCK), jnp.float32),
            pltpu.SMEM((8, POSITIONS), jnp.int32),
            pltpu.VMEM((POSITIONS // GROUP, GROUP, BLOCK), jnp.float32),
            dma((1,)),
            dma((2, 4, 2)), dma((2, 4, 2)), dma((2, 2, 2)), dma((2, 2, 2)), dma((X, 2)), dma((X, 2)),
            dma((2, XC)), dma((2, XC)), dma((2, Z)), dma((2, Z)),
        ],
        compiler_params=pltpu.CompilerParams(
            collective_id=0, has_side_effects=True, vmem_limit_bytes=28 * 1024 * 1024
        ),
    )(ensemble, control, small, live, home, local)

    part = pl.pallas_call(
        functools.partial(extra_kernel, blocks),
        out_shape=shape(part.shape, part.dtype),
        in_specs=[smem] + [vmem] * (len(SLOTS) + 6),
        out_specs=vmem,
        scratch_shapes=[
            pltpu.SMEM(table.shape, jnp.int32), pltpu.SMEM(found.shape, jnp.int32),
            pltpu.SMEM(east.shape, jnp.float32), pltpu.SMEM(north.shape, jnp.float32),
            dma((4,)),
        ],
        compiler_params=pltpu.CompilerParams(vmem_limit_bytes=24 * 1024 * 1024),
    )(extra, part, table, found, east, north, *givers, taking)
    part = part.reshape(XC, blocks, BLOCK)

    return pl.pallas_call(
        sum_kernel,
        out_shape=jax.ShapeDtypeStruct((LEVELS, columns // mems), jnp.float32),
        in_specs=[vmem],
        out_specs=vmem,
        scratch_shapes=[
            pltpu.VMEM((XC, blocks, BLOCK), jnp.float32),
            pltpu.VMEM((mems, 8, BLOCK), jnp.float32),
            pltpu.VMEM((mems, 8, BLOCK), jnp.float32),
            dma((XC,)), dma((XC,)), dma((mems,)), dma((mems,)),
        ],
        compiler_params=pltpu.CompilerParams(
            collective_id=1, has_side_effects=True, vmem_limit_bytes=8 * 1024 * 1024
        ),
    )(part)


def solution(mesh):
    return jax.shard_map(
        shards,
        mesh=mesh,
        in_specs=(P("mem", "col"), P(None, "col"), P(), P(), P("col"), P(None, "col")),
        out_specs=P(None, ("col", "mem")),
        check_vma=False,
    )
```

```python
import functools

import jax
import jax.numpy as jnp
import numpy as np
from jax import lax
from jax.experimental import pallas as pl
from jax.experimental.pallas import tpu as pltpu
from jax.sharding import PartitionSpec as P

MEMBERS = 80
LEVELS = 4
SIDE = 16
BLOCK = 256
SPACING_KM = 200.0
HALF_WIDTH = 250.0
XC = 8
Z = 8
X = 4
LANES = 128
GROUP = 8
ROW_CAP = 16
SLOTS = ((0, 7, 1), (6, 2), (5, 3), (4,))
CAPS = (112, 80, 80, 48)
STARTS = (0, 112, 192, 272)
EARLY = 256
POSITIONS = 384
USED = 1 << 25
MESH_ID = pl.DeviceIdType.MESH


def gaspari_cohn(squared):
    scaled = jnp.sqrt(squared * (1.0 / (HALF_WIDTH * HALF_WIDTH)))
    near_part = (
        ((-0.25 * scaled + 0.5) * scaled + 0.625) * scaled - 5.0 / 3.0
    ) * scaled * scaled + 1.0
    bounded = jnp.maximum(scaled, 1.0)
    far_part = (
        ((((scaled * (1.0 / 12.0) - 0.5) * scaled + 0.625) * scaled + 5.0 / 3.0) * scaled - 5.0) * scaled
        + 4.0
        - (2.0 / 3.0) / bounded
    )
    return jnp.where(scaled <= 1.0, near_part, jnp.where(scaled <= 2.0, far_part, 0.0))


def tap_rows(east, north):
    shape = (east.shape[0] if east.ndim else 1, BLOCK)
    lane = lax.broadcasted_iota(jnp.int32, shape, 1) + SIDE // 2
    de = east - SPACING_KM * ((lane & (SIDE - 1)) - SIDE // 2).astype(jnp.float32)
    dn = north + SPACING_KM * (SIDE // 2 - (lane >> 4)).astype(jnp.float32)
    return gaspari_cohn(de * de + dn * dn).astype(jnp.bfloat16).astype(jnp.float32)


def place():
    col = lax.axis_index("col")
    return col, col // XC, (col % XC) // 2, col % 2


def row_peer(z, x, core, slot):
    return {"col": z * XC + lax.rem(x + slot // 2, X) * 2 + lax.rem(core + slot % 2, 2)}


def column_peer(col, z, step):
    return {"col": col + (lax.rem(z + step, Z) - z) * XC}


def mirrored(slot):
    return (X - slot // 2) % X * 2 + slot % 2


def greet(peers):
    barrier = pltpu.get_barrier_semaphore()
    for peer in peers:
        pl.semaphore_signal(barrier, inc=1, device_id=peer, device_id_type=MESH_ID)
    return lambda: pl.semaphore_wait(barrier, len(peers))


def turn(a, shift):
    return pltpu.roll(a, shift % a.shape[1], 1)


def own_entries(home, local, count, z, x, core):
    lane = lax.broadcasted_iota(jnp.int32, home.shape, 1)
    even = (lane & 1) == 0
    other_home = jnp.where(even, turn(home, -1), turn(home, 1))
    other_local = jnp.where(even, turn(local, -1), turn(local, 1))
    mine = ((home >> 3) == z) & ((other_home & 7) == x * 2 + core) & ((lane >> 1) < count)
    slot = ((((home >> 1) & 3) - x) & 3) * 2 + ((home ^ core) & 1)
    turned = ((other_home >> 3) - z) & 7
    return mine, slot, other_local, turned


def by_slot(turned, values):
    found = jnp.zeros_like(turned)
    for t, value in values.items():
        found = jnp.where(turned == t, value, found)
    return found


def running(a, axis):
    size = a.shape[axis]
    at = lax.broadcasted_iota(jnp.int32, a.shape, axis)

    def step(b, a):
        by = lax.shift_left(jnp.int32(1), b)
        return a + jnp.where(at >= by, pltpu.roll(a, by, axis), 0)

    return lax.fori_loop(0, size.bit_length() - 1, step, a)


def row_rank(mine):
    return running(mine.astype(jnp.int32), 1) - 1


def pack_rows(mine, rank, arrays):
    lanes = rank.shape[1]
    lane = lax.broadcasted_iota(jnp.int32, rank.shape, 1)

    def step(b, held):
        by = lax.shift_left(jnp.int32(1), b)
        move, arrays = held
        next_move = pltpu.roll(move, lanes - by, 1)
        arrives, leaves = (next_move & by) != 0, (move & by) != 0
        arrays = tuple(
            jnp.where(arrives, pltpu.roll(a, lanes - by, 1), jnp.where(leaves, jnp.zeros_like(a), a)) for a in arrays
        )
        return jnp.where(arrives, next_move, jnp.where(leaves, 0, move)), arrays

    held = jnp.where(mine, lane - rank, 0), tuple(jnp.where(mine, a, jnp.zeros_like(a)) for a in arrays)
    return lax.fori_loop(0, lanes.bit_length() - 1, step, held)[1]


def group_rank(mine, group):
    rows, lanes = mine.shape
    rank = jnp.zeros((rows, lanes), jnp.int32)
    for t in range(0, len(CAPS), 2):
        low, high = mine & (group == t), mine & (group == t + 1)
        upto = running(low.astype(jnp.int32) + (high.astype(jnp.int32) << 16), 1)
        whole = jnp.broadcast_to(upto[:, lanes - 1 :], (rows, lanes))
        upto = upto + running(whole, 0) - whole
        rank = jnp.where(low, (upto & 0xFFFF) - 1, jnp.where(high, (upto >> 16) - 1, rank))
    return rank


def make_lists(mine, slot, local, giver, turned, east, north, blocks):
    in_row = row_rank(mine)
    kept = mine & (in_row < ROW_CAP)
    group = by_slot(turned, {t: g for g, slots in enumerate(SLOTS) for t in slots})
    rank = group_rank(kept, group)
    kept = kept & (rank < by_slot(group, dict(enumerate(CAPS))))
    place_at = by_slot(group, dict(enumerate(STARTS))) + rank
    giver = giver + by_slot(turned, {t: i * blocks for slots in SLOTS for i, t in enumerate(slots)})
    code = slot | (local << 3) | (giver << 8) | (place_at << 15) | USED
    rank = row_rank(kept)
    code, east, north = pack_rows(kept, rank, [code, east, north])
    rows = code.shape[0]
    place_at = jnp.where(code >= USED, (code >> 15) & 1023, -1)
    lane = lax.broadcasted_iota(jnp.int32, (rows, POSITIONS), 1)

    def step(j, held):
        (place_at, *columns), sums = held
        hit = place_at[:, 0:1] == lane
        sums = tuple(s + jnp.where(hit, c[:, 0:1], jnp.zeros_like(s)) for s, c in zip(sums, columns))
        return tuple(pltpu.roll(c, c.shape[1] - 1, 1) for c in (place_at, *columns)), sums

    sums = tuple(jnp.zeros((rows, POSITIONS), a.dtype) for a in (code, east, north))
    columns = tuple(a[:, :LANES] for a in (place_at, code, east, north))
    words, easts, norths = lax.fori_loop(0, ROW_CAP, step, (columns, sums))[1]
    words, easts, norths = [jnp.sum(v, axis=0, keepdims=True) for v in (words, easts, norths)]
    return words, jnp.where(words >= USED, easts, 1e5), norths, mine & ~kept


def taper_tile(row):
    within = lax.broadcasted_iota(jnp.int32, (SIDE, BLOCK), 1) & (SIDE - 1)
    within = jnp.abs(within - lax.broadcasted_iota(jnp.int32, (SIDE, BLOCK), 0)) <= SIDE // 4
    taps = pltpu.roll(jnp.broadcast_to(row, (SIDE, BLOCK)), 0, 1, stride=1, stride_axis=0)
    taps = jnp.where(within, taps, 0.0)
    left, right = taps[:, :LANES], taps[:, LANES:]
    lane = lax.broadcasted_iota(jnp.int32, left.shape, 1)
    middle, first, last = [], [], []
    for k in range(8):
        low = lane < 16 * k
        a, b = turn(left, 16 * k), turn(right, 16 * k)
        middle.append(jnp.where(low, a, b).astype(jnp.bfloat16))
        if k < 4:
            first.append(jnp.where(low, 0.0, a).astype(jnp.bfloat16))
        else:
            last.append(jnp.where(low, b, 0.0).astype(jnp.bfloat16))
    return jnp.concatenate(middle + first + last)


def pair_sum(row, give, take):
    south, north = [give[:, i * LANES : (i + 1) * LANES].astype(jnp.float32) for i in range(2)]
    low = lax.broadcasted_iota(jnp.int32, south.shape, 1) < LANES // 2
    give = jnp.concatenate([
        jnp.concatenate([south, jnp.where(low, north, 0.0)], axis=1),
        jnp.concatenate([north, jnp.where(low, 0.0, south)], axis=1),
    ]).astype(jnp.bfloat16)
    reached = jnp.dot(give, taper_tile(row), preferred_element_type=jnp.float32)
    count = take.shape[0]
    sums = [
        jnp.sum(reached[i * count : (i + 1) * count] * take[:, i * LANES : (i + 1) * LANES].astype(jnp.float32),
                axis=0, keepdims=True)
        for i in range(2)
    ]
    return jnp.concatenate(sums, axis=1)


def gather_kernel(
    blocks, ensemble, control, small, live, home, local, *refs,
):
    givers, refs = refs[: len(SLOTS)], refs[len(SLOTS) :]
    taking, part_out, table, found, extra, east, north = refs[:7]
    (
        seen, counts, words, shifts, taps, words_s, row_sums, local_sem,
        z_send, z_recv, x_send, x_recv, core_send, core_recv, row_send, row_recv, col_send, col_recv,
    ) = refs[7:]
    col, z, x, core = place()
    entered = greet([row_peer(z, x, core, s) for s in range(1, XC)] + [column_peer(col, z, s) for s in range(1, Z)])
    member_rows, columns = ensemble.shape
    half = blocks // 2
    level = (lax.axis_index("mem") * member_rows) // MEMBERS
    scale = jnp.zeros((1, columns), jnp.float32)
    for l in range(LEVELS):
        scale = jnp.where(level == l, control[l : l + 1, :].astype(jnp.float32), scale)
    for b in range(blocks):
        own = ensemble[:, b * BLOCK : (b + 1) * BLOCK]
        taking[b] = own
        givers[0][b] = (own.astype(jnp.float32) * scale[:, b * BLOCK : (b + 1) * BLOCK]).astype(jnp.bfloat16)
    seen[pl.ds(pl.multiple_of(col * 8, 8), 8), :] = small[...]
    counts[pl.ds(pl.multiple_of(col * 8, 8), 8), :] = live[...]

    entered()

    sent = []

    def send(source, target, send_sem, recv_sem, peer):
        copy = pltpu.make_async_remote_copy(
            src_ref=source, dst_ref=target, send_sem=send_sem, recv_sem=recv_sem,
            device_id=peer, device_id_type=MESH_ID,
        )
        copy.start()
        sent.append(copy)
        return copy

    def part(ref, slot, c):
        return ref.at[pl.ds(slot * blocks + c * half, half)]

    def giver_part(turned, c):
        for ref, slots in zip(givers, SLOTS):
            if turned in slots:
                return part(ref, slots.index(turned), c)

    def send_z(way, step, c):
        sign = 1 if way == 0 else -1
        return send(
            giver_part(-sign * step % Z, c), giver_part(-sign * (step + 1) % Z, c),
            z_send.at[way, step, c], z_recv.at[way, step, c], column_peer(col, z, sign % Z),
        )

    def send_x(way, step, c):
        sign = 1 if way == 0 else -1
        return send(
            part(taking, (-sign * step) % X * 2, c), part(taking, (-sign * (step + 1)) % X * 2, c),
            x_send.at[way, step, c], x_recv.at[way, step, c], row_peer(z, x, core, sign % X * 2),
        )

    def send_core(turned, c):
        return send(
            part(taking, turned * 2, c), part(taking, turned * 2 + 1, c),
            core_send.at[turned, c], core_recv.at[turned, c], row_peer(z, x, core, 1),
        )

    row_copies = []
    for i, ref in enumerate((seen, counts)):
        rows = ref.at[pl.ds(pl.multiple_of(col * 8, 8), 8), :]
        for s in range(1, XC):
            row_copies.append(send(rows, rows, row_send.at[i, s], row_recv.at[i, s], row_peer(z, x, core, s)))
    zs, xs, cores = {}, {}, []
    for c in range(2):
        for way in range(2):
            zs[way, 0, c] = send_z(way, 0, c)
            xs[way, 0, c] = send_x(way, 0, c)
    for c in range(2):
        cores.append(send_core(0, c))
    for copy in row_copies:
        copy.wait_recv()
    col_copies = []
    for i, ref in enumerate((seen, counts)):
        rows = ref.at[pl.ds(pl.multiple_of(z * 64, 64), 64), :]
        for s in range(1, Z):
            col_copies.append(send(rows, rows, col_send.at[i, s], col_recv.at[i, s], column_peer(col, z, s)))

    def row_arrivals(step, c):
        for way in range(2):
            turned = (-(1 if way == 0 else -1) * (step + 1)) % X
            if step == 0 or (step == 1 and c == way):
                xs[way, step, c].wait_recv()
                if step == 0 and c == way:
                    xs[way, 1, c] = send_x(way, 1, c)
                cores.append(send_core(turned, c))

    def arrivals(step, c, rows=True):
        if rows:
            row_arrivals(step, c)
        for way in range(2):
            if step < 3 or c == way:
                zs[way, step, c].wait_recv()
                if step < 2 or (step == 2 and c == way):
                    zs[way, step + 1, c] = send_z(way, step + 1, c)
    def lists():
        for copy in col_copies:
            copy.wait_recv()
        owners = seen.shape[0] // 8
        rows = [seen[pl.ds(i, owners, stride=8), :] for i in range(4)]
        east[...] = jnp.concatenate(rows[0:2], axis=1)
        north[...] = jnp.concatenate(rows[2:4], axis=1)
        count = counts[pl.ds(0, owners, stride=8), :]
        count = jnp.concatenate([count, count], axis=1)
        homes = jnp.concatenate([home[pl.ds(i, owners, stride=2), :] for i in range(2)], axis=1)
        locals_ = jnp.concatenate([local[pl.ds(i, owners, stride=2), :] for i in range(2)], axis=1)
        mine, slot, giver, turned = own_entries(homes, locals_, count, z, x, core)
        lane = lax.broadcasted_iota(jnp.int32, mine.shape, 1)
        word, shift_e, shift_n, left = make_lists(
            mine, slot, locals_, giver, turned, east[...], north[...], blocks
        )
        words[...] = jnp.broadcast_to(word, words.shape)
        copy = pltpu.make_async_copy(words, words_s, local_sem.at[0])
        copy.start()
        shifts[...] = jnp.concatenate([shift_e, shift_n, jnp.zeros((6, POSITIONS), jnp.float32)]).T

        def some_taps(n, carry):
            at = pl.ds(pl.multiple_of(n * 32, 32), 32)
            taps[at, :] = tap_rows(shifts[at, 0:1], shifts[at, 1:2])
            return carry

        lax.fori_loop(0, POSITIONS // 32, some_taps, 0)
        receiver = slot * blocks + locals_
        rank = row_rank(left)
        table[...] = pack_rows(left, rank, [receiver | (turned << 8) | (giver << 11) | (lane << 16)])[0]
        amount = jnp.max(rank, axis=1, keepdims=True) + 1
        found[...] = jnp.broadcast_to(amount, found.shape)
        extra[...] = jnp.broadcast_to(jnp.max(amount, axis=0, keepdims=True), extra.shape)
        copy.wait()

    def work(group, begin=0, end=None):
        first = STARTS[group] // GROUP

        def some(n, carry):
            rows = taps[pl.ds(pl.multiple_of(n * GROUP, GROUP), GROUP), :]
            sums = []
            for g in range(GROUP):
                word = words_s[0, n * GROUP + g]
                sums.append(pair_sum(
                    rows[g : g + 1, :],
                    givers[group][(word >> 8) & 127], taking[(word & 7) * blocks + ((word >> 3) & 31)],
                ))
            row_sums[n] = jnp.concatenate(sums)
            return carry

        end = CAPS[group] if end is None else end
        lax.fori_loop(first + begin // GROUP, first + end // GROUP, some, 0)

    row_sums[...] = jnp.zeros_like(row_sums)
    lists()
    arrivals(0, 0)
    arrivals(0, 1)
    arrivals(1, 0)
    row_arrivals(1, 1)
    for copy in cores:
        copy.wait_recv()
    work(0, 0, 48)
    arrivals(1, 1, False)
    work(0, 48)
    arrivals(2, 0)
    work(1)
    arrivals(2, 1)
    work(2)

    taken = (words[0:1, :] & 7) * blocks + ((words[0:1, :] >> 3) & 31)
    count = part_out.shape[0]

    def spread(begin, end):
        hot = lax.broadcasted_iota(jnp.int32, (count, end - begin), 0) == taken[:, begin:end]
        sums = row_sums[begin // GROUP : end // GROUP].reshape(end - begin, BLOCK)
        return jnp.dot(
            hot.astype(jnp.float32), sums, preferred_element_type=jnp.float32, precision=lax.Precision.HIGHEST
        )

    part_out[...] = spread(0, EARLY)
    arrivals(3, 0)
    arrivals(3, 1)
    work(3)
    part_out[...] += spread(EARLY, POSITIONS)
    for copy in sent:
        copy.wait_send()


def extra_kernel(blocks, extra, part, table, found, east, north, *refs):
    givers, taking, refs = refs[: len(SLOTS)], refs[len(SLOTS)], refs[len(SLOTS) + 1 :]
    out, table_s, found_s, east_s, north_s, sems = refs
    out[...] = part[...]

    @pl.when(extra[0, 0] > 0)
    def _():
        copies = [
            pltpu.make_async_copy(a, b, sems.at[i])
            for i, (a, b) in enumerate([(table, table_s), (found, found_s), (east, east_s), (north, north_s)])
        ]
        for copy in copies:
            copy.start()
        for copy in copies:
            copy.wait()

        def row_step(row, carry):
            def entry_step(k, carry):
                word = table_s[row, k]
                receiver, turned, giver, lane = word & 255, (word >> 8) & 7, (word >> 11) & 31, word >> 16
                line = tap_rows(east_s[row, lane], north_s[row, lane])
                for ref, slots in zip(givers, SLOTS):
                    for i, t in enumerate(slots):

                        @pl.when(turned == t)
                        def _():
                            out[pl.ds(receiver, 1), :] += pair_sum(line, ref[i * blocks + giver], taking[receiver])

                return carry

            return lax.fori_loop(0, found_s[row, 0], entry_step, carry)

        lax.fori_loop(0, table.shape[0], row_step, 0)


def sum_kernel(part, out, rows_in, mine, pieces, row_send, row_recv, mem_send, mem_recv):
    _, z, x, core = place()
    mem = lax.axis_index("mem")
    mems = mine.shape[0]

    def mem_peer(step):
        return {"mem": lax.rem(mem + step, mems)}

    greet([row_peer(z, x, core, s) for s in range(1, XC)] + [mem_peer(s) for s in range(1, mems)])()
    copies = []
    for s in range(1, XC):
        copy = pltpu.make_async_remote_copy(
            src_ref=part.at[s], dst_ref=rows_in.at[mirrored(s)],
            send_sem=row_send.at[s], recv_sem=row_recv.at[mirrored(s)],
            device_id=row_peer(z, x, core, s), device_id_type=MESH_ID,
        )
        copy.start()
        copies.append(copy)
    summed = part[0]
    for s in range(1, XC):
        copies[s - 1].wait()
    for s in range(1, XC):
        summed = summed + rows_in[s]
    each = summed.shape[0] // mems
    for m in range(mems):
        mine[m, :each, :] = summed[m * each : (m + 1) * each, :]
        mine[m, each:, :] = jnp.zeros((mine.shape[1] - each, BLOCK), jnp.float32)
    pieces[mem] = mine[mem]
    copies = []
    for s in range(1, mems):
        copy = pltpu.make_async_remote_copy(
            src_ref=mine.at[lax.rem(mem + s, mems)], dst_ref=pieces.at[mem],
            send_sem=mem_send.at[s], recv_sem=mem_recv.at[s],
            device_id=mem_peer(s), device_id_type=MESH_ID,
        )
        copy.start()
        copies.append(copy)
    for copy in copies:
        copy.wait()
    for l in range(LEVELS):
        first = l * (mems // LEVELS)
        both = pieces[first]
        for m in range(first + 1, first + mems // LEVELS):
            both = both + pieces[m]
        both = both / (MEMBERS - 1.0)
        for i in range(each):
            out[l : l + 1, i * BLOCK : (i + 1) * BLOCK] = both[i : i + 1, :]


def shards(ensemble, control, pair_home, pair_local, pair_count, pair_shift):
    member_rows, columns = ensemble.shape
    blocks = columns // BLOCK
    owners = lax.axis_size("col")
    mems = lax.axis_size("mem")
    entries = 2 * pair_shift.shape[1]
    sign = jnp.asarray(np.array([1.0, -1.0], np.float32))
    both = (pair_shift[:, :, None] * sign).reshape(2, entries)
    small = jnp.concatenate([both.reshape(4, LANES), jnp.zeros((4, LANES), jnp.float32)])
    live = jnp.broadcast_to(pair_count[:, None], (8, LANES))
    home = pair_home.reshape(-1, LANES)
    local = pair_local.reshape(-1, LANES)
    smem = pl.BlockSpec(memory_space=pltpu.SMEM)
    vmem = pl.BlockSpec(memory_space=pltpu.VMEM)
    dma = pltpu.SemaphoreType.DMA
    shape = jax.ShapeDtypeStruct

    *givers, taking, part, table, found, extra, east, north = pl.pallas_call(
        functools.partial(gather_kernel, blocks),
        out_shape=[shape((len(slots) * blocks, member_rows, BLOCK), jnp.bfloat16) for slots in SLOTS] + [
            shape((XC * blocks, member_rows, BLOCK), jnp.bfloat16),
            shape((XC * blocks, BLOCK), jnp.float32),
            shape((owners, entries), jnp.int32),
            shape((owners, LANES), jnp.int32),
            shape((8, LANES), jnp.int32),
            shape((owners, entries), jnp.float32),
            shape((owners, entries), jnp.float32),
        ],
        in_specs=[vmem] * 6,
        out_specs=[vmem] * (len(SLOTS) + 7),
        scratch_shapes=[
            pltpu.VMEM((owners * 8, LANES), jnp.float32),
            pltpu.VMEM((owners * 8, LANES), jnp.int32),
            pltpu.VMEM((8, POSITIONS), jnp.int32),
            pltpu.VMEM((POSITIONS, 8), jnp.float32),
            pltpu.VMEM((POSITIONS, BLOCK), jnp.float32),
            pltpu.SMEM((8, POSITIONS), jnp.int32),
            pltpu.VMEM((POSITIONS // GROUP, GROUP, BLOCK), jnp.float32),
            dma((1,)),
            dma((2, 4, 2)), dma((2, 4, 2)), dma((2, 2, 2)), dma((2, 2, 2)), dma((X, 2)), dma((X, 2)),
            dma((2, XC)), dma((2, XC)), dma((2, Z)), dma((2, Z)),
        ],
        compiler_params=pltpu.CompilerParams(
            collective_id=0, has_side_effects=True, vmem_limit_bytes=28 * 1024 * 1024
        ),
    )(ensemble, control, small, live, home, local)

    part = pl.pallas_call(
        functools.partial(extra_kernel, blocks),
        out_shape=shape(part.shape, part.dtype),
        in_specs=[smem] + [vmem] * (len(SLOTS) + 6),
        out_specs=vmem,
        scratch_shapes=[
            pltpu.SMEM(table.shape, jnp.int32), pltpu.SMEM(found.shape, jnp.int32),
            pltpu.SMEM(east.shape, jnp.float32), pltpu.SMEM(north.shape, jnp.float32),
            dma((4,)),
        ],
        compiler_params=pltpu.CompilerParams(vmem_limit_bytes=24 * 1024 * 1024),
    )(extra, part, table, found, east, north, *givers, taking)
    part = part.reshape(XC, blocks, BLOCK)

    return pl.pallas_call(
        sum_kernel,
        out_shape=jax.ShapeDtypeStruct((LEVELS, columns // mems), jnp.float32),
        in_specs=[vmem],
        out_specs=vmem,
        scratch_shapes=[
            pltpu.VMEM((XC, blocks, BLOCK), jnp.float32),
            pltpu.VMEM((mems, 8, BLOCK), jnp.float32),
            pltpu.VMEM((mems, 8, BLOCK), jnp.float32),
            dma((XC,)), dma((XC,)), dma((mems,)), dma((mems,)),
        ],
        compiler_params=pltpu.CompilerParams(
            collective_id=1, has_side_effects=True, vmem_limit_bytes=8 * 1024 * 1024
        ),
    )(part)


def solution(mesh):
    return jax.shard_map(
        shards,
        mesh=mesh,
        in_specs=(P("mem", "col"), P(None, "col"), P(), P(), P("col"), P(None, "col")),
        out_specs=P(None, ("col", "mem")),
        check_vma=False,
    )
```

```python
import functools

import jax
import jax.numpy as jnp
import numpy as np
from jax import lax
from jax.experimental import pallas as pl
from jax.experimental.pallas import tpu as pltpu
from jax.sharding import PartitionSpec as P

MEMBERS = 80
LEVELS = 4
SIDE = 16
BLOCK = 256
SPACING_KM = 200.0
HALF_WIDTH = 250.0
XC = 8
Z = 8
X = 4
LANES = 128
GROUP = 16
ROW_CAP = 16
SLOTS = ((0, 7, 1), (6, 2), (5, 3), (4,))
CAPS = (112, 80, 80, 48)
STARTS = (0, 112, 192, 272)
EARLY = 256
POSITIONS = 384
USED = 1 << 25
DONE = 1 << 30
MESH_ID = pl.DeviceIdType.MESH


def gaspari_cohn(squared):
    scaled = jnp.sqrt(squared * (1.0 / (HALF_WIDTH * HALF_WIDTH)))
    near_part = (
        ((-0.25 * scaled + 0.5) * scaled + 0.625) * scaled - 5.0 / 3.0
    ) * scaled * scaled + 1.0
    bounded = jnp.maximum(scaled, 1.0)
    far_part = (
        ((((scaled * (1.0 / 12.0) - 0.5) * scaled + 0.625) * scaled + 5.0 / 3.0) * scaled - 5.0) * scaled
        + 4.0
        - (2.0 / 3.0) / bounded
    )
    return jnp.where(scaled <= 1.0, near_part, jnp.where(scaled <= 2.0, far_part, 0.0))


def tap_rows(east, north):
    shape = (east.shape[0] if east.ndim else 1, BLOCK)
    lane = lax.broadcasted_iota(jnp.int32, shape, 1) + SIDE // 2
    de = east - SPACING_KM * ((lane & (SIDE - 1)) - SIDE // 2).astype(jnp.float32)
    dn = north + SPACING_KM * (SIDE // 2 - (lane >> 4)).astype(jnp.float32)
    return gaspari_cohn(de * de + dn * dn).astype(jnp.bfloat16).astype(jnp.float32)


def place():
    col = lax.axis_index("col")
    return col, col // XC, (col % XC) // 2, col % 2


def row_peer(z, x, core, slot):
    return {"col": z * XC + lax.rem(x + slot // 2, X) * 2 + lax.rem(core + slot % 2, 2)}


def column_peer(col, z, step):
    return {"col": col + (lax.rem(z + step, Z) - z) * XC}


def mirrored(slot):
    return (X - slot // 2) % X * 2 + slot % 2


def greet(peers):
    barrier = pltpu.get_barrier_semaphore()
    for peer in peers:
        pl.semaphore_signal(barrier, inc=1, device_id=peer, device_id_type=MESH_ID)
    return lambda: pl.semaphore_wait(barrier, len(peers))


def turn(a, shift):
    return pltpu.roll(a, shift % a.shape[1], 1)


def own_entries(home, local, count, z, x, core):
    lane = lax.broadcasted_iota(jnp.int32, home.shape, 1)
    even = (lane & 1) == 0
    other_home = jnp.where(even, turn(home, -1), turn(home, 1))
    other_local = jnp.where(even, turn(local, -1), turn(local, 1))
    mine = ((home >> 3) == z) & ((other_home & 7) == x * 2 + core) & ((lane >> 1) < count)
    slot = ((((home >> 1) & 3) - x) & 3) * 2 + ((home ^ core) & 1)
    turned = ((other_home >> 3) - z) & 7
    return mine, slot, other_local, turned


def by_slot(turned, values):
    found = jnp.zeros_like(turned)
    for t, value in values.items():
        found = jnp.where(turned == t, value, found)
    return found


def row_rank(mine):
    rank = mine.astype(jnp.int32)
    lane = lax.broadcasted_iota(jnp.int32, rank.shape, 1)
    step = 1
    while step < rank.shape[1]:
        rank = rank + jnp.where(lane >= step, turn(rank, step), 0)
        step *= 2
    return rank - 1


def pack_rows(mine, rank, arrays):
    lane = lax.broadcasted_iota(jnp.int32, rank.shape, 1)
    move = jnp.where(mine, lane - rank, 0)
    arrays = [jnp.where(mine, a, 0) for a in arrays]
    step = 1
    while step < rank.shape[1]:
        next_move = turn(move, -step)
        arrives, leaves = (next_move & step) != 0, (move & step) != 0
        arrays = [jnp.where(arrives, turn(a, -step), jnp.where(leaves, 0, a)) for a in arrays]
        move = jnp.where(arrives, next_move, jnp.where(leaves, 0, move))
        step *= 2
    return arrays


def group_rank(mine, group):
    rows, lanes = mine.shape
    line = lax.broadcasted_iota(jnp.int32, (rows, lanes), 0)
    lane = lax.broadcasted_iota(jnp.int32, (rows, lanes), 1)
    rank = jnp.zeros((rows, lanes), jnp.int32)
    for t in range(0, len(CAPS), 2):
        low, high = mine & (group == t), mine & (group == t + 1)
        upto = low.astype(jnp.int32) + (high.astype(jnp.int32) << 16)
        step = 1
        while step < ROW_CAP:
            upto = upto + jnp.where(lane >= step, turn(upto, step), 0)
            step *= 2
        whole = jnp.broadcast_to(upto[:, ROW_CAP - 1 : ROW_CAP], (rows, lanes))
        above = whole
        step = 1
        while step < rows:
            above = above + jnp.where(line >= step, pltpu.roll(above, step, 0), 0)
            step *= 2
        upto = upto + above - whole
        rank = jnp.where(low, (upto & 0xFFFF) - 1, jnp.where(high, (upto >> 16) - 1, rank))
    return rank


def packed_entries(mine, slot, local, giver, turned, east, north):
    lane = lax.broadcasted_iota(jnp.int32, mine.shape, 1)
    code = slot | (local << 3) | (giver << 8) | (turned << 13) | (lane << 16) | (1 << 24)
    rank = row_rank(mine)
    return pack_rows(mine, rank, [code, east, north]), jnp.max(rank, axis=1, keepdims=True) + 1


def make_lists(code, east, north, blocks):
    table = code
    code, east, north = code[:, :LANES], east[:, :LANES], north[:, :LANES]
    kept = (code != 0) & (lax.broadcasted_iota(jnp.int32, code.shape, 1) < ROW_CAP)
    turned = (code >> 13) & 7
    group = by_slot(turned, {t: g for g, slots in enumerate(SLOTS) for t in slots})
    rank = group_rank(kept, group)
    kept = kept & (rank < by_slot(group, dict(enumerate(CAPS))))
    place_at = jnp.where(kept, by_slot(group, dict(enumerate(STARTS))) + rank, -1)
    giver = ((code >> 8) & 31) + by_slot(turned, {t: i * blocks for slots in SLOTS for i, t in enumerate(slots)})
    table = jnp.concatenate([jnp.where(kept, code | DONE, code), table[:, LANES:]], axis=1)
    code = (code & 255) | (giver << 8) | USED
    rows = code.shape[0]
    lane = lax.broadcasted_iota(jnp.int32, (rows, POSITIONS), 1)
    words = jnp.zeros((rows, POSITIONS), jnp.int32)
    easts = jnp.zeros((rows, POSITIONS), jnp.float32)
    norths = jnp.zeros((rows, POSITIONS), jnp.float32)
    for j in range(ROW_CAP):
        hit = place_at[:, j : j + 1] == lane
        words = words + jnp.where(hit, code[:, j : j + 1], 0)
        easts = easts + jnp.where(hit, east[:, j : j + 1], 0.0)
        norths = norths + jnp.where(hit, north[:, j : j + 1], 0.0)
    words, easts, norths = [jnp.sum(v, axis=0, keepdims=True) for v in (words, easts, norths)]
    return words, jnp.where(words >= USED, easts, 1e5), norths, table


def taper_tile(row):
    within = lax.broadcasted_iota(jnp.int32, (SIDE, BLOCK), 1) & (SIDE - 1)
    within = jnp.abs(within - lax.broadcasted_iota(jnp.int32, (SIDE, BLOCK), 0)) <= SIDE // 4
    taps = pltpu.roll(jnp.broadcast_to(row, (SIDE, BLOCK)), 0, 1, stride=1, stride_axis=0)
    taps = jnp.where(within, taps, 0.0)
    left, right = taps[:, :LANES], taps[:, LANES:]
    lane = lax.broadcasted_iota(jnp.int32, left.shape, 1)
    middle, first, last = [], [], []
    for k in range(8):
        low = lane < 16 * k
        a, b = turn(left, 16 * k), turn(right, 16 * k)
        middle.append(jnp.where(low, a, b).astype(jnp.bfloat16))
        if k < 4:
            first.append(jnp.where(low, 0.0, a).astype(jnp.bfloat16))
        else:
            last.append(jnp.where(low, b, 0.0).astype(jnp.bfloat16))
    return jnp.concatenate(middle + first + last)


def pair_sum(row, give, take):
    south, north = [give[:, i * LANES : (i + 1) * LANES].astype(jnp.float32) for i in range(2)]
    low = lax.broadcasted_iota(jnp.int32, south.shape, 1) < LANES // 2
    give = jnp.concatenate([
        jnp.concatenate([south, jnp.where(low, north, 0.0)], axis=1),
        jnp.concatenate([north, jnp.where(low, 0.0, south)], axis=1),
    ]).astype(jnp.bfloat16)
    reached = jnp.dot(give, taper_tile(row), preferred_element_type=jnp.float32)
    count = take.shape[0]
    sums = [
        jnp.sum(reached[i * count : (i + 1) * count] * take[:, i * LANES : (i + 1) * LANES].astype(jnp.float32),
                axis=0, keepdims=True)
        for i in range(2)
    ]
    return jnp.concatenate(sums, axis=1)


def gather_kernel(
    blocks, ensemble, control, small, live, home, local, *refs,
):
    givers, refs = refs[: len(SLOTS)], refs[len(SLOTS) :]
    taking, part_out, table, found, extra, east, north = refs[:7]
    (
        seen, counts, words, taps, words_s, row_sums, local_sem,
        z_send, z_recv, x_send, x_recv, core_send, core_recv, row_send, row_recv, col_send, col_recv,
    ) = refs[7:]
    col, z, x, core = place()
    entered = greet([row_peer(z, x, core, s) for s in range(1, XC)] + [column_peer(col, z, s) for s in range(1, Z)])
    member_rows, columns = ensemble.shape
    half = blocks // 2
    level = (lax.axis_index("mem") * member_rows) // MEMBERS
    scale = jnp.zeros((1, columns), jnp.float32)
    for l in range(LEVELS):
        scale = jnp.where(level == l, control[l : l + 1, :].astype(jnp.float32), scale)
    for b in range(blocks):
        own = ensemble[:, b * BLOCK : (b + 1) * BLOCK]
        taking[b] = own
        givers[0][b] = (own.astype(jnp.float32) * scale[:, b * BLOCK : (b + 1) * BLOCK]).astype(jnp.bfloat16)
    seen[pl.ds(pl.multiple_of(col * 8, 8), 8), :] = small[...]
    counts[pl.ds(pl.multiple_of(col * 8, 8), 8), :] = live[...]

    entered()

    sent = []

    def send(source, target, send_sem, recv_sem, peer):
        copy = pltpu.make_async_remote_copy(
            src_ref=source, dst_ref=target, send_sem=send_sem, recv_sem=recv_sem,
            device_id=peer, device_id_type=MESH_ID,
        )
        copy.start()
        sent.append(copy)
        return copy

    def part(ref, slot, c):
        return ref.at[pl.ds(slot * blocks + c * half, half)]

    def giver_part(turned, c):
        for ref, slots in zip(givers, SLOTS):
            if turned in slots:
                return part(ref, slots.index(turned), c)

    def send_z(way, step, c):
        sign = 1 if way == 0 else -1
        return send(
            giver_part(-sign * step % Z, c), giver_part(-sign * (step + 1) % Z, c),
            z_send.at[way, step, c], z_recv.at[way, step, c], column_peer(col, z, sign % Z),
        )

    def send_x(way, step, c):
        sign = 1 if way == 0 else -1
        return send(
            part(taking, (-sign * step) % X * 2, c), part(taking, (-sign * (step + 1)) % X * 2, c),
            x_send.at[way, step, c], x_recv.at[way, step, c], row_peer(z, x, core, sign % X * 2),
        )

    def send_core(turned, c):
        return send(
            part(taking, turned * 2, c), part(taking, turned * 2 + 1, c),
            core_send.at[turned, c], core_recv.at[turned, c], row_peer(z, x, core, 1),
        )

    row_copies = []
    for i, ref in enumerate((seen, counts)):
        rows = ref.at[pl.ds(pl.multiple_of(col * 8, 8), 8), :]
        for s in range(1, XC):
            row_copies.append(send(rows, rows, row_send.at[i, s], row_recv.at[i, s], row_peer(z, x, core, s)))
    zs, xs, cores = {}, {}, []
    for c in range(2):
        for way in range(2):
            zs[way, 0, c] = send_z(way, 0, c)
            xs[way, 0, c] = send_x(way, 0, c)
    for c in range(2):
        cores.append(send_core(0, c))
    for copy in row_copies:
        copy.wait_recv()
    col_copies = []
    for i, ref in enumerate((seen, counts)):
        rows = ref.at[pl.ds(pl.multiple_of(z * 64, 64), 64), :]
        for s in range(1, Z):
            col_copies.append(send(rows, rows, col_send.at[i, s], col_recv.at[i, s], column_peer(col, z, s)))

    def row_arrivals(step, c):
        for way in range(2):
            turned = (-(1 if way == 0 else -1) * (step + 1)) % X
            if step == 0 or (step == 1 and c == way):
                xs[way, step, c].wait_recv()
                if step == 0 and c == way:
                    xs[way, 1, c] = send_x(way, 1, c)
                cores.append(send_core(turned, c))

    def arrivals(step, c, rows=True):
        if rows:
            row_arrivals(step, c)
        for way in range(2):
            if step < 3 or c == way:
                zs[way, step, c].wait_recv()
                if step < 2 or (step == 2 and c == way):
                    zs[way, step + 1, c] = send_z(way, step + 1, c)
    def own_lists():
        for copy in col_copies:
            copy.wait_recv()
        owners = seen.shape[0] // 8
        rows = [seen[pl.ds(i, owners, stride=8), :] for i in range(4)]
        shift_e, shift_n = jnp.concatenate(rows[0:2], axis=1), jnp.concatenate(rows[2:4], axis=1)
        east[...], north[...] = shift_e, shift_n
        count = counts[pl.ds(0, owners, stride=8), :]
        count = jnp.concatenate([count, count], axis=1)
        homes = jnp.concatenate([home[pl.ds(i, owners, stride=2), :] for i in range(2)], axis=1)
        locals_ = jnp.concatenate([local[pl.ds(i, owners, stride=2), :] for i in range(2)], axis=1)
        mine, slot, giver, turned = own_entries(homes, locals_, count, z, x, core)
        packed, amount = packed_entries(mine, slot, locals_, giver, turned, shift_e, shift_n)
        found[...] = jnp.broadcast_to(amount, found.shape)
        return packed

    list_copy = pltpu.make_async_copy(words, words_s, local_sem.at[0])

    def place_lists(packed):
        word, shift_e, shift_n, entries = make_lists(*packed, blocks)
        words[...] = jnp.broadcast_to(word, words.shape)
        list_copy.start()
        table[...] = entries
        left = ((entries != 0) & (entries < DONE)).astype(jnp.int32)
        left = jnp.max(jnp.max(left, axis=1, keepdims=True), axis=0, keepdims=True)
        extra[...] = jnp.broadcast_to(left, extra.shape)
        return jnp.concatenate([shift_e, shift_n, jnp.zeros((6, POSITIONS), jnp.float32)]).T

    def some_taps(shift, c):
        at = slice(c * LANES, (c + 1) * LANES)
        taps[at, :] = tap_rows(shift[at, 0:1], shift[at, 1:2])

    def work(group, begin=0, end=None):
        first = STARTS[group] // GROUP

        def some(n, carry):
            rows = taps[pl.ds(pl.multiple_of(n * GROUP, GROUP), GROUP), :]
            sums = []
            for g in range(GROUP):
                word = words_s[0, n * GROUP + g]
                sums.append(pair_sum(
                    rows[g : g + 1, :],
                    givers[group][(word >> 8) & 127], taking[(word & 7) * blocks + ((word >> 3) & 31)],
                ))
            row_sums[n] = jnp.concatenate(sums)
            return carry

        end = CAPS[group] if end is None else end
        lax.fori_loop(first + begin // GROUP, first + end // GROUP, some, 0)

    row_sums[...] = jnp.zeros_like(row_sums)
    packed = own_lists()
    arrivals(0, 0)
    shift = place_lists(packed)
    arrivals(0, 1)
    some_taps(shift, 0)
    arrivals(1, 0)
    list_copy.wait()
    row_arrivals(1, 1)
    for copy in cores:
        copy.wait_recv()
    work(0, 0, 48)
    arrivals(1, 1, False)
    work(0, 48)
    some_taps(shift, 1)
    arrivals(2, 0)
    work(1)
    some_taps(shift, 2)
    arrivals(2, 1)
    work(2)

    taken = (words[0:1, :] & 7) * blocks + ((words[0:1, :] >> 3) & 31)
    count = part_out.shape[0]

    def spread(begin, end):
        hot = lax.broadcasted_iota(jnp.int32, (count, end - begin), 0) == taken[:, begin:end]
        sums = row_sums[begin // GROUP : end // GROUP].reshape(end - begin, BLOCK)
        return jnp.dot(
            hot.astype(jnp.float32), sums, preferred_element_type=jnp.float32, precision=lax.Precision.HIGHEST
        )

    part_out[...] = spread(0, EARLY)
    arrivals(3, 0)
    arrivals(3, 1)
    work(3)
    part_out[...] += spread(EARLY, POSITIONS)
    for copy in sent:
        copy.wait_send()


def extra_kernel(blocks, extra, part, table, found, east, north, *refs):
    givers, taking, refs = refs[: len(SLOTS)], refs[len(SLOTS)], refs[len(SLOTS) + 1 :]
    out, table_s, found_s, east_s, north_s, sems = refs
    out[...] = part[...]

    @pl.when(extra[0, 0] > 0)
    def _():
        copies = [
            pltpu.make_async_copy(a, b, sems.at[i])
            for i, (a, b) in enumerate([(table, table_s), (found, found_s), (east, east_s), (north, north_s)])
        ]
        for copy in copies:
            copy.start()
        for copy in copies:
            copy.wait()

        def row_step(row, carry):
            def entry_step(k, carry):
                word = table_s[row, k]
                receiver = (word & 7) * blocks + ((word >> 3) & 31)
                giver, turned, lane = (word >> 8) & 31, (word >> 13) & 7, (word >> 16) & 255
                line = tap_rows(east_s[row, lane], north_s[row, lane])
                for ref, slots in zip(givers, SLOTS):
                    for i, t in enumerate(slots):

                        @pl.when((turned == t) & (word < DONE))
                        def _():
                            out[pl.ds(receiver, 1), :] += pair_sum(line, ref[i * blocks + giver], taking[receiver])

                return carry

            return lax.fori_loop(0, found_s[row, 0], entry_step, carry)

        lax.fori_loop(0, table.shape[0], row_step, 0)


def sum_kernel(part, out, rows_in, mine, pieces, row_send, row_recv, mem_send, mem_recv):
    _, z, x, core = place()
    mem = lax.axis_index("mem")
    mems = mine.shape[0]

    def mem_peer(step):
        return {"mem": lax.rem(mem + step, mems)}

    greet([row_peer(z, x, core, s) for s in range(1, XC)] + [mem_peer(s) for s in range(1, mems)])()
    copies = []
    for s in range(1, XC):
        copy = pltpu.make_async_remote_copy(
            src_ref=part.at[s], dst_ref=rows_in.at[mirrored(s)],
            send_sem=row_send.at[s], recv_sem=row_recv.at[mirrored(s)],
            device_id=row_peer(z, x, core, s), device_id_type=MESH_ID,
        )
        copy.start()
        copies.append(copy)
    summed = part[0]
    for s in range(1, XC):
        copies[s - 1].wait()
    for s in range(1, XC):
        summed = summed + rows_in[s]
    each = summed.shape[0] // mems
    for m in range(mems):
        mine[m, :each, :] = summed[m * each : (m + 1) * each, :]
        mine[m, each:, :] = jnp.zeros((mine.shape[1] - each, BLOCK), jnp.float32)
    pieces[mem] = mine[mem]
    copies = []
    for s in range(1, mems):
        copy = pltpu.make_async_remote_copy(
            src_ref=mine.at[lax.rem(mem + s, mems)], dst_ref=pieces.at[mem],
            send_sem=mem_send.at[s], recv_sem=mem_recv.at[s],
            device_id=mem_peer(s), device_id_type=MESH_ID,
        )
        copy.start()
        copies.append(copy)
    for copy in copies:
        copy.wait()
    for l in range(LEVELS):
        first = l * (mems // LEVELS)
        both = pieces[first]
        for m in range(first + 1, first + mems // LEVELS):
            both = both + pieces[m]
        both = both / (MEMBERS - 1.0)
        for i in range(each):
            out[l : l + 1, i * BLOCK : (i + 1) * BLOCK] = both[i : i + 1, :]


def shards(ensemble, control, pair_home, pair_local, pair_count, pair_shift):
    member_rows, columns = ensemble.shape
    blocks = columns // BLOCK
    owners = lax.axis_size("col")
    mems = lax.axis_size("mem")
    entries = 2 * pair_shift.shape[1]
    sign = jnp.asarray(np.array([1.0, -1.0], np.float32))
    both = (pair_shift[:, :, None] * sign).reshape(2, entries)
    small = jnp.concatenate([both.reshape(4, LANES), jnp.zeros((4, LANES), jnp.float32)])
    live = jnp.broadcast_to(pair_count[:, None], (8, LANES))
    home = pair_home.reshape(-1, LANES)
    local = pair_local.reshape(-1, LANES)
    smem = pl.BlockSpec(memory_space=pltpu.SMEM)
    vmem = pl.BlockSpec(memory_space=pltpu.VMEM)
    dma = pltpu.SemaphoreType.DMA
    shape = jax.ShapeDtypeStruct

    *givers, taking, part, table, found, extra, east, north = pl.pallas_call(
        functools.partial(gather_kernel, blocks),
        out_shape=[shape((len(slots) * blocks, member_rows, BLOCK), jnp.bfloat16) for slots in SLOTS] + [
            shape((XC * blocks, member_rows, BLOCK), jnp.bfloat16),
            shape((XC * blocks, BLOCK), jnp.float32),
            shape((owners, entries), jnp.int32),
            shape((owners, LANES), jnp.int32),
            shape((8, LANES), jnp.int32),
            shape((owners, entries), jnp.float32),
            shape((owners, entries), jnp.float32),
        ],
        in_specs=[vmem] * 6,
        out_specs=[vmem] * (len(SLOTS) + 7),
        scratch_shapes=[
            pltpu.VMEM((owners * 8, LANES), jnp.float32),
            pltpu.VMEM((owners * 8, LANES), jnp.int32),
            pltpu.VMEM((8, POSITIONS), jnp.int32),
            pltpu.VMEM((POSITIONS, BLOCK), jnp.float32),
            pltpu.SMEM((8, POSITIONS), jnp.int32),
            pltpu.VMEM((POSITIONS // GROUP, GROUP, BLOCK), jnp.float32),
            dma((1,)),
            dma((2, 4, 2)), dma((2, 4, 2)), dma((2, 2, 2)), dma((2, 2, 2)), dma((X, 2)), dma((X, 2)),
            dma((2, XC)), dma((2, XC)), dma((2, Z)), dma((2, Z)),
        ],
        compiler_params=pltpu.CompilerParams(
            collective_id=0, has_side_effects=True, vmem_limit_bytes=28 * 1024 * 1024
        ),
    )(ensemble, control, small, live, home, local)

    part = pl.pallas_call(
        functools.partial(extra_kernel, blocks),
        out_shape=shape(part.shape, part.dtype),
        in_specs=[smem] + [vmem] * (len(SLOTS) + 6),
        out_specs=vmem,
        scratch_shapes=[
            pltpu.SMEM(table.shape, jnp.int32), pltpu.SMEM(found.shape, jnp.int32),
            pltpu.SMEM(east.shape, jnp.float32), pltpu.SMEM(north.shape, jnp.float32),
            dma((4,)),
        ],
        compiler_params=pltpu.CompilerParams(vmem_limit_bytes=24 * 1024 * 1024),
    )(extra, part, table, found, east, north, *givers, taking)
    part = part.reshape(XC, blocks, BLOCK)

    return pl.pallas_call(
        sum_kernel,
        out_shape=jax.ShapeDtypeStruct((LEVELS, columns // mems), jnp.float32),
        in_specs=[vmem],
        out_specs=vmem,
        scratch_shapes=[
            pltpu.VMEM((XC, blocks, BLOCK), jnp.float32),
            pltpu.VMEM((mems, 8, BLOCK), jnp.float32),
            pltpu.VMEM((mems, 8, BLOCK), jnp.float32),
            dma((XC,)), dma((XC,)), dma((mems,)), dma((mems,)),
        ],
        compiler_params=pltpu.CompilerParams(
            collective_id=1, has_side_effects=True, vmem_limit_bytes=8 * 1024 * 1024
        ),
    )(part)


def solution(mesh):
    return jax.shard_map(
        shards,
        mesh=mesh,
        in_specs=(P("mem", "col"), P(None, "col"), P(), P(), P("col"), P(None, "col")),
        out_specs=P(None, ("col", "mem")),
        check_vma=False,
    )
```

```python
import functools

import jax
import jax.numpy as jnp
import numpy as np
from jax import lax
from jax.experimental import pallas as pl
from jax.experimental.pallas import tpu as pltpu
from jax.sharding import PartitionSpec as P

MEMBERS = 80
LEVELS = 4
SIDE = 16
BLOCK = 256
SPACING_KM = 200.0
HALF_WIDTH = 250.0
XC = 8
Z = 8
X = 4
LANES = 128
GROUP = 16
ROW_CAP = 16
SLOTS = ((0, 7, 1), (6, 2), (5, 3), (4,))
CAPS = (112, 80, 80, 48)
STARTS = (0, 112, 192, 272)
EARLY = 256
POSITIONS = 384
USED = 1 << 25
DONE = 1 << 30
MESH_ID = pl.DeviceIdType.MESH


def gaspari_cohn(squared):
    scaled = jnp.sqrt(squared * (1.0 / (HALF_WIDTH * HALF_WIDTH)))
    near_part = (
        ((-0.25 * scaled + 0.5) * scaled + 0.625) * scaled - 5.0 / 3.0
    ) * scaled * scaled + 1.0
    bounded = jnp.maximum(scaled, 1.0)
    far_part = (
        ((((scaled * (1.0 / 12.0) - 0.5) * scaled + 0.625) * scaled + 5.0 / 3.0) * scaled - 5.0) * scaled
        + 4.0
        - (2.0 / 3.0) / bounded
    )
    return jnp.where(scaled <= 1.0, near_part, jnp.where(scaled <= 2.0, far_part, 0.0))


def tap_rows(east, north):
    shape = (east.shape[0] if east.ndim else 1, BLOCK)
    lane = lax.broadcasted_iota(jnp.int32, shape, 1) + SIDE // 2
    de = east - SPACING_KM * ((lane & (SIDE - 1)) - SIDE // 2).astype(jnp.float32)
    dn = north + SPACING_KM * (SIDE // 2 - (lane >> 4)).astype(jnp.float32)
    return gaspari_cohn(de * de + dn * dn).astype(jnp.bfloat16).astype(jnp.float32)


def place():
    col = lax.axis_index("col")
    return col, col // XC, (col % XC) // 2, col % 2


def row_peer(z, x, core, slot):
    return {"col": z * XC + lax.rem(x + slot // 2, X) * 2 + lax.rem(core + slot % 2, 2)}


def column_peer(col, z, step):
    return {"col": col + (lax.rem(z + step, Z) - z) * XC}


def mirrored(slot):
    return (X - slot // 2) % X * 2 + slot % 2


def greet(peers):
    barrier = pltpu.get_barrier_semaphore()
    for peer in peers:
        pl.semaphore_signal(barrier, inc=1, device_id=peer, device_id_type=MESH_ID)
    return lambda: pl.semaphore_wait(barrier, len(peers))


def turn(a, shift):
    return pltpu.roll(a, shift % a.shape[1], 1)


def own_entries(home, local, count, z, x, core):
    lane = lax.broadcasted_iota(jnp.int32, home.shape, 1)
    even = (lane & 1) == 0
    other_home = jnp.where(even, turn(home, -1), turn(home, 1))
    other_local = jnp.where(even, turn(local, -1), turn(local, 1))
    mine = ((home >> 3) == z) & ((other_home & 7) == x * 2 + core) & ((lane >> 1) < count)
    slot = ((((home >> 1) & 3) - x) & 3) * 2 + ((home ^ core) & 1)
    turned = ((other_home >> 3) - z) & 7
    return mine, slot, other_local, turned


def by_slot(turned, values):
    found = jnp.zeros_like(turned)
    for t, value in values.items():
        found = jnp.where(turned == t, value, found)
    return found


def row_rank(mine):
    rank = mine.astype(jnp.int32)
    lane = lax.broadcasted_iota(jnp.int32, rank.shape, 1)
    step = 1
    while step < rank.shape[1]:
        rank = rank + jnp.where(lane >= step, turn(rank, step), 0)
        step *= 2
    return rank - 1


def pack_rows(mine, rank, arrays):
    lane = lax.broadcasted_iota(jnp.int32, rank.shape, 1)
    move = jnp.where(mine, lane - rank, 0)
    arrays = [jnp.where(mine, a, 0) for a in arrays]
    step = 1
    while step < rank.shape[1]:
        next_move = turn(move, -step)
        arrives, leaves = (next_move & step) != 0, (move & step) != 0
        arrays = [jnp.where(arrives, turn(a, -step), jnp.where(leaves, 0, a)) for a in arrays]
        move = jnp.where(arrives, next_move, jnp.where(leaves, 0, move))
        step *= 2
    return arrays


def group_rank(mine, group):
    rows, lanes = mine.shape
    line = lax.broadcasted_iota(jnp.int32, (rows, lanes), 0)
    lane = lax.broadcasted_iota(jnp.int32, (rows, lanes), 1)
    rank = jnp.zeros((rows, lanes), jnp.int32)
    for t in range(0, len(CAPS), 2):
        low, high = mine & (group == t), mine & (group == t + 1)
        upto = low.astype(jnp.int32) + (high.astype(jnp.int32) << 16)
        step = 1
        while step < ROW_CAP:
            upto = upto + jnp.where(lane >= step, turn(upto, step), 0)
            step *= 2
        whole = jnp.broadcast_to(upto[:, ROW_CAP - 1 : ROW_CAP], (rows, lanes))
        above = whole
        step = 1
        while step < rows:
            above = above + jnp.where(line >= step, pltpu.roll(above, step, 0), 0)
            step *= 2
        upto = upto + above - whole
        rank = jnp.where(low, (upto & 0xFFFF) - 1, jnp.where(high, (upto >> 16) - 1, rank))
    return rank


def packed_entries(mine, slot, local, giver, turned, east, north):
    lane = lax.broadcasted_iota(jnp.int32, mine.shape, 1)
    code = slot | (local << 3) | (giver << 8) | (turned << 13) | (lane << 16) | (1 << 24)
    rank = row_rank(mine)
    return pack_rows(mine, rank, [code, east, north]), jnp.max(rank, axis=1, keepdims=True) + 1


def make_lists(code, east, north, blocks):
    table = code
    code, east, north = code[:, :LANES], east[:, :LANES], north[:, :LANES]
    kept = (code != 0) & (lax.broadcasted_iota(jnp.int32, code.shape, 1) < ROW_CAP)
    turned = (code >> 13) & 7
    group = by_slot(turned, {t: g for g, slots in enumerate(SLOTS) for t in slots})
    rank = group_rank(kept, group)
    kept = kept & (rank < by_slot(group, dict(enumerate(CAPS))))
    place_at = jnp.where(kept, by_slot(group, dict(enumerate(STARTS))) + rank, -1)
    giver = ((code >> 8) & 31) + by_slot(turned, {t: i * blocks for slots in SLOTS for i, t in enumerate(slots)})
    table = jnp.concatenate([jnp.where(kept, code | DONE, code), table[:, LANES:]], axis=1)
    code = (code & 255) | (giver << 8) | USED
    rows = code.shape[0]
    lane = lax.broadcasted_iota(jnp.int32, (rows, POSITIONS), 1)
    words = jnp.zeros((rows, POSITIONS), jnp.int32)
    easts = jnp.zeros((rows, POSITIONS), jnp.float32)
    norths = jnp.zeros((rows, POSITIONS), jnp.float32)
    for j in range(ROW_CAP):
        hit = place_at[:, j : j + 1] == lane
        words = words + jnp.where(hit, code[:, j : j + 1], 0)
        easts = easts + jnp.where(hit, east[:, j : j + 1], 0.0)
        norths = norths + jnp.where(hit, north[:, j : j + 1], 0.0)
    words, easts, norths = [jnp.sum(v, axis=0, keepdims=True) for v in (words, easts, norths)]
    return words, jnp.where(words >= USED, easts, 1e5), norths, table


def taper_tile(row):
    within = lax.broadcasted_iota(jnp.int32, (SIDE, BLOCK), 1) & (SIDE - 1)
    within = jnp.abs(within - lax.broadcasted_iota(jnp.int32, (SIDE, BLOCK), 0)) <= SIDE // 4
    taps = pltpu.roll(jnp.broadcast_to(row, (SIDE, BLOCK)), 0, 1, stride=1, stride_axis=0)
    taps = jnp.where(within, taps, 0.0)
    left, right = taps[:, :LANES], taps[:, LANES:]
    lane = lax.broadcasted_iota(jnp.int32, left.shape, 1)
    middle, first, last = [], [], []
    for k in range(8):
        low = lane < 16 * k
        a, b = turn(left, 16 * k), turn(right, 16 * k)
        middle.append(jnp.where(low, a, b).astype(jnp.bfloat16))
        if k < 4:
            first.append(jnp.where(low, 0.0, a).astype(jnp.bfloat16))
        else:
            last.append(jnp.where(low, b, 0.0).astype(jnp.bfloat16))
    return jnp.concatenate(middle + first + last)


def pair_sum(row, give, take):
    south, north = [give[:, i * LANES : (i + 1) * LANES].astype(jnp.float32) for i in range(2)]
    low = lax.broadcasted_iota(jnp.int32, south.shape, 1) < LANES // 2
    give = jnp.concatenate([
        jnp.concatenate([south, jnp.where(low, north, 0.0)], axis=1),
        jnp.concatenate([north, jnp.where(low, 0.0, south)], axis=1),
    ]).astype(jnp.bfloat16)
    reached = jnp.dot(give, taper_tile(row), preferred_element_type=jnp.float32)
    count = take.shape[0]
    sums = [
        jnp.sum(reached[i * count : (i + 1) * count] * take[:, i * LANES : (i + 1) * LANES].astype(jnp.float32),
                axis=0, keepdims=True)
        for i in range(2)
    ]
    return jnp.concatenate(sums, axis=1)


def gather_kernel(
    blocks, ensemble, control, small, live, named, *refs,
):
    givers, refs = refs[: len(SLOTS)], refs[len(SLOTS) :]
    taking, part_out, table, found, extra, east, north = refs[:7]
    (
        seen, counts, words, taps, words_s, row_sums, local_sem,
        z_send, z_recv, x_send, x_recv, core_send, core_recv, row_send, row_recv, col_send, col_recv,
    ) = refs[7:]
    col, z, x, core = place()
    entered = greet([row_peer(z, x, core, s) for s in range(1, XC)] + [column_peer(col, z, s) for s in range(1, Z)])
    member_rows, columns = ensemble.shape
    half = blocks // 2
    level = (lax.axis_index("mem") * member_rows) // MEMBERS
    scale = jnp.zeros((1, columns), jnp.float32)
    for l in range(LEVELS):
        scale = jnp.where(level == l, control[l : l + 1, :].astype(jnp.float32), scale)
    for b in range(blocks):
        own = ensemble[:, b * BLOCK : (b + 1) * BLOCK]
        taking[b] = own
        givers[0][b] = (own.astype(jnp.float32) * scale[:, b * BLOCK : (b + 1) * BLOCK]).astype(jnp.bfloat16)
    seen[pl.ds(pl.multiple_of(col * 8, 8), 8), :] = small[...]
    counts[pl.ds(pl.multiple_of(col * 8, 8), 8), :] = live[...]

    entered()

    sent = []

    def send(source, target, send_sem, recv_sem, peer):
        copy = pltpu.make_async_remote_copy(
            src_ref=source, dst_ref=target, send_sem=send_sem, recv_sem=recv_sem,
            device_id=peer, device_id_type=MESH_ID,
        )
        copy.start()
        sent.append(copy)
        return copy

    def part(ref, slot, c):
        return ref.at[pl.ds(slot * blocks + c * half, half)]

    def giver_part(turned, c):
        for ref, slots in zip(givers, SLOTS):
            if turned in slots:
                return part(ref, slots.index(turned), c)

    def send_z(way, step, c):
        sign = 1 if way == 0 else -1
        return send(
            giver_part(-sign * step % Z, c), giver_part(-sign * (step + 1) % Z, c),
            z_send.at[way, step, c], z_recv.at[way, step, c], column_peer(col, z, sign % Z),
        )

    def send_x(way, step, c):
        sign = 1 if way == 0 else -1
        return send(
            part(taking, (-sign * step) % X * 2, c), part(taking, (-sign * (step + 1)) % X * 2, c),
            x_send.at[way, step, c], x_recv.at[way, step, c], row_peer(z, x, core, sign % X * 2),
        )

    def send_core(turned, c):
        return send(
            part(taking, turned * 2, c), part(taking, turned * 2 + 1, c),
            core_send.at[turned, c], core_recv.at[turned, c], row_peer(z, x, core, 1),
        )

    row_copies = []
    for i, ref in enumerate((seen, counts)):
        rows = ref.at[pl.ds(pl.multiple_of(col * 8, 8), 8), :]
        for s in range(1, XC):
            row_copies.append(send(rows, rows, row_send.at[i, s], row_recv.at[i, s], row_peer(z, x, core, s)))
    zs, xs, cores = {}, {}, []
    for c in range(2):
        for way in range(2):
            zs[way, 0, c] = send_z(way, 0, c)
            xs[way, 0, c] = send_x(way, 0, c)
    for c in range(2):
        cores.append(send_core(0, c))
    for copy in row_copies:
        copy.wait_recv()
    col_copies = []
    for i, ref in enumerate((seen, counts)):
        rows = ref.at[pl.ds(pl.multiple_of(z * 64, 64), 64), :]
        for s in range(1, Z):
            col_copies.append(send(rows, rows, col_send.at[i, s], col_recv.at[i, s], column_peer(col, z, s)))

    def row_arrivals(step, c):
        for way in range(2):
            turned = (-(1 if way == 0 else -1) * (step + 1)) % X
            if step == 0 or (step == 1 and c == way):
                xs[way, step, c].wait_recv()
                if step == 0 and c == way:
                    xs[way, 1, c] = send_x(way, 1, c)
                cores.append(send_core(turned, c))

    def arrivals(step, c, rows=True):
        if rows:
            row_arrivals(step, c)
        for way in range(2):
            if step < 3 or c == way:
                zs[way, step, c].wait_recv()
                if step < 2 or (step == 2 and c == way):
                    zs[way, step + 1, c] = send_z(way, step + 1, c)
    def own_lists():
        for copy in col_copies:
            copy.wait_recv()
        owners = seen.shape[0] // 8
        rows = [seen[pl.ds(i, owners, stride=8), :] for i in range(4)]
        shift_e, shift_n = jnp.concatenate(rows[0:2], axis=1), jnp.concatenate(rows[2:4], axis=1)
        east[...], north[...] = shift_e, shift_n
        count = counts[pl.ds(0, owners, stride=8), :]
        count = jnp.concatenate([count, count], axis=1)
        names = jnp.concatenate([named[pl.ds(i, owners, stride=2), :] for i in range(2)], axis=1)
        homes, locals_ = names & 63, names >> 6
        mine, slot, giver, turned = own_entries(homes, locals_, count, z, x, core)
        packed, amount = packed_entries(mine, slot, locals_, giver, turned, shift_e, shift_n)
        found[...] = jnp.broadcast_to(amount, found.shape)
        return packed

    list_copy = pltpu.make_async_copy(words, words_s, local_sem.at[0])

    def place_lists(packed):
        word, shift_e, shift_n, entries = make_lists(*packed, blocks)
        words[...] = jnp.broadcast_to(word, words.shape)
        list_copy.start()
        table[...] = entries
        left = ((entries != 0) & (entries < DONE)).astype(jnp.int32)
        left = jnp.max(jnp.max(left, axis=1, keepdims=True), axis=0, keepdims=True)
        extra[...] = jnp.broadcast_to(left, extra.shape)
        return jnp.concatenate([shift_e, shift_n, jnp.zeros((6, POSITIONS), jnp.float32)]).T

    def some_taps(shift, c):
        at = slice(c * LANES, (c + 1) * LANES)
        taps[at, :] = tap_rows(shift[at, 0:1], shift[at, 1:2])

    def work(group, begin=0, end=None):
        first = STARTS[group] // GROUP

        def some(n, carry):
            rows = taps[pl.ds(pl.multiple_of(n * GROUP, GROUP), GROUP), :]
            sums = []
            for g in range(GROUP):
                word = words_s[0, n * GROUP + g]
                sums.append(pair_sum(
                    rows[g : g + 1, :],
                    givers[group][(word >> 8) & 127], taking[(word & 7) * blocks + ((word >> 3) & 31)],
                ))
            row_sums[n] = jnp.concatenate(sums)
            return carry

        end = CAPS[group] if end is None else end
        lax.fori_loop(first + begin // GROUP, first + end // GROUP, some, 0)

    row_sums[...] = jnp.zeros_like(row_sums)
    packed = own_lists()
    arrivals(0, 0)
    shift = place_lists(packed)
    arrivals(0, 1)
    some_taps(shift, 0)
    arrivals(1, 0)
    list_copy.wait()
    row_arrivals(1, 1)
    for copy in cores:
        copy.wait_recv()
    work(0, 0, 48)
    arrivals(1, 1, False)
    work(0, 48)
    some_taps(shift, 1)
    arrivals(2, 0)
    work(1)
    some_taps(shift, 2)
    arrivals(2, 1)
    work(2)

    taken = (words[0:1, :] & 7) * blocks + ((words[0:1, :] >> 3) & 31)
    count = part_out.shape[0]

    def spread(begin, end):
        hot = lax.broadcasted_iota(jnp.int32, (count, end - begin), 0) == taken[:, begin:end]
        sums = row_sums[begin // GROUP : end // GROUP].reshape(end - begin, BLOCK)
        return jnp.dot(
            hot.astype(jnp.float32), sums, preferred_element_type=jnp.float32, precision=lax.Precision.HIGHEST
        )

    part_out[...] = spread(0, EARLY)
    arrivals(3, 0)
    arrivals(3, 1)
    work(3)
    part_out[...] += spread(EARLY, POSITIONS)
    for copy in sent:
        copy.wait_send()


def extra_kernel(blocks, extra, part, table, found, east, north, *refs):
    givers, taking, refs = refs[: len(SLOTS)], refs[len(SLOTS)], refs[len(SLOTS) + 1 :]
    out, table_s, found_s, east_s, north_s, sems = refs
    out[...] = part[...]

    @pl.when(extra[0, 0] > 0)
    def _():
        copies = [
            pltpu.make_async_copy(a, b, sems.at[i])
            for i, (a, b) in enumerate([(table, table_s), (found, found_s), (east, east_s), (north, north_s)])
        ]
        for copy in copies:
            copy.start()
        for copy in copies:
            copy.wait()

        def row_step(row, carry):
            def entry_step(k, carry):
                word = table_s[row, k]
                receiver = (word & 7) * blocks + ((word >> 3) & 31)
                giver, turned, lane = (word >> 8) & 31, (word >> 13) & 7, (word >> 16) & 255
                line = tap_rows(east_s[row, lane], north_s[row, lane])
                for ref, slots in zip(givers, SLOTS):
                    for i, t in enumerate(slots):

                        @pl.when((turned == t) & (word < DONE))
                        def _():
                            out[pl.ds(receiver, 1), :] += pair_sum(line, ref[i * blocks + giver], taking[receiver])

                return carry

            return lax.fori_loop(0, found_s[row, 0], entry_step, carry)

        lax.fori_loop(0, table.shape[0], row_step, 0)


def sum_kernel(part, out, rows_in, mine, pieces, row_send, row_recv, mem_send, mem_recv):
    _, z, x, core = place()
    mem = lax.axis_index("mem")
    mems = mine.shape[0]

    def mem_peer(step):
        return {"mem": lax.rem(mem + step, mems)}

    entered = greet([row_peer(z, x, core, s) for s in range(1, XC)] + [mem_peer(s) for s in range(1, mems)])
    mine[...] = jnp.zeros_like(mine)
    entered()
    copies = []
    for s in range(1, XC):
        copy = pltpu.make_async_remote_copy(
            src_ref=part.at[s], dst_ref=rows_in.at[mirrored(s)],
            send_sem=row_send.at[s], recv_sem=row_recv.at[mirrored(s)],
            device_id=row_peer(z, x, core, s), device_id_type=MESH_ID,
        )
        copy.start()
        copies.append(copy)
    summed = part[0]
    for copy in copies:
        copy.wait_recv()
    first = list(copies)
    for s in range(1, XC):
        summed = summed + rows_in[s]
    each = summed.shape[0] // mems
    for m in range(mems):
        mine[m, :each, :] = summed[m * each : (m + 1) * each, :]
    pieces[mem] = mine[mem]
    copies = []
    for s in range(1, mems):
        copy = pltpu.make_async_remote_copy(
            src_ref=mine.at[lax.rem(mem + s, mems)], dst_ref=pieces.at[mem],
            send_sem=mem_send.at[s], recv_sem=mem_recv.at[s],
            device_id=mem_peer(s), device_id_type=MESH_ID,
        )
        copy.start()
        copies.append(copy)
    for copy in copies:
        copy.wait_recv()
    for copy in first + copies:
        copy.wait_send()
    for l in range(LEVELS):
        first = l * (mems // LEVELS)
        both = pieces[first]
        for m in range(first + 1, first + mems // LEVELS):
            both = both + pieces[m]
        both = both / (MEMBERS - 1.0)
        for i in range(each):
            out[l : l + 1, i * BLOCK : (i + 1) * BLOCK] = both[i : i + 1, :]


def shards(ensemble, control, pair_home, pair_local, pair_count, pair_shift):
    member_rows, columns = ensemble.shape
    blocks = columns // BLOCK
    owners = lax.axis_size("col")
    mems = lax.axis_size("mem")
    entries = 2 * pair_shift.shape[1]
    sign = jnp.asarray(np.array([1.0, -1.0], np.float32))
    both = (pair_shift[:, :, None] * sign).reshape(2, entries)
    small = jnp.concatenate([both.reshape(4, LANES), jnp.zeros((4, LANES), jnp.float32)])
    live = jnp.broadcast_to(pair_count[:, None], (8, LANES))
    named = pair_home.reshape(-1, LANES) | (pair_local.reshape(-1, LANES) << 6)
    smem = pl.BlockSpec(memory_space=pltpu.SMEM)
    vmem = pl.BlockSpec(memory_space=pltpu.VMEM)
    dma = pltpu.SemaphoreType.DMA
    shape = jax.ShapeDtypeStruct

    *givers, taking, part, table, found, extra, east, north = pl.pallas_call(
        functools.partial(gather_kernel, blocks),
        out_shape=[shape((len(slots) * blocks, member_rows, BLOCK), jnp.bfloat16) for slots in SLOTS] + [
            shape((XC * blocks, member_rows, BLOCK), jnp.bfloat16),
            shape((XC * blocks, BLOCK), jnp.float32),
            shape((owners, entries), jnp.int32),
            shape((owners, LANES), jnp.int32),
            shape((8, LANES), jnp.int32),
            shape((owners, entries), jnp.float32),
            shape((owners, entries), jnp.float32),
        ],
        in_specs=[vmem] * 5,
        out_specs=[vmem] * (len(SLOTS) + 7),
        scratch_shapes=[
            pltpu.VMEM((owners * 8, LANES), jnp.float32),
            pltpu.VMEM((owners * 8, LANES), jnp.int32),
            pltpu.VMEM((8, POSITIONS), jnp.int32),
            pltpu.VMEM((POSITIONS, BLOCK), jnp.float32),
            pltpu.SMEM((8, POSITIONS), jnp.int32),
            pltpu.VMEM((POSITIONS // GROUP, GROUP, BLOCK), jnp.float32),
            dma((1,)),
            dma((2, 4, 2)), dma((2, 4, 2)), dma((2, 2, 2)), dma((2, 2, 2)), dma((X, 2)), dma((X, 2)),
            dma((2, XC)), dma((2, XC)), dma((2, Z)), dma((2, Z)),
        ],
        compiler_params=pltpu.CompilerParams(
            collective_id=0, has_side_effects=True, vmem_limit_bytes=28 * 1024 * 1024
        ),
    )(ensemble, control, small, live, named)

    part = pl.pallas_call(
        functools.partial(extra_kernel, blocks),
        out_shape=shape(part.shape, part.dtype),
        in_specs=[smem] + [vmem] * (len(SLOTS) + 6),
        out_specs=vmem,
        scratch_shapes=[
            pltpu.SMEM(table.shape, jnp.int32), pltpu.SMEM(found.shape, jnp.int32),
            pltpu.SMEM(east.shape, jnp.float32), pltpu.SMEM(north.shape, jnp.float32),
            dma((4,)),
        ],
        compiler_params=pltpu.CompilerParams(vmem_limit_bytes=24 * 1024 * 1024),
    )(extra, part, table, found, east, north, *givers, taking)
    part = part.reshape(XC, blocks, BLOCK)

    return pl.pallas_call(
        sum_kernel,
        out_shape=jax.ShapeDtypeStruct((LEVELS, columns // mems), jnp.float32),
        in_specs=[vmem],
        out_specs=vmem,
        scratch_shapes=[
            pltpu.VMEM((XC, blocks, BLOCK), jnp.float32),
            pltpu.VMEM((mems, 8, BLOCK), jnp.float32),
            pltpu.VMEM((mems, 8, BLOCK), jnp.float32),
            dma((XC,)), dma((XC,)), dma((mems,)), dma((mems,)),
        ],
        compiler_params=pltpu.CompilerParams(
            collective_id=1, has_side_effects=True, vmem_limit_bytes=8 * 1024 * 1024
        ),
    )(part)


def solution(mesh):
    return jax.shard_map(
        shards,
        mesh=mesh,
        in_specs=(P("mem", "col"), P(None, "col"), P(), P(), P("col"), P(None, "col")),
        out_specs=P(None, ("col", "mem")),
        check_vma=False,
    )
```

```python
import functools

import jax
import jax.numpy as jnp
import numpy as np
from jax import lax
from jax.experimental import pallas as pl
from jax.experimental.pallas import tpu as pltpu
from jax.sharding import PartitionSpec as P

MEMBERS = 80
LEVELS = 4
SIDE = 16
BLOCK = 256
SPACING_KM = 200.0
HALF_WIDTH = 250.0
XC = 8
Z = 8
X = 4
LANES = 128
GROUP = 8
ROW_CAP = 16
SLOTS = ((0, 7, 1), (6, 2), (5, 3), (4,))
CAPS = (104, 72, 72, 40)
STARTS = (0, 104, 176, 256)
EARLY = 256
POSITIONS = 384
USED = 1 << 25
DONE = 1 << 30
MESH_ID = pl.DeviceIdType.MESH


def gaspari_cohn(squared):
    scaled = jnp.sqrt(squared * (1.0 / (HALF_WIDTH * HALF_WIDTH)))
    near_part = (
        ((-0.25 * scaled + 0.5) * scaled + 0.625) * scaled - 5.0 / 3.0
    ) * scaled * scaled + 1.0
    bounded = jnp.maximum(scaled, 1.0)
    far_part = (
        ((((scaled * (1.0 / 12.0) - 0.5) * scaled + 0.625) * scaled + 5.0 / 3.0) * scaled - 5.0) * scaled
        + 4.0
        - (2.0 / 3.0) / bounded
    )
    return jnp.where(scaled <= 1.0, near_part, jnp.where(scaled <= 2.0, far_part, 0.0))


def tap_rows(east, north):
    shape = (east.shape[0] if east.ndim else 1, BLOCK)
    lane = lax.broadcasted_iota(jnp.int32, shape, 1) + SIDE // 2
    de = east - SPACING_KM * ((lane & (SIDE - 1)) - SIDE // 2).astype(jnp.float32)
    dn = north + SPACING_KM * (SIDE // 2 - (lane >> 4)).astype(jnp.float32)
    return gaspari_cohn(de * de + dn * dn).astype(jnp.bfloat16).astype(jnp.float32)


def place():
    col = lax.axis_index("col")
    return col, col // XC, (col % XC) // 2, col % 2


def row_peer(z, x, core, slot):
    return {"col": z * XC + lax.rem(x + slot // 2, X) * 2 + lax.rem(core + slot % 2, 2)}


def column_peer(col, z, step):
    return {"col": col + (lax.rem(z + step, Z) - z) * XC}


def mirrored(slot):
    return (X - slot // 2) % X * 2 + slot % 2


def greet(peers):
    barrier = pltpu.get_barrier_semaphore()
    for peer in peers:
        pl.semaphore_signal(barrier, inc=1, device_id=peer, device_id_type=MESH_ID)
    return lambda: pl.semaphore_wait(barrier, len(peers))


def turn(a, shift):
    return pltpu.roll(a, shift % a.shape[1], 1)


def own_entries(home, local, count, z, x, core):
    lane = lax.broadcasted_iota(jnp.int32, home.shape, 1)
    even = (lane & 1) == 0
    other_home = jnp.where(even, turn(home, -1), turn(home, 1))
    other_local = jnp.where(even, turn(local, -1), turn(local, 1))
    mine = ((home >> 3) == z) & ((other_home & 7) == x * 2 + core) & ((lane >> 1) < count)
    slot = ((((home >> 1) & 3) - x) & 3) * 2 + ((home ^ core) & 1)
    turned = ((other_home >> 3) - z) & 7
    return mine, slot, other_local, turned


def by_slot(turned, values):
    found = jnp.zeros_like(turned)
    for t, value in values.items():
        found = jnp.where(turned == t, value, found)
    return found


def row_rank(mine):
    rank = mine.astype(jnp.int32)
    lane = lax.broadcasted_iota(jnp.int32, rank.shape, 1)
    step = 1
    while step < rank.shape[1]:
        rank = rank + jnp.where(lane >= step, turn(rank, step), 0)
        step *= 2
    return rank - 1


def pack_rows(mine, rank, arrays):
    lane = lax.broadcasted_iota(jnp.int32, rank.shape, 1)
    move = jnp.where(mine, lane - rank, 0)
    arrays = [jnp.where(mine, a, 0) for a in arrays]
    step = 1
    while step < rank.shape[1]:
        next_move = turn(move, -step)
        arrives, leaves = (next_move & step) != 0, (move & step) != 0
        arrays = [jnp.where(arrives, turn(a, -step), jnp.where(leaves, 0, a)) for a in arrays]
        move = jnp.where(arrives, next_move, jnp.where(leaves, 0, move))
        step *= 2
    return arrays


def group_rank(mine, group):
    rows, lanes = mine.shape
    line = lax.broadcasted_iota(jnp.int32, (rows, lanes), 0)
    lane = lax.broadcasted_iota(jnp.int32, (rows, lanes), 1)
    rank = jnp.zeros((rows, lanes), jnp.int32)
    for t in range(0, len(CAPS), 2):
        low, high = mine & (group == t), mine & (group == t + 1)
        upto = low.astype(jnp.int32) + (high.astype(jnp.int32) << 16)
        step = 1
        while step < ROW_CAP:
            upto = upto + jnp.where(lane >= step, turn(upto, step), 0)
            step *= 2
        whole = jnp.broadcast_to(upto[:, ROW_CAP - 1 : ROW_CAP], (rows, lanes))
        above = whole
        step = 1
        while step < rows:
            above = above + jnp.where(line >= step, pltpu.roll(above, step, 0), 0)
            step *= 2
        upto = upto + above - whole
        rank = jnp.where(low, (upto & 0xFFFF) - 1, jnp.where(high, (upto >> 16) - 1, rank))
    return rank


def packed_entries(mine, slot, local, giver, turned, east, north):
    lane = lax.broadcasted_iota(jnp.int32, mine.shape, 1)
    code = slot | (local << 3) | (giver << 8) | (turned << 13) | (lane << 16) | (1 << 24)
    rank = row_rank(mine)
    return pack_rows(mine, rank, [code, east, north]), jnp.max(rank, axis=1, keepdims=True) + 1


def make_lists(code, east, north, blocks):
    table = code
    code, east, north = code[:, :LANES], east[:, :LANES], north[:, :LANES]
    kept = (code != 0) & (lax.broadcasted_iota(jnp.int32, code.shape, 1) < ROW_CAP)
    turned = (code >> 13) & 7
    group = by_slot(turned, {t: g for g, slots in enumerate(SLOTS) for t in slots})
    rank = group_rank(kept, group)
    kept = kept & (rank < by_slot(group, dict(enumerate(CAPS))))
    place_at = jnp.where(kept, by_slot(group, dict(enumerate(STARTS))) + rank, -1)
    giver = ((code >> 8) & 31) + by_slot(turned, {t: i * blocks for slots in SLOTS for i, t in enumerate(slots)})
    table = jnp.concatenate([jnp.where(kept, code | DONE, code), table[:, LANES:]], axis=1)
    code = (code & 255) | (giver << 8) | USED
    rows = code.shape[0]
    lane = lax.broadcasted_iota(jnp.int32, (rows, POSITIONS), 1)
    words = jnp.zeros((rows, POSITIONS), jnp.int32)
    easts = jnp.zeros((rows, POSITIONS), jnp.float32)
    norths = jnp.zeros((rows, POSITIONS), jnp.float32)
    for j in range(ROW_CAP):
        hit = place_at[:, j : j + 1] == lane
        words = words + jnp.where(hit, code[:, j : j + 1], 0)
        easts = easts + jnp.where(hit, east[:, j : j + 1], 0.0)
        norths = norths + jnp.where(hit, north[:, j : j + 1], 0.0)
    words, easts, norths = [jnp.sum(v, axis=0, keepdims=True) for v in (words, easts, norths)]
    return words, jnp.where(words >= USED, easts, 1e5), norths, table


def taper_tile(row):
    within = lax.broadcasted_iota(jnp.int32, (SIDE, BLOCK), 1) & (SIDE - 1)
    within = jnp.abs(within - lax.broadcasted_iota(jnp.int32, (SIDE, BLOCK), 0)) <= SIDE // 4
    taps = pltpu.roll(jnp.broadcast_to(row, (SIDE, BLOCK)), 0, 1, stride=1, stride_axis=0)
    taps = jnp.where(within, taps, 0.0)
    left, right = taps[:, :LANES], taps[:, LANES:]
    lane = lax.broadcasted_iota(jnp.int32, left.shape, 1)
    middle, first, last = [], [], []
    for k in range(8):
        low = lane < 16 * k
        a, b = turn(left, 16 * k), turn(right, 16 * k)
        middle.append(jnp.where(low, a, b).astype(jnp.bfloat16))
        if k < 4:
            first.append(jnp.where(low, 0.0, a).astype(jnp.bfloat16))
        else:
            last.append(jnp.where(low, b, 0.0).astype(jnp.bfloat16))
    return jnp.concatenate(middle + first + last)


def pair_sum(row, give, take):
    south, north = [give[:, i * LANES : (i + 1) * LANES].astype(jnp.float32) for i in range(2)]
    low = lax.broadcasted_iota(jnp.int32, south.shape, 1) < LANES // 2
    give = jnp.concatenate([
        jnp.concatenate([south, jnp.where(low, north, 0.0)], axis=1),
        jnp.concatenate([north, jnp.where(low, 0.0, south)], axis=1),
    ]).astype(jnp.bfloat16)
    reached = jnp.dot(give, taper_tile(row), preferred_element_type=jnp.float32)
    count = take.shape[0]
    sums = [
        jnp.sum(reached[i * count : (i + 1) * count] * take[:, i * LANES : (i + 1) * LANES].astype(jnp.float32),
                axis=0, keepdims=True)
        for i in range(2)
    ]
    return jnp.concatenate(sums, axis=1)


def gather_kernel(
    blocks, ensemble, control, small, live, named, *refs,
):
    givers, refs = refs[: len(SLOTS)], refs[len(SLOTS) :]
    taking, part_out, table, found, extra, east, north = refs[:7]
    (
        seen, counts, words, taps, words_s, row_sums, local_sem,
        z_send, z_recv, x_send, x_recv, core_send, core_recv, row_send, row_recv, col_send, col_recv,
    ) = refs[7:]
    col, z, x, core = place()
    entered = greet([row_peer(z, x, core, s) for s in range(1, XC)] + [column_peer(col, z, s) for s in range(1, Z)])
    member_rows, columns = ensemble.shape
    half = blocks // 2
    level = (lax.axis_index("mem") * member_rows) // MEMBERS
    scale = jnp.zeros((1, columns), jnp.float32)
    for l in range(LEVELS):
        scale = jnp.where(level == l, control[l : l + 1, :].astype(jnp.float32), scale)
    for b in range(blocks):
        own = ensemble[:, b * BLOCK : (b + 1) * BLOCK]
        taking[b] = own
        givers[0][b] = (own.astype(jnp.float32) * scale[:, b * BLOCK : (b + 1) * BLOCK]).astype(jnp.bfloat16)
    seen[pl.ds(pl.multiple_of(col * 8, 8), 8), :] = small[...]
    counts[pl.ds(pl.multiple_of(col * 8, 8), 8), :] = live[...]

    entered()

    sent = []

    def send(source, target, send_sem, recv_sem, peer):
        copy = pltpu.make_async_remote_copy(
            src_ref=source, dst_ref=target, send_sem=send_sem, recv_sem=recv_sem,
            device_id=peer, device_id_type=MESH_ID,
        )
        copy.start()
        sent.append(copy)
        return copy

    def part(ref, slot, c):
        return ref.at[pl.ds(slot * blocks + c * half, half)]

    def giver_part(turned, c):
        for ref, slots in zip(givers, SLOTS):
            if turned in slots:
                return part(ref, slots.index(turned), c)

    def send_z(way, step, c):
        sign = 1 if way == 0 else -1
        return send(
            giver_part(-sign * step % Z, c), giver_part(-sign * (step + 1) % Z, c),
            z_send.at[way, step, c], z_recv.at[way, step, c], column_peer(col, z, sign % Z),
        )

    def send_x(way, step, c):
        sign = 1 if way == 0 else -1
        return send(
            part(taking, (-sign * step) % X * 2, c), part(taking, (-sign * (step + 1)) % X * 2, c),
            x_send.at[way, step, c], x_recv.at[way, step, c], row_peer(z, x, core, sign % X * 2),
        )

    def send_core(turned, c):
        return send(
            part(taking, turned * 2, c), part(taking, turned * 2 + 1, c),
            core_send.at[turned, c], core_recv.at[turned, c], row_peer(z, x, core, 1),
        )

    row_copies = []
    for i, ref in enumerate((seen, counts)):
        rows = ref.at[pl.ds(pl.multiple_of(col * 8, 8), 8), :]
        for s in range(1, XC):
            row_copies.append(send(rows, rows, row_send.at[i, s], row_recv.at[i, s], row_peer(z, x, core, s)))
    zs, xs, cores = {}, {}, []
    for c in range(2):
        for way in range(2):
            zs[way, 0, c] = send_z(way, 0, c)
            xs[way, 0, c] = send_x(way, 0, c)
    for c in range(2):
        cores.append(send_core(0, c))
    for copy in row_copies:
        copy.wait_recv()
    col_copies = []
    for i, ref in enumerate((seen, counts)):
        rows = ref.at[pl.ds(pl.multiple_of(z * 64, 64), 64), :]
        for s in range(1, Z):
            col_copies.append(send(rows, rows, col_send.at[i, s], col_recv.at[i, s], column_peer(col, z, s)))

    def row_arrivals(step, c):
        for way in range(2):
            turned = (-(1 if way == 0 else -1) * (step + 1)) % X
            if step == 0 or (step == 1 and c == way):
                xs[way, step, c].wait_recv()
                if step == 0 and c == way:
                    xs[way, 1, c] = send_x(way, 1, c)
                cores.append(send_core(turned, c))

    def arrivals(step, c, rows=True):
        if rows:
            row_arrivals(step, c)
        for way in range(2):
            if step < 3 or c == way:
                zs[way, step, c].wait_recv()
                if step < 2 or (step == 2 and c == way):
                    zs[way, step + 1, c] = send_z(way, step + 1, c)
    def own_lists():
        for copy in col_copies:
            copy.wait_recv()
        owners = seen.shape[0] // 8
        rows = [seen[pl.ds(i, owners, stride=8), :] for i in range(4)]
        shift_e, shift_n = jnp.concatenate(rows[0:2], axis=1), jnp.concatenate(rows[2:4], axis=1)
        east[...], north[...] = shift_e, shift_n
        count = counts[pl.ds(0, owners, stride=8), :]
        count = jnp.concatenate([count, count], axis=1)
        names = jnp.concatenate([named[pl.ds(i, owners, stride=2), :] for i in range(2)], axis=1)
        homes, locals_ = names & 63, names >> 6
        mine, slot, giver, turned = own_entries(homes, locals_, count, z, x, core)
        packed, amount = packed_entries(mine, slot, locals_, giver, turned, shift_e, shift_n)
        found[...] = jnp.broadcast_to(amount, found.shape)
        return packed

    list_copy = pltpu.make_async_copy(words, words_s, local_sem.at[0])

    def place_lists(packed):
        word, shift_e, shift_n, entries = make_lists(*packed, blocks)
        words[...] = jnp.broadcast_to(word, words.shape)
        list_copy.start()
        table[...] = entries
        left = ((entries != 0) & (entries < DONE)).astype(jnp.int32)
        left = jnp.max(jnp.max(left, axis=1, keepdims=True), axis=0, keepdims=True)
        extra[...] = jnp.broadcast_to(left, extra.shape)
        return jnp.concatenate([shift_e, shift_n, jnp.zeros((6, POSITIONS), jnp.float32)]).T

    def some_taps(shift, c):
        at = slice(c * LANES, (c + 1) * LANES)
        taps[at, :] = tap_rows(shift[at, 0:1], shift[at, 1:2])

    def work(group, begin=0, end=None):
        first = STARTS[group] // GROUP

        def some(n, carry):
            rows = taps[pl.ds(pl.multiple_of(n * GROUP, GROUP), GROUP), :]
            sums = []
            for g in range(GROUP):
                word = words_s[0, n * GROUP + g]
                sums.append(pair_sum(
                    rows[g : g + 1, :],
                    givers[group][(word >> 8) & 127], taking[(word & 7) * blocks + ((word >> 3) & 31)],
                ))
            row_sums[n] = jnp.concatenate(sums)
            return carry

        end = CAPS[group] if end is None else end
        lax.fori_loop(first + begin // GROUP, first + end // GROUP, some, 0)

    row_sums[...] = jnp.zeros_like(row_sums)
    packed = own_lists()
    arrivals(0, 0)
    shift = place_lists(packed)
    arrivals(0, 1)
    some_taps(shift, 0)
    arrivals(1, 0)
    list_copy.wait()
    row_arrivals(1, 1)
    for copy in cores:
        copy.wait_recv()
    work(0, 0, 48)
    arrivals(1, 1, False)
    work(0, 48)
    some_taps(shift, 1)
    arrivals(2, 0)
    work(1)
    some_taps(shift, 2)
    arrivals(2, 1)
    work(2)

    taken = (words[0:1, :] & 7) * blocks + ((words[0:1, :] >> 3) & 31)
    count = part_out.shape[0]

    def spread(begin, end):
        hot = lax.broadcasted_iota(jnp.int32, (count, end - begin), 0) == taken[:, begin:end]
        sums = row_sums[begin // GROUP : end // GROUP].reshape(end - begin, BLOCK)
        return jnp.dot(
            hot.astype(jnp.float32), sums, preferred_element_type=jnp.float32, precision=lax.Precision.HIGHEST
        )

    part_out[...] = spread(0, EARLY)
    arrivals(3, 0)
    arrivals(3, 1)
    work(3)
    part_out[...] += spread(EARLY, POSITIONS)
    for copy in sent:
        copy.wait_send()


def extra_kernel(blocks, extra, part, table, found, east, north, *refs):
    givers, taking, refs = refs[: len(SLOTS)], refs[len(SLOTS)], refs[len(SLOTS) + 1 :]
    out, table_s, found_s, east_s, north_s, sems = refs
    out[...] = part[...]

    @pl.when(extra[0, 0] > 0)
    def _():
        copies = [
            pltpu.make_async_copy(a, b, sems.at[i])
            for i, (a, b) in enumerate([(table, table_s), (found, found_s), (east, east_s), (north, north_s)])
        ]
        for copy in copies:
            copy.start()
        for copy in copies:
            copy.wait()

        def row_step(row, carry):
            def entry_step(k, carry):
                word = table_s[row, k]
                receiver = (word & 7) * blocks + ((word >> 3) & 31)
                giver, turned, lane = (word >> 8) & 31, (word >> 13) & 7, (word >> 16) & 255
                line = tap_rows(east_s[row, lane], north_s[row, lane])
                for ref, slots in zip(givers, SLOTS):
                    for i, t in enumerate(slots):

                        @pl.when((turned == t) & (word < DONE))
                        def _():
                            out[pl.ds(receiver, 1), :] += pair_sum(line, ref[i * blocks + giver], taking[receiver])

                return carry

            return lax.fori_loop(0, found_s[row, 0], entry_step, carry)

        lax.fori_loop(0, table.shape[0], row_step, 0)


def sum_kernel(part, out, rows_in, mine, pieces, row_send, row_recv, mem_send, mem_recv):
    _, z, x, core = place()
    mem = lax.axis_index("mem")
    mems = mine.shape[0]

    def mem_peer(step):
        return {"mem": lax.rem(mem + step, mems)}

    entered = greet([row_peer(z, x, core, s) for s in range(1, XC)] + [mem_peer(s) for s in range(1, mems)])
    mine[...] = jnp.zeros_like(mine)
    entered()
    copies = []
    for s in range(1, XC):
        copy = pltpu.make_async_remote_copy(
            src_ref=part.at[s], dst_ref=rows_in.at[mirrored(s)],
            send_sem=row_send.at[s], recv_sem=row_recv.at[mirrored(s)],
            device_id=row_peer(z, x, core, s), device_id_type=MESH_ID,
        )
        copy.start()
        copies.append(copy)
    summed = part[0]
    for copy in copies:
        copy.wait_recv()
    first = list(copies)
    for s in range(1, XC):
        summed = summed + rows_in[s]
    each = summed.shape[0] // mems
    for m in range(mems):
        mine[m, :each, :] = summed[m * each : (m + 1) * each, :]
    pieces[mem] = mine[mem]
    copies = []
    for s in range(1, mems):
        copy = pltpu.make_async_remote_copy(
            src_ref=mine.at[lax.rem(mem + s, mems)], dst_ref=pieces.at[mem],
            send_sem=mem_send.at[s], recv_sem=mem_recv.at[s],
            device_id=mem_peer(s), device_id_type=MESH_ID,
        )
        copy.start()
        copies.append(copy)
    for copy in copies:
        copy.wait_recv()
    for copy in first + copies:
        copy.wait_send()
    for l in range(LEVELS):
        first = l * (mems // LEVELS)
        both = pieces[first]
        for m in range(first + 1, first + mems // LEVELS):
            both = both + pieces[m]
        both = both / (MEMBERS - 1.0)
        for i in range(each):
            out[l : l + 1, i * BLOCK : (i + 1) * BLOCK] = both[i : i + 1, :]


def shards(ensemble, control, pair_home, pair_local, pair_count, pair_shift):
    member_rows, columns = ensemble.shape
    blocks = columns // BLOCK
    owners = lax.axis_size("col")
    mems = lax.axis_size("mem")
    entries = 2 * pair_shift.shape[1]
    sign = jnp.asarray(np.array([1.0, -1.0], np.float32))
    both = (pair_shift[:, :, None] * sign).reshape(2, entries)
    small = jnp.concatenate([both.reshape(4, LANES), jnp.zeros((4, LANES), jnp.float32)])
    live = jnp.broadcast_to(pair_count[:, None], (8, LANES))
    named = pair_home.reshape(-1, LANES) | (pair_local.reshape(-1, LANES) << 6)
    smem = pl.BlockSpec(memory_space=pltpu.SMEM)
    vmem = pl.BlockSpec(memory_space=pltpu.VMEM)
    dma = pltpu.SemaphoreType.DMA
    shape = jax.ShapeDtypeStruct

    *givers, taking, part, table, found, extra, east, north = pl.pallas_call(
        functools.partial(gather_kernel, blocks),
        out_shape=[shape((len(slots) * blocks, member_rows, BLOCK), jnp.bfloat16) for slots in SLOTS] + [
            shape((XC * blocks, member_rows, BLOCK), jnp.bfloat16),
            shape((XC * blocks, BLOCK), jnp.float32),
            shape((owners, entries), jnp.int32),
            shape((owners, LANES), jnp.int32),
            shape((8, LANES), jnp.int32),
            shape((owners, entries), jnp.float32),
            shape((owners, entries), jnp.float32),
        ],
        in_specs=[vmem] * 5,
        out_specs=[vmem] * (len(SLOTS) + 7),
        scratch_shapes=[
            pltpu.VMEM((owners * 8, LANES), jnp.float32),
            pltpu.VMEM((owners * 8, LANES), jnp.int32),
            pltpu.VMEM((8, POSITIONS), jnp.int32),
            pltpu.VMEM((POSITIONS, BLOCK), jnp.float32),
            pltpu.SMEM((8, POSITIONS), jnp.int32),
            pltpu.VMEM((POSITIONS // GROUP, GROUP, BLOCK), jnp.float32),
            dma((1,)),
            dma((2, 4, 2)), dma((2, 4, 2)), dma((2, 2, 2)), dma((2, 2, 2)), dma((X, 2)), dma((X, 2)),
            dma((2, XC)), dma((2, XC)), dma((2, Z)), dma((2, Z)),
        ],
        compiler_params=pltpu.CompilerParams(
            collective_id=0, has_side_effects=True, vmem_limit_bytes=28 * 1024 * 1024
        ),
    )(ensemble, control, small, live, named)

    part = pl.pallas_call(
        functools.partial(extra_kernel, blocks),
        out_shape=shape(part.shape, part.dtype),
        in_specs=[smem] + [vmem] * (len(SLOTS) + 6),
        out_specs=vmem,
        scratch_shapes=[
            pltpu.SMEM(table.shape, jnp.int32), pltpu.SMEM(found.shape, jnp.int32),
            pltpu.SMEM(east.shape, jnp.float32), pltpu.SMEM(north.shape, jnp.float32),
            dma((4,)),
        ],
        compiler_params=pltpu.CompilerParams(vmem_limit_bytes=24 * 1024 * 1024),
    )(extra, part, table, found, east, north, *givers, taking)
    part = part.reshape(XC, blocks, BLOCK)

    return pl.pallas_call(
        sum_kernel,
        out_shape=jax.ShapeDtypeStruct((LEVELS, columns // mems), jnp.float32),
        in_specs=[vmem],
        out_specs=vmem,
        scratch_shapes=[
            pltpu.VMEM((XC, blocks, BLOCK), jnp.float32),
            pltpu.VMEM((mems, 8, BLOCK), jnp.float32),
            pltpu.VMEM((mems, 8, BLOCK), jnp.float32),
            dma((XC,)), dma((XC,)), dma((mems,)), dma((mems,)),
        ],
        compiler_params=pltpu.CompilerParams(
            collective_id=1, has_side_effects=True, vmem_limit_bytes=8 * 1024 * 1024
        ),
    )(part)


def solution(mesh):
    return jax.shard_map(
        shards,
        mesh=mesh,
        in_specs=(P("mem", "col"), P(None, "col"), P(), P(), P("col"), P(None, "col")),
        out_specs=P(None, ("col", "mem")),
        check_vma=False,
    )
```
